32 devices in a mesh: patch: 8 (over y, x, core), head: 4 (over z).
Axes of the slice: x: 2, y: 2, z: 4, core: 2. Of those that a mesh axis runs over, the one named last changes fastest.
Arguments:
- patches: bfloat16 [2, 512, 9216], P(None, 'head', 'patch'), may hold values from -8 to 8
- hole_mask: int32 [2, 9216], P(None, 'patch'), may hold values from 0 to 1, as said below
- seg_start: int32 [2, 256], replicated, may hold values from 0 to 9215, as said below
- cotangent: bfloat16 [2, 512, 9216], P(None, 'head', 'patch'), may hold values from -6 to 6
- qkv_weight: float32 [1536, 512], P('head'), may hold values from -0.375 to 0.375
- out_weight: float32 [512, 512], P('head'), may hold values from -0.25 to 0.25
- norm_params: float32 [2, 512], replicated, may hold values from -1.2 to 1.8, as said below
- biases: float32 [4, 512], P(None, 'head'), may hold values from -1.5 to 1.5
- kernels: float32 [83, 512], P(None, 'head'), may hold values from -0.5 to 0.5
- conv_weight: float32 [8, 33], P('head'), may hold values from -1 to 1
- qkv_rows: float32 [1536], P('head'), may hold values from 1843.2 to 27648
- qkv_cols: float32 [512], replicated, may hold values from 1843.2 to 27648
- out_rows: float32 [512], P('head'), may hold values from 9216 to 147456
- out_cols: float32 [512], replicated, may hold values from 9216 to 147456
- norm_second: float32 [2, 512], replicated, may hold values from 9216 to 147456
- bias_second: float32 [4, 512], P(None, 'head'), may hold values from 2764.8 to 40550.4
- kernel_second: float32 [83, 512], P(None, 'head'), may hold values from 9216 to 129024
- conv_second: float32 [8, 33], P('head'), may hold values from 460800 to 7004160
Outputs:
- block_out: bfloat16 [2, 512, 9216], P(None, 'head', 'patch')
- patch_grad: float32 [2, 512, 9216], P(None, 'head', 'patch')
- qkv_grad: float32 [1536, 512], P('head')
- out_grad: float32 [512, 512], P('head')
- norm_grad: float32 [2, 512], replicated
- bias_grad: float32 [4, 512], P(None, 'head')
- kernel_grad: float32 [83, 512], P(None, 'head')
- conv_grad: float32 [8, 33], P('head')
- qkv_rows_new: float32 [1536], P('head')
- qkv_cols_new: float32 [512], replicated
- out_rows_new: float32 [512], P('head')
- out_cols_new: float32 [512], replicated
- norm_second_new: float32 [2, 512], replicated
- bias_second_new: float32 [4, 512], P(None, 'head')
- kernel_second_new: float32 [83, 512], P(None, 'head')
- conv_second_new: float32 [8, 33], P('head')
- qkv_new: float32 [1536, 512], P('head')
- out_new: float32 [512, 512], P('head')
- norm_new: float32 [2, 512], replicated
- bias_new: float32 [4, 512], P(None, 'head')
- kernel_new: float32 [83, 512], P(None, 'head')
- conv_new: float32 [8, 33], P('head')
The draws below stay inside these ranges and needn't reach their ends.
Inputs may be any that keep to these rules, and one draw needn't show every extreme that they name: `seg_start`: in each slide strictly rising; the first is 0. `hole_mask`: the first token of every landmark segment of a slide is tissue. `norm_params`: gains are positive.
All inputs are finite; a program needn't handle non-finite values.
Results may differ from the reference program's by a relative error of at most 0.01065.
The reference program's roundings to bfloat16 on the way count: a program that leaves them out, or rounds other values in their place, can miss the bound.
Values may be sent and summed in bfloat16 or wider, within the bound.
No kernel may reach another device: no remote copies, remote signals or barrier semaphores. Data moves between devices by JAX's collectives and lax.ppermute only.
A program may use at most 320 MiB of HBM per device.

```python
import math
import jax
import jax.numpy as jnp
from jax import lax

D = 512
HEADS = 8
HD = 64
LANDMARKS = 256
PINV_ITERS = 6
SLIDES = 2
SIDE = 96
STEP = 10
NTOK = 9216


def segment_starts(key):
    slide_keys = jax.random.split(key, SLIDES)

    def one_slide(slide_key):
        picked = jax.random.permutation(slide_key, NTOK - 1)[:LANDMARKS - 1] + 1
        return jnp.concatenate([jnp.zeros((1,), jnp.int32), jnp.sort(picked).astype(jnp.int32)])
    return jax.vmap(one_slide)(slide_keys)


def draw_seg_start(key, part):
    return segment_starts(key)


def draw_hole_mask(key, part):
    starts = segment_starts(key)
    key = jax.random.fold_in(key, 3)
    position = jnp.arange(NTOK, dtype=jnp.int32)
    grid_row = position // SIDE
    level = 300 + 600 * grid_row // (SIDE - 1)
    ticket = jax.random.randint(key, (SLIDES, NTOK), 0, 1000)
    slide_index = jnp.arange(SLIDES, dtype=jnp.int32)[:, None]
    first_token = jnp.zeros((SLIDES, NTOK), jnp.int32).at[slide_index, starts].set(1)
    return jnp.maximum((ticket < level[None, :]).astype(jnp.int32), first_token)


def draw_patches(key, part):
    starts = segment_starts(key)
    key = jax.random.fold_in(key, 5)
    region_key, noise_key = jax.random.split(key)
    position = jnp.arange(NTOK, dtype=jnp.int32)
    owner = jnp.sum((position[None, :, None] >= starts[:, None, :]).astype(jnp.int32), axis=2) - 1
    region = jax.random.truncated_normal(region_key, -4.0, 4.0, (SLIDES, LANDMARKS, D), jnp.float32)
    noise = jax.random.truncated_normal(noise_key, -4.0, 4.0, (SLIDES, NTOK, D), jnp.float32)
    placed = jnp.take_along_axis(region, owner[:, :, None], axis=1)
    return jnp.swapaxes(placed + noise, 1, 2).astype(jnp.bfloat16)


def draw_norm_params(key, part):
    key = jax.random.fold_in(key, 7)
    gain_key, bias_key = jax.random.split(key)
    slope = 0.5 + jnp.arange(D, dtype=jnp.float32) / D
    gain = slope * jax.random.uniform(gain_key, (D,), jnp.float32, 0.8, 1.2)
    offset_row = 0.3 * jax.random.truncated_normal(bias_key, -4.0, 4.0, (D,), jnp.float32)
    return jnp.stack([gain, offset_row])


def steps_of(key, dims, cuts, smallest, top_value):
    loudness, own = 1.0, jax.random.fold_in(key, 6)
    for dim, blocks in cuts:
        draws = jnp.exp(jax.random.uniform(jax.random.fold_in(own, dim), (blocks,), jnp.float32, smallest / len(cuts), top_value / len(cuts)))
        loudness = loudness * jnp.repeat(draws, dims[dim] // blocks).reshape([-1 if axis == dim else 1 for axis in range(len(dims))])
    return loudness


def bell_draw(rng, shape, spread, bound, cuts=(), kind=jnp.bfloat16):
    array = spread * jax.random.normal(rng, shape, jnp.float32)
    if cuts:
        array = array * steps_of(rng, shape, cuts, -0.22, 0.18)
    return jnp.clip(array, -bound, bound).astype(kind)


def setup_inputs(seed: int = 0) -> dict:
    streams_of = jax.random.split(jax.random.key(seed), 19)
    return {
        "patches": draw_patches(jax.random.fold_in(streams_of[18], 71), 0),
        "hole_mask": draw_hole_mask(jax.random.fold_in(streams_of[18], 71), 0),
        "seg_start": draw_seg_start(jax.random.fold_in(streams_of[18], 71), 0),
        "cotangent": bell_draw(streams_of[3], (SLIDES, D, NTOK), 1.0, 6.0, ((1, 4), (2, 8))),
        "qkv_weight": bell_draw(streams_of[4], (3 * D, D), (D // 2) ** -0.5, 0.375, ((0, 4),), jnp.float32),
        "out_weight": bell_draw(streams_of[5], (D, D), D ** -0.5, 0.25, ((0, 4),), jnp.float32),
        "norm_params": draw_norm_params(jax.random.fold_in(streams_of[18], 71), 0),
        "biases": bell_draw(streams_of[7], (4, D), 0.3, 1.5, ((1, 4),), jnp.float32),
        "kernels": bell_draw(streams_of[8], (83, D), 0.1, 0.5, ((1, 4),), jnp.float32),
        "conv_weight": bell_draw(streams_of[9], (HEADS, 33), 33 ** -0.5, 1.0, ((0, 4),), jnp.float32),
        "qkv_rows": jnp.clip(jnp.exp(math.log(27648.0) - 2.7080502 * jax.random.uniform(streams_of[10], (3 * D,), jnp.float32) ** steps_of(streams_of[10], (3 * D,), ((0, 4),), -0.2, 0.2)), 1843.2, 27648.0),
        "qkv_cols": jnp.clip(jnp.exp(jax.random.uniform(streams_of[11], (D,), jnp.float32, math.log(1843.2), math.log(27648.0))), 1843.2, 27648.0),
        "out_rows": jnp.clip(jnp.exp(math.log(147456.0) - 2.7725887 * jax.random.uniform(streams_of[12], (D,), jnp.float32) ** steps_of(streams_of[12], (D,), ((0, 4),), -0.2, 0.2)), 9216.0, 147456.0),
        "out_cols": jnp.clip(jnp.exp(jax.random.uniform(streams_of[13], (D,), jnp.float32, math.log(9216.0), math.log(147456.0))), 9216.0, 147456.0),
        "norm_second": jnp.clip(jnp.exp(jax.random.uniform(streams_of[14], (2, D), jnp.float32, math.log(9216.0), math.log(147456.0))), 9216.0, 147456.0),
        "bias_second": jnp.clip(jnp.exp(math.log(40550.4) - 2.6855773 * jax.random.uniform(streams_of[15], (4, D), jnp.float32) ** steps_of(streams_of[15], (4, D), ((1, 4),), -0.2, 0.2)), 2764.8, 40550.4),
        "kernel_second": jnp.clip(jnp.exp(math.log(129024.0) - 2.6390573 * jax.random.uniform(streams_of[16], (83, D), jnp.float32) ** steps_of(streams_of[16], (83, D), ((1, 4),), -0.2, 0.2)), 9216.0, 129024.0),
        "conv_second": jnp.clip(jnp.exp(math.log(7004160) - 2.7212954 * jax.random.uniform(streams_of[17], (HEADS, 33), jnp.float32) ** steps_of(streams_of[17], (HEADS, 33), ((0, 4),), -0.2, 0.2)), 460800.0, 7004160),
    }


EPS_NORM = 1e-05
EPS_FACTOR = 1e-30
RATE = 0.5
HIGHEST = lax.Precision.HIGHEST
BLOCKS = ((0, 49), (49, 74), (74, 83))

@jax.custom_vjp
def low(v):
    return lax.optimization_barrier(v.astype(jnp.bfloat16)).astype(jnp.float32)

@jax.custom_vjp
def low_back(v):
    return v

def low_keep(v):
    return (low(v), None)

def low_pass(kept, grad):
    return (grad,)

def back_keep(v):
    return (v, None)

def back_low(kept, grad):
    return (low(grad),)
low.defvjp(low_keep, low_pass)
low_back.defvjp(back_keep, back_low)

def low_pair(value_in):
    return low_back(low(value_in))

def matmul(left_side, right_side):
    return jnp.matmul(left_side, right_side, precision=HIGHEST)

def pseudo_inverse_of(kernel_two):
    frobenius = lax.optimization_barrier(jnp.sum(kernel_two * kernel_two, axis=(1, 2), keepdims=True))
    approx = jnp.swapaxes(kernel_two, 1, 2) / frobenius
    identity = jnp.eye(kernel_two.shape[1], dtype=kernel_two.dtype)
    for turn_index in range(PINV_ITERS):
        product = matmul(kernel_two, approx)
        inner_term = 7.0 * identity - product
        inner_term = 15.0 * identity - matmul(product, inner_term)
        inner_term = 13.0 * identity - matmul(product, inner_term)
        approx = 0.25 * matmul(approx, inner_term)
    return approx

def landmark_kernel(query_marks, key_marks):
    scores = jnp.einsum('mhe,khe->hmk', query_marks, key_marks, precision=HIGHEST)
    return pseudo_inverse_of(jax.nn.softmax(scores, axis=-1))

def full_kernel(kernels):
    channels = kernels.shape[1]
    large_part = kernels[0:49].reshape(7, 7, channels)
    middle_part = jnp.pad(kernels[49:74].reshape(5, 5, channels), ((1, 1), (1, 1), (0, 0)))
    small_part = jnp.pad(kernels[74:83].reshape(3, 3, channels), ((2, 2), (2, 2), (0, 0)))
    return large_part + middle_part + small_part

def line_conv(value_rows, conv_weight):
    padded = jnp.pad(value_rows, ((16, 16), (0, 0), (0, 0)))
    running = jnp.zeros_like(value_rows)
    for tap_index in range(33):
        running = running + conv_weight[:, tap_index][None, :, None] * padded[tap_index:tap_index + NTOK]
    return running

def grid_mix(grid_one, kernels):
    padded = jnp.pad(grid_one, ((3, 3), (3, 3), (0, 0)))
    kernel = full_kernel(kernels)
    running = jnp.zeros_like(grid_one)
    for row_shift in range(7):
        for col_shift in range(7):
            running = running + kernel[row_shift, col_shift] * padded[row_shift:row_shift + SIDE, col_shift:col_shift + SIDE]
    return running

def forward(patch_float, norm_params, qkv_weight, out_weight, biases, kernels, conv_weight, mask_float, onehot):
    mean_value = lax.optimization_barrier(jnp.mean(patch_float, axis=1, keepdims=True))
    variance = lax.optimization_barrier(jnp.mean(patch_float * patch_float, axis=1, keepdims=True)) - mean_value * mean_value
    inv_std = lax.rsqrt(variance + EPS_NORM)
    normed = low((patch_float - mean_value) * inv_std * norm_params[0] + norm_params[1])
    projected = matmul(normed, jnp.transpose(low(qkv_weight))).reshape(NTOK, HEADS, 3, HD)
    gate_mask = mask_float[:, None, None]
    queries = low_pair(projected[:, :, 0] * gate_mask * HD ** (-0.5))
    key_rows = low_pair(projected[:, :, 1] * gate_mask)
    value_rows = low_pair(projected[:, :, 2] * gate_mask)
    counts = lax.optimization_barrier(jnp.sum(onehot * mask_float[:, None], axis=0))
    query_sum = low_back(jnp.einsum('nm,nhe->mhe', onehot, queries, precision=HIGHEST))
    key_sum = low_back(jnp.einsum('nm,nhe->mhe', onehot, key_rows, precision=HIGHEST))
    query_marks = low(query_sum / counts[:, None, None])
    key_marks = low(key_sum / counts[:, None, None])
    scores_one = low_back(jnp.einsum('nhe,mhe->hnm', queries, key_marks, precision=HIGHEST))
    kernel_one = low(jax.nn.softmax(scores_one, axis=-1))
    pseudo_inverse = landmark_kernel(query_marks, key_marks)
    scores_three = low_back(jnp.einsum('mhe,nhe->hmn', query_marks, key_rows, precision=HIGHEST))
    weights_three = low(jnp.exp(scores_three) * mask_float[None, None, :])
    weight_sum = lax.optimization_barrier(jnp.sum(weights_three, axis=-1))
    gathered_sum = low_back(jnp.einsum('hmn,nhe->hme', weights_three, value_rows, precision=HIGHEST))
    mark_values = gathered_sum / weight_sum[..., None]
    mixed_marks = low(matmul(pseudo_inverse, mark_values))
    attended = jnp.einsum('hnm,hme->nhe', kernel_one, mixed_marks, precision=HIGHEST)
    residual = jax.checkpoint(line_conv)(value_rows, conv_weight)
    heads_out = low_pair(attended + residual).reshape(NTOK, D)
    section_one = patch_float + low_back(matmul(heads_out, low(out_weight))) + biases[0]
    grid_one = section_one.reshape(SIDE, SIDE, D)
    mixed_grid = jax.checkpoint(grid_mix)(grid_one, kernels)
    result = grid_one + mixed_grid + (biases[1] + biases[2] + biases[3])
    return result.reshape(NTOK, D)

def scaled(update, weight):
    clip_factor = jnp.maximum(1.0, jnp.sqrt(jnp.mean(update * update)))
    return RATE * jnp.sqrt(jnp.mean(weight * weight)) * update / clip_factor

def factored(grad_in, weight, rows_old, cols_old, decay_rate):
    squares = grad_in * grad_in
    rows_new = decay_rate * rows_old + (1.0 - decay_rate) * (lax.optimization_barrier(jnp.mean(squares, axis=1)) + EPS_FACTOR)
    cols_new = decay_rate * cols_old + (1.0 - decay_rate) * (lax.optimization_barrier(jnp.mean(squares, axis=0)) + EPS_FACTOR)
    update = grad_in * lax.rsqrt(rows_new[:, None] * cols_new[None, :] / jnp.mean(rows_new))
    return (rows_new, cols_new, weight - scaled(update, weight))

def plain_step(grad_in, weight, second, decay_rate):
    second_new = decay_rate * second + (1.0 - decay_rate) * (grad_in * grad_in + EPS_FACTOR)
    update = grad_in * lax.rsqrt(second_new)
    return (second_new, weight - scaled(update, weight))

def reference(patches, hole_mask, seg_start, cotangent, qkv_weight, out_weight, norm_params, biases, kernels, conv_weight, qkv_rows, qkv_cols, out_rows, out_cols, norm_second, bias_second, kernel_second, conv_second):
    decay_rate = 1.0 - STEP ** (-0.8)
    position = jnp.arange(NTOK, dtype=jnp.int32)[:, None]

    def one_slide(carried, slide_in):
        patch_slide, mask_slide, start_slide, cot_slide = slide_in
        mask_float = mask_slide.astype(jnp.float32)
        seg_end = jnp.concatenate([start_slide[1:].astype(jnp.int32), jnp.full((1,), NTOK, jnp.int32)])
        onehot = ((position >= start_slide.astype(jnp.int32)[None, :]) & (position < seg_end[None, :])).astype(jnp.float32)

        def whole_layer(patch_float, norm_in, qkv_in, out_in, bias_in, kernel_in, conv_in):
            return forward(patch_float, norm_in, qkv_in, out_in, bias_in, kernel_in, conv_in, mask_float, onehot)
        block_value, pull_back = jax.vjp(whole_layer, jnp.transpose(patch_slide.astype(jnp.float32)), norm_params, qkv_weight, out_weight, biases, kernels, conv_weight)
        grads = pull_back(jnp.transpose(cot_slide.astype(jnp.float32)))
        summed = tuple((total + piece for total, piece in zip(carried, grads[1:])))
        return (summed, (jnp.transpose(block_value).astype(jnp.bfloat16), jnp.transpose(grads[0])))
    initial = (jnp.zeros_like(norm_params), jnp.zeros_like(qkv_weight), jnp.zeros_like(out_weight), jnp.zeros_like(biases), jnp.zeros_like(kernels), jnp.zeros_like(conv_weight))
    totals, (block_out, patch_grad) = lax.scan(one_slide, initial, (patches, hole_mask, seg_start, cotangent))
    norm_grad, qkv_grad, out_grad, bias_grad, kernel_grad, conv_grad = totals
    qkv_rows_new, qkv_cols_new, qkv_new = factored(qkv_grad, qkv_weight, qkv_rows, qkv_cols, decay_rate)
    out_rows_new, out_cols_new, out_new = factored(out_grad, out_weight, out_rows, out_cols, decay_rate)
    norm_pairs = [plain_step(norm_grad[row_index], norm_params[row_index], norm_second[row_index], decay_rate) for row_index in range(2)]
    bias_pairs = [plain_step(bias_grad[row_index], biases[row_index], bias_second[row_index], decay_rate) for row_index in range(4)]
    kernel_pairs = [plain_step(kernel_grad[start_row:end_row], kernels[start_row:end_row], kernel_second[start_row:end_row], decay_rate) for start_row, end_row in BLOCKS]
    conv_second_new, conv_new = plain_step(conv_grad, conv_weight, conv_second, decay_rate)
    norm_second_new = jnp.stack([pair_item[0] for pair_item in norm_pairs])
    norm_new = jnp.stack([pair_item[1] for pair_item in norm_pairs])
    bias_second_new = jnp.stack([pair_item[0] for pair_item in bias_pairs])
    bias_new = jnp.stack([pair_item[1] for pair_item in bias_pairs])
    kernel_second_new = jnp.concatenate([pair_item[0] for pair_item in kernel_pairs], axis=0)
    kernel_new = jnp.concatenate([pair_item[1] for pair_item in kernel_pairs], axis=0)
    return (block_out, patch_grad, qkv_grad, out_grad, norm_grad, bias_grad, kernel_grad, conv_grad, qkv_rows_new, qkv_cols_new, out_rows_new, out_cols_new, norm_second_new, bias_second_new, kernel_second_new, conv_second_new, qkv_new, out_new, norm_new, bias_new, kernel_new, conv_new)
```

```python
import functools
import math

import jax
import jax.numpy as jnp
from jax import lax
from jax.experimental import pallas as pl
from jax.experimental.pallas import tpu as pltpu
from jax.sharding import PartitionSpec as P

HEADS = 8
HD = 64
PINV_ITERS = 6
STEP = 10
TAPS = 33
REACH = 16

EPS_NORM = 1e-05
EPS_FACTOR = 1e-30
RATE = 0.5
BLOCKS = ((0, 49), (49, 74), (74, 83))

SMALL = 16
CONV_ROW = 13
NORM_ROW = 14
ROOM = 16
GRID_ROOM = 18
LARGE_ROOM = 56
PULL_ROOM = 56
MARK_ROOM = 56
PULL_MICROS = 2
F32 = jnp.float32
BF16 = jnp.bfloat16


def swap(value, axis, bit):
    return swap_bits(value, axis, 1 << bit)


def swap_bits(value, axis, bits):
    count = lax.axis_size(axis)
    return lax.ppermute(value, axis, [(i, i ^ bits) for i in range(count)])


def bit_of(axis, bit):
    return (lax.axis_index(axis) >> bit) & 1


def keep_half(value, axis, bit):
    mine = bit_of(axis, bit)
    kept = lax.dynamic_index_in_dim(value, mine, 0, keepdims=False)
    sent = lax.dynamic_index_in_dim(value, 1 - mine, 0, keepdims=False)
    return kept + swap(sent, axis, bit)


def join_half(value, axis, bit):
    other = swap(value, axis, bit)
    first = bit_of(axis, bit) == 0
    return jnp.stack([jnp.where(first, value, other), jnp.where(first, other, value)])


def all_sum(value, axis, first_bit=0):
    bits = (lax.axis_size(axis) - 1).bit_length()
    for bit in range(first_bit, bits):
        value = value + swap(value, axis, bit)
    return value


def sum_to_owner(scalars, kept, sent, after=None, direct=()):
    received = swap(sent, "patch", 0)
    count = lax.axis_size("patch")
    if kept.shape[0] != 2:
        return all_sum((kept + received)[0], "patch", 1)
    flat = (2 * kept.shape[1], kept.shape[2])
    kept, sent = fold_halves(
        scalars, kept.reshape(flat), received.reshape(flat), 1, scalars, F32
    )
    if direct and count >= 8:
        near, far = swap_bits(sent, "patch", 2), swap_bits(sent, "patch", 6)
        value = add_four(kept, swap_bits(kept, "patch", 4), near, far, direct)
        return all_sum(value, "patch", 3)
    received = swap(sent, "patch", 1)
    value = kept + received if after is None else add_parts(kept, received, after)
    return all_sum(value, "patch", 2)


def from_owner(value, heads, scalars, after):
    if heads == 2:
        value = join_heads(scalars, value, swap(value, "patch", 1), after)
    else:
        value = value[None]
    return join_half(value, "patch", 0)


def sum_rows(scalars, kept, sent, small, axis, orders):
    bits = (lax.axis_size(axis) - 1).bit_length()
    for bit in range(1, bits):
        received = swap(sent, axis, bit - 1)
        after = orders[bit - 1] if bit <= len(orders) else scalars
        kept, sent = fold_halves(scalars, kept, received, bit, after)
    value = (kept + swap(sent, axis, bits - 1).astype(F32)).astype(BF16)
    for bit in reversed(range(bits)):
        rows = value.shape[0]
        small = lax.reduce_precision(small, 8, 7)
        other = swap(jnp.concatenate([value, small.astype(BF16)], axis=0), axis, bit)
        small = small + other[rows:].astype(F32)
        other = other[:rows]
        first = bit_of(axis, bit) == 0
        value = jnp.concatenate(
            [jnp.where(first, value, other), jnp.where(first, other, value)], axis=0
        )
    return value, small


def neighbours(value, width, kind=BF16):
    count = lax.axis_size("patch")
    odd = bit_of("patch", 0) == 1
    last = value.shape[-1] - width
    axis = value.ndim - 1
    inner = lax.dynamic_slice_in_dim(value, jnp.where(odd, 0, last), width, axis)
    outer = lax.dynamic_slice_in_dim(value, jnp.where(odd, last, 0), width, axis)
    inner, outer = inner.astype(kind), outer.astype(kind)
    inner = swap(inner, "patch", 0)
    steps = [(i, i + 1) for i in range(1, count - 1, 2)]
    outer = lax.ppermute(outer, "patch", steps + [(j, i) for i, j in steps])
    return inner, outer


def in_order(scalars_ref, inner, outer):
    odd = scalars_ref[2] == 1
    return jnp.where(odd, inner, outer), jnp.where(odd, outer, inner)


NN = (((1,), (0,)), ((), ()))
NT = (((1,), (1,)), ((), ()))
TN = (((0,), (0,)), ((), ()))


def dot(left, right, dims=NN):
    return lax.dot_general(left, right, dims, preferred_element_type=F32)


def parts(value):
    high = value.astype(BF16)
    return high, (value - high.astype(F32)).astype(BF16)


def dot3(left, right, dims=NN):
    return dot(left[0], right[0], dims) + (
        dot(left[0], right[1], dims) + dot(left[1], right[0], dims)
    )


def eye(size):
    rows = lax.broadcasted_iota(jnp.int32, (size, size), 0)
    cols = lax.broadcasted_iota(jnp.int32, (size, size), 1)
    return (rows == cols).astype(F32)


HALF = PINV_ITERS // 2


def inverse_turns(product, inverse, turns, q_ref, p_ref):
    identity = eye(product.shape[0])
    for turn in range(turns):
        p_ref[turn] = product
        now = parts(product)
        square = dot3(now, now)
        square_parts = parts(square)
        cube = dot3(square_parts, now)
        fourth = dot3(square_parts, square_parts)
        factor = 0.25 * (13.0 * identity - 15.0 * product + 7.0 * square - cube)
        q_ref[turn] = factor
        inverse = dot3(parts(inverse), parts(factor))
        product = 0.25 * (13.0 * product - 15.0 * square + 7.0 * cube - fourth)
    return product, inverse


def inverse_early_kernel(marks_ref, kernel_ref, q_ref, p_ref, carried_ref, done_ref):
    done_ref[...] = jnp.zeros_like(done_ref)
    marks = marks_ref[...]
    scores = dot(marks[:HD], marks[HD:], TN)
    raised = jnp.exp(scores - jnp.max(scores, axis=-1, keepdims=True))
    kernel = raised * (1.0 / jnp.sum(raised, axis=-1, keepdims=True))
    kernel_ref[...] = kernel
    scale = 1.0 / norm_of(kernel)
    halves = parts(kernel)
    product = dot3(halves, halves, NT) * scale
    carried_ref[0], carried_ref[1] = inverse_turns(product, kernel.T * scale, HALF, q_ref, p_ref)


def inverse_late_kernel(carried_ref, z_ref, q_ref, p_ref):
    turns = PINV_ITERS - HALF
    _, z_ref[...] = inverse_turns(carried_ref[0], carried_ref[1], turns, q_ref, p_ref)


def norm_of(kernel):
    return jnp.sum(jnp.sum(kernel * kernel, axis=0, keepdims=True), axis=1, keepdims=True)


def mixed_marks_kernel(sums_ref, z_ref, out_ref):
    values = sums_ref[:HD] / sums_ref[HD : HD + 1]
    out_ref[...] = dot3(parts(values), parts(z_ref[...]), NT).astype(BF16)


def grad_values_kernel(sums_ref, grads_ref, z_ref, out_ref):
    weight_sum = sums_ref[HD : HD + 1]
    values = sums_ref[:HD] / weight_sum
    left = dot3(parts(grads_ref[...]), parts(z_ref[...]))
    high, low = parts(-jnp.sum(left * values, axis=0, keepdims=True) / weight_sum)
    rows = out_ref.shape[0] - HD
    row = lax.broadcasted_iota(jnp.int32, (rows, out_ref.shape[1]), 0)
    tail = jnp.where(row == 0, high.astype(F32), jnp.where(row == 1, low.astype(F32), 0.0))
    out_ref[:HD] = (left / weight_sum).astype(BF16)
    out_ref[HD:] = tail.astype(BF16)


def total_of(value):
    return jnp.sum(jnp.sum(value, axis=0, keepdims=True), axis=1, keepdims=True)


def even(value):
    return 0.5 * (value + value.T)


def pull_turns(carried, turns, q_ref, p_ref, thin_ref, first):
    for turn in reversed(range(turns)):
        product = parts(p_ref[turn])
        left, right = thin_ref[first + turn], thin_ref[PINV_ITERS + first + turn]
        outer = dot3(parts(left), parts(right), TN)
        held = 0.0
        if carried is not None:
            now = parts(carried)
            outer = outer + dot3(product, now)
            held = dot3(now, parts(q_ref[turn]))
        outer = even(outer)
        once = dot3(product, parts(outer))
        once_parts = parts(once)
        twice = dot3(product, once_parts) + 0.5 * dot3(once_parts, product)
        carried = even(held + 3.5 * once - 0.5 * twice) - 3.75 * outer
    return carried


def chains_kernel(sums_ref, grads_ref, kernel_ref, early_ref, late_ref, thin_ref, done_ref):
    kernel = kernel_ref[...]
    factors = [parts(early_ref[turn]) for turn in range(HALF)]
    factors += [parts(late_ref[turn]) for turn in range(PINV_ITERS - HALF)]
    right = sums_ref[:HD] / sums_ref[HD : HD + 1]
    left = dot3(parts(grads_ref[...]), parts(kernel), NT) * (1.0 / norm_of(kernel))
    for turn in range(PINV_ITERS):
        back = PINV_ITERS - 1 - turn
        thin_ref[turn] = left
        thin_ref[PINV_ITERS + back] = right
        left = dot3(parts(left), factors[turn])
        right = dot3(parts(right), factors[back])
    thin_ref[2 * PINV_ITERS] = right
    done_ref[...] = jnp.zeros_like(done_ref)


def pull_late_kernel(thin_ref, q_ref, p_ref, out_ref):
    out_ref[...] = pull_turns(None, PINV_ITERS - HALF, q_ref, p_ref, thin_ref, HALF)


def pull_early_kernel(carried_ref, marks_ref, grads_ref, kernel_ref, q_ref, p_ref, thin_ref, out_ref):
    marks = marks_ref[...]
    kernel = kernel_ref[...]
    scale = 1.0 / norm_of(kernel)
    halves = parts(kernel)
    grads = grads_ref[...]
    whole = parts(thin_ref[2 * PINV_ITERS])
    carried = pull_turns(carried_ref[...], HALF, q_ref, p_ref, thin_ref, 0)
    mixed = dot3(whole, halves) * scale
    grad_norm = -(total_of(grads * mixed) + total_of(carried * p_ref[0])) * scale
    grad_kernel = (
        dot3(whole, parts(grads), TN) * scale
        + (2.0 * scale) * dot3(parts(carried), halves)
        + 2.0 * grad_norm * kernel
    )
    grad_scores = kernel * (grad_kernel - jnp.sum(kernel * grad_kernel, axis=-1, keepdims=True))
    high, low = parts(grad_scores)
    out_ref[:HD] = dot(marks[HD:], high, NT) + dot(marks[HD:], low, NT)
    out_ref[HD:] = dot(marks[:HD], high) + dot(marks[:HD], low)


def ordered(kernel, count, inputs):
    def body(*refs):
        return kernel(*refs[: inputs - count], *refs[inputs:])

    return body


ANYWHERE = pl.BlockSpec(memory_space=pl.ANY)
WHOLE = pl.BlockSpec(memory_space=pltpu.VMEM)
SCALARS = pl.BlockSpec(memory_space=pltpu.SMEM)
STAY = pl.BlockSpec(memory_space=pltpu.HBM)


def call(kernel, outs, micros, room=ROOM, **grid):
    return pl.pallas_call(
        kernel,
        out_shape=outs,
        compiler_params=pltpu.CompilerParams(vmem_limit_bytes=room * 1024 * 1024),
        **grid,
        cost_estimate=pl.CostEstimate(
            flops=int(micros * 10**9), bytes_accessed=1024, transcendentals=0
        ),
    )


def inverse_early(marks, after):
    size = marks.shape[-1]
    stack = jax.ShapeDtypeStruct((HALF, size, size), F32)
    return call(
        ordered(inverse_early_kernel, 1, 2),
        (
            jax.ShapeDtypeStruct((size, size), F32),
            stack,
            stack,
            jax.ShapeDtypeStruct((2, size, size), F32),
            jax.ShapeDtypeStruct((8, 128), F32),
        ),
        0.1,
        room=MARK_ROOM,
        in_specs=[WHOLE, ANYWHERE],
    )(marks, after)


def inverse_late(carried, after):
    size = carried.shape[-1]
    stack = jax.ShapeDtypeStruct((PINV_ITERS - HALF, size, size), F32)
    return call(
        ordered(inverse_late_kernel, 1, 2),
        (jax.ShapeDtypeStruct((size, size), F32), stack, stack),
        0.1,
        room=MARK_ROOM,
        in_specs=[WHOLE, ANYWHERE],
    )(carried, after)


def mixed_marks_of(sums, inverse, after):
    return call(
        ordered(mixed_marks_kernel, 1, 3),
        jax.ShapeDtypeStruct((HD, sums.shape[1]), BF16),
        0.1,
        in_specs=[WHOLE] * 2 + [ANYWHERE],
    )(sums, inverse, after)


def grad_values_of(sums, grads, inverse, after):
    return call(
        ordered(grad_values_kernel, 1, 4),
        jax.ShapeDtypeStruct((HD + 16, sums.shape[1]), BF16),
        0.1,
        in_specs=[WHOLE] * 3 + [ANYWHERE],
    )(sums, grads, inverse, after)


def thin_chains(sums, grads, kernel, early, late):
    size = kernel.shape[-1]
    return call(
        chains_kernel,
        (
            jax.ShapeDtypeStruct((2 * PINV_ITERS + 1, HD, size), F32),
            jax.ShapeDtypeStruct((8, 128), F32),
        ),
        1,
        room=PULL_ROOM,
    )(sums, grads, kernel, early, late)


def landmark_pull(marks, grads, kernel, early, late, thin, after, later):
    size = kernel.shape[-1]
    carried = call(
        ordered(pull_late_kernel, 1, 4),
        jax.ShapeDtypeStruct((size, size), F32),
        PULL_MICROS,
        room=PULL_ROOM,
        in_specs=[WHOLE] * 3 + [ANYWHERE],
    )(thin, *late, after)
    return call(
        ordered(pull_early_kernel, len(later), 7 + len(later)),
        jax.ShapeDtypeStruct((2 * HD, size), F32),
        PULL_MICROS,
        room=PULL_ROOM,
        in_specs=[WHOLE] * 7 + [ANYWHERE] * len(later),
    )(carried, marks, grads, kernel, *early, thin, *later)


def finish_kernel(sums_ref, inverse_ref, counts_ref, out_ref):
    out_ref[...] = ((sums_ref[...] + inverse_ref[...]) / counts_ref[...]).astype(BF16)


def finish_marks(sums, inverse, counts, after):
    return call(
        ordered(finish_kernel, 1, 4),
        jax.ShapeDtypeStruct(sums.shape, BF16),
        0.5,
        in_specs=[WHOLE] * 3 + [ANYWHERE],
    )(sums, inverse, counts, after)


def fold_kernel(bit, scalars_ref, kept_ref, received_ref, out_kept_ref, out_sent_ref):
    value = kept_ref[...] + received_ref[...].astype(F32)
    half = value.shape[0] // 2
    own_first = scalars_ref[2 + bit] == 0
    first, second = value[:half], value[half:]
    out_kept_ref[...] = jnp.where(own_first, first, second)
    out_sent_ref[...] = jnp.where(own_first, second, first).astype(out_sent_ref.dtype)


def fold_halves(scalars, kept, received, bit, after, kind=BF16):
    shape = (kept.shape[0] // 2, kept.shape[1])
    return call(
        ordered(functools.partial(fold_kernel, bit), 1, 4),
        (jax.ShapeDtypeStruct(shape, F32), jax.ShapeDtypeStruct(shape, kind)),
        0.1,
        in_specs=[SCALARS, WHOLE, WHOLE, ANYWHERE],
    )(scalars, kept, received, after)


def add_kernel(first_ref, second_ref, out_ref):
    out_ref[...] = first_ref[...] + second_ref[...]


def add_four_kernel(kept_ref, beside_ref, near_ref, far_ref, out_ref):
    out_ref[...] = (kept_ref[...] + beside_ref[...]) + (near_ref[...] + far_ref[...])


def add_four(kept, beside, near, far, after):
    return call(
        ordered(add_four_kernel, len(after), 4 + len(after)),
        jax.ShapeDtypeStruct(kept.shape, kept.dtype),
        0.1,
        in_specs=[WHOLE] * 4 + [ANYWHERE] * len(after),
    )(kept, beside, near, far, *after)


def add_parts(first, second, after):
    return call(
        ordered(add_kernel, 1, 3),
        jax.ShapeDtypeStruct(first.shape, first.dtype),
        0.1,
        in_specs=[WHOLE, WHOLE, ANYWHERE],
    )(first, second, after)


def join_kernel(scalars_ref, own_ref, other_ref, out_ref):
    own, other = own_ref[...], other_ref[...]
    own_first = scalars_ref[3] == 0
    out_ref[0] = jnp.where(own_first, own, other)
    out_ref[1] = jnp.where(own_first, other, own)


def join_heads(scalars, own, other, after):
    return call(
        ordered(join_kernel, 1, 4),
        jax.ShapeDtypeStruct((2,) + own.shape, own.dtype),
        0.1,
        in_specs=[SCALARS, WHOLE, WHOLE, ANYWHERE],
    )(scalars, own, other, after)


def row_of(column):
    return jnp.broadcast_to(column, (column.shape[0], 128)).T[:1]


def column_of(row):
    return jnp.broadcast_to(row, (8, row.shape[1])).T[:, :1]


def segments_of(starts, scalars_ref, tokens, offset=0):
    size = starts.shape[1]
    starts = starts.astype(F32)
    lane = lax.broadcasted_iota(jnp.int32, (1, size), 1)
    last = scalars_ref[1].astype(F32)
    ends = jnp.where(lane == size - 1, last, pltpu.roll(starts, size - 1, 1))
    place = lax.broadcasted_iota(jnp.int32, (1, tokens), 1) + (scalars_ref[0] + offset)
    place = place.astype(F32)
    member = (place >= column_of(starts)) & (place < column_of(ends))
    return jnp.where(member, 1.0, 0.0).astype(BF16)


def full_kernel(kernels):
    channels = kernels.shape[1]
    large_part = kernels[0:49].reshape(7, 7, channels)
    middle_part = jnp.pad(kernels[49:74].reshape(5, 5, channels), ((1, 1), (1, 1), (0, 0)))
    small_part = jnp.pad(kernels[74:83].reshape(3, 3, channels), ((2, 2), (2, 2), (0, 0)))
    return large_part + middle_part + small_part


def lay_grid(scalars_ref, inner_ref, own_ref, outer_ref, padded_ref, shifted_ref):
    rows, cols, feats = shifted_ref.shape[1:]
    padded_ref[:, 0:8] = jnp.zeros((rows, 8, feats), F32)
    padded_ref[:, 8 + cols :] = jnp.zeros((rows, 8, feats), F32)

    def laid(value):
        return value.astype(F32).T.reshape(-1, cols, feats)

    before, after = in_order(scalars_ref, inner_ref[0], outer_ref[0])
    padded_ref[0:3, 8 : 8 + cols] = laid(before)
    padded_ref[3 : rows - 3, 8 : 8 + cols] = laid(own_ref[0])
    padded_ref[rows - 3 :, 8 : 8 + cols] = laid(after)
    for col in range(7):
        shifted_ref[col] = padded_ref[:, 5 + col : 5 + col + cols]


def back_kernel(scalars_ref, before_ref, own_ref, after_ref, taps_ref, out_ref, low_ref, sums_ref, padded_ref, shifted_ref, flat_ref):
    lay_grid(scalars_ref, before_ref, own_ref, after_ref, padded_ref, shifted_ref)
    rows, cols, feats = shifted_ref.shape[1:]

    def one_row(row, sums):
        centre = shifted_ref[3, row + 3]
        total = centre
        for col in range(7):
            for shift in range(7):
                tap = 48 - (shift * 7 + col)
                total = total + taps_ref[tap : tap + 1] * shifted_ref[col, row + shift]
        flat_ref[row] = total
        return (
            sums[0] + jnp.sum(total, axis=0, keepdims=True),
            sums[1] + jnp.sum(centre, axis=0, keepdims=True),
        )

    zero = jnp.zeros((1, feats), F32)
    sums = lax.fori_loop(0, rows - 6, one_row, (zero, zero))
    sums = jnp.concatenate([sums[0], sums[1], jnp.zeros((6, feats), F32)], axis=0)

    @pl.when(pl.program_id(0) == 0)
    def _():
        sums_ref[...] = sums

    @pl.when(pl.program_id(0) > 0)
    def _():
        sums_ref[...] += sums

    back = flat_ref[...].reshape(-1, feats).T
    out_ref[0] = back
    low_ref[0] = back.astype(BF16)


def kernel_grad_kernel(scalars_ref, inner_ref, own_ref, outer_ref, cot_ref, held_ref, grad_ref, padded_ref, shifted_ref, cot_grid_ref):
    lay_grid(scalars_ref, inner_ref, own_ref, outer_ref, padded_ref, shifted_ref)
    rows, cols, feats = shifted_ref.shape[1:]
    cot_grid_ref[...] = cot_ref[0].astype(F32).T.reshape(-1, cols, feats)
    grad_ref[...] = held_ref[...]

    def one_row(row, carried):
        cot = cot_grid_ref[row]
        for col in range(7):
            for shift in range(7):
                cells = cot * shifted_ref[col, row + shift]
                grad_ref[shift * 7 + col] += jnp.sum(cells.reshape(-1, 8, feats), axis=0)
        return carried

    lax.fori_loop(0, rows - 6, one_row, 0)


def mix_kernel(scalars_ref, inner_ref, own_ref, outer_ref, taps_ref, biases_ref, out_ref, padded_ref, shifted_ref, flat_ref):
    lay_grid(scalars_ref, inner_ref, own_ref, outer_ref, padded_ref, shifted_ref)
    rows, cols, feats = shifted_ref.shape[1:]
    bias = biases_ref[1:2] + biases_ref[2:3] + biases_ref[3:4]

    def one_row(row, carried):
        total = shifted_ref[3, row + 3] + bias
        for col in range(7):
            for shift in range(7):
                tap = shift * 7 + col
                total = total + taps_ref[tap : tap + 1] * shifted_ref[col, row + shift]
        flat_ref[row] = total
        return carried

    lax.fori_loop(0, rows - 6, one_row, 0)
    out_ref[0] = flat_ref[...].reshape(-1, feats).T.astype(BF16)


def grid_scratch(rows, cols, feats):
    return [
        pltpu.VMEM((rows + 6, cols + 16, feats), F32),
        pltpu.VMEM((7, rows + 6, cols, feats), F32),
        pltpu.VMEM((rows, cols, feats), F32),
    ]


def per_slide(shape):
    zeros = (0,) * (len(shape) - 1)
    return pl.BlockSpec((1,) + tuple(shape[1:]), lambda s: (s,) + zeros)


def whole_block(shape):
    zeros = (0,) * len(shape)
    return pl.BlockSpec(tuple(shape), lambda *_: zeros)


def grid_back(scalars, before, own, after, taps, cols, first):
    slides, feats, tokens = own.shape
    rows = tokens // cols
    return call(
        ordered(back_kernel, 1, 6),
        (
            jax.ShapeDtypeStruct(own.shape, F32),
            jax.ShapeDtypeStruct(own.shape, BF16),
            jax.ShapeDtypeStruct((8, feats), F32),
        ),
        8,
        room=GRID_ROOM,
        grid=(slides,),
        in_specs=[
            SCALARS,
            per_slide(before.shape),
            per_slide(own.shape),
            per_slide(after.shape),
            whole_block(taps.shape),
            ANYWHERE,
        ],
        out_specs=(per_slide(own.shape), per_slide(own.shape), whole_block((8, feats))),
        scratch_shapes=grid_scratch(rows, cols, feats),
    )(scalars, before, own, after, taps, first)


def one_slide(slide, shape):
    return pl.BlockSpec((1,) + tuple(shape[1:]), lambda i: (slide, 0, 0))


def grid_kernel_grad(scalars, inner, own, outer, cotangent, held, cols, slide):
    slides, feats, tokens = own.shape
    rows = tokens // cols
    return call(
        kernel_grad_kernel,
        jax.ShapeDtypeStruct(held.shape, F32),
        1,
        room=GRID_ROOM,
        grid=(1,),
        in_specs=[SCALARS]
        + [one_slide(slide, item.shape) for item in (inner, own, outer, cotangent)]
        + [whole_block(held.shape)],
        out_specs=whole_block(held.shape),
        scratch_shapes=grid_scratch(rows, cols, feats),
    )(scalars, inner, own, outer, cotangent, held)


def grid_mix(scalars, inner, own, outer, taps, biases, cols, slide, out=None):
    slides, feats, tokens = own.shape
    rows = tokens // cols
    kernel, extra, specs, aliases = mix_kernel, (), [], {}
    if out is not None:
        kernel, extra, specs, aliases = ordered(mix_kernel, 1, 7), (out,), [ANYWHERE], {6: 0}
    return call(
        kernel,
        jax.ShapeDtypeStruct(own.shape, BF16),
        1,
        room=GRID_ROOM,
        grid=(1,),
        in_specs=[SCALARS]
        + [one_slide(slide, item.shape) for item in (inner, own, outer)]
        + [whole_block(item.shape) for item in (taps, biases)]
        + specs,
        out_specs=one_slide(slide, own.shape),
        scratch_shapes=grid_scratch(rows, cols, feats),
        input_output_aliases=aliases,
    )(scalars, inner, own, outer, taps, biases, *extra)


def pack_kernel(sums_ref, bias_ref, lines_ref, conv_ref, out_ref):
    feats = sums_ref.shape[2]
    share = out_ref.shape[1] // feats
    out_ref[...] = jnp.zeros_like(out_ref)
    totals = jnp.sum(sums_ref[...], axis=1)
    for row in range(51):
        line = totals[row : row + 1] if row < 49 else bias_ref[row - 49 : row - 48]
        at = row % share * feats
        out_ref[row // share : row // share + 1, at : at + feats] = line
    for head in range(conv_ref.shape[0]):
        line = conv_ref[head, :, 0:1]
        line = jnp.concatenate([line, jnp.zeros((64 - line.shape[0], 1), F32)], axis=0)
        out_ref[CONV_ROW : CONV_ROW + 1, head * 64 : head * 64 + 64] = row_of(line)
    out_ref[NORM_ROW : NORM_ROW + 2] = lines_ref[0:2]


def pack_sums(sums, bias_sums, lines, conv, full):
    return call(pack_kernel, jax.ShapeDtypeStruct((SMALL, full), F32), 0.2)(
        sums, bias_sums, lines, conv
    )


def lay_line(before, rows, after, line_ref):
    tokens = rows.shape[1]
    width = line_ref.shape[1]
    line_ref[:, :REACH] = before
    line_ref[:, REACH : REACH + tokens] = rows
    line_ref[:, REACH + tokens : 2 * REACH + tokens] = after
    line_ref[:, 2 * REACH + tokens :] = jnp.zeros((HD, width - tokens - 2 * REACH), BF16)


def line_width(tokens):
    return (-(-tokens // 128) + 1) * 128


def pairs_of(ref):
    return [(s, h) for h in range(ref.shape[1]) for s in range(ref.shape[0])]


def band(line):
    wide = jnp.broadcast_to(line, (128, 256))
    return parts(pltpu.roll(wide, 0, 1, stride=1, stride_axis=0))


def line_conv(line_ref, bands, out_ref, at):
    tokens = out_ref.shape[-1]
    high, low = bands
    for begin in range(0, tokens, 128):
        width = min(128, tokens - begin)
        held = line_ref[:, begin : begin + 256]
        out = dot(held, high, NT) + dot(held, low, NT)
        out_ref[at[0], at[1], :, begin : begin + width] = out[:, :width].astype(out_ref.dtype)


def residual_kernel(scalars_ref, inner_ref, rows_ref, outer_ref, taps_ref, out_ref, done_ref, lines_ref):
    done_ref[...] = jnp.zeros_like(done_ref)
    for index, at in enumerate(pairs_of(rows_ref)):
        line_ref = lines_ref.at[index]
        before, after = in_order(scalars_ref, inner_ref[at], outer_ref[at])
        lay_line(before, rows_ref[at[0], at[1], 2 * HD :], after, line_ref)
        line_conv(line_ref, band(taps_ref[at[1]]), out_ref, at)


def back_line_kernel(
    scalars_ref, value_inner_ref, rows_ref, value_outer_ref, inner_ref, low_ref, outer_ref, taps_ref,
    out_ref, grad_ref, values_ref, lines_ref,
):
    tokens = out_ref.shape[-1]
    gap = lax.broadcasted_iota(jnp.int32, (128, 256), 1) - lax.broadcasted_iota(
        jnp.int32, (128, 256), 0
    )
    cross = jnp.zeros((128, 256), F32)
    for index, at in enumerate(pairs_of(rows_ref)):
        value_ref, line_ref = values_ref.at[index], lines_ref.at[index]
        rows = rows_ref[at[0], at[1], 2 * HD :]
        before, after = in_order(scalars_ref, value_inner_ref[at], value_outer_ref[at])
        lay_line(before, rows, after, value_ref)
        before, after = in_order(scalars_ref, inner_ref[at], outer_ref[at])
        lay_line(before, low_ref[at], after, line_ref)
        line_conv(line_ref, band(taps_ref[at[1]]), out_ref, at)
        for begin in range(0, tokens, 128):
            width = min(128, tokens - begin)
            lane = lax.broadcasted_iota(jnp.int32, (HD, 256), 1)
            inside = (lane >= REACH) & (lane < REACH + width)
            centre = line_ref[:, begin : begin + 256].astype(F32)
            centre = jnp.where(inside, centre, 0.0).astype(BF16)
            held = value_ref[:, begin : begin + 256]
            cross = cross + dot(centre, held, TN)[: 128 + REACH][REACH:]
        if at[0] == rows_ref.shape[0] - 1:
            lines = [
                jnp.sum(jnp.where(gap == tap, cross, 0.0), axis=0, keepdims=True)
                for tap in range(TAPS)
            ]
            lines.append(jnp.zeros((40 - TAPS, 256), F32))
            totals = jnp.sum(jnp.concatenate(lines, axis=0), axis=1, keepdims=True)
            grad_ref[at[1]] = jnp.broadcast_to(totals, (40, 128))
            cross = jnp.zeros((128, 256), F32)


def line_taps(conv_weight):
    return jnp.pad(conv_weight, ((0, 0), (0, 256 - TAPS)))[:, None, :]


def residual_of(scalars, before, rows, after, conv_weight):
    slides, heads, _, tokens = rows.shape
    return call(
        residual_kernel,
        (
            jax.ShapeDtypeStruct((slides, heads, HD, tokens), F32),
            jax.ShapeDtypeStruct((8, 128), F32),
        ),
        0.1,
        in_specs=[SCALARS] + [WHOLE] * 4,
        scratch_shapes=[pltpu.VMEM((slides * heads, HD, line_width(tokens)), BF16)],
    )(scalars, before, rows, after, line_taps(conv_weight))


def back_line(scalars, value_before, rows, value_after, before, low, after, conv_weight, later):
    slides, heads, _, tokens = rows.shape
    lines = pltpu.VMEM((slides * heads, HD, line_width(tokens)), BF16)
    return call(
        ordered(back_line_kernel, 1, 9),
        (
            jax.ShapeDtypeStruct((slides, heads, HD, tokens), BF16),
            jax.ShapeDtypeStruct((heads, 40, 128), F32),
        ),
        1,
        in_specs=[SCALARS] + [WHOLE] * 7 + [ANYWHERE],
        scratch_shapes=[lines, lines],
    )(scalars, value_before, rows, value_after, before, low, after, line_taps(conv_weight[:, ::-1]), later)


def put_halves(kept_ref, sent_ref, mine, sums):
    own_first = mine == 0
    for head, (first, second) in enumerate(zip(*sums)):
        kept_ref[head] = jnp.where(own_first, first, second)
        sent_ref[head] = jnp.where(own_first, second, first)


def all_blocks(shape):
    zeros = (0,) * (len(shape) - 2)
    return pl.BlockSpec((shape[0], 1) + tuple(shape[2:]), lambda s: (0, s) + zeros)


def norm_kernel(scalars_ref, gathered_ref, weight_ref, norm_ref, mask_ref, starts_ref, normed_ref, stats_ref, rows_ref, kept_ref, sent_ref, sums_ref):
    count, _, feats, tokens = gathered_ref.shape
    heads = rows_ref.shape[1]
    full = feats * count
    slide, chunk = pl.program_id(0), pl.program_id(1)
    total, squares = 0.0, 0.0
    for slot in range(count):
        cells = gathered_ref[slot, 0].astype(F32)
        total = total + jnp.sum(cells, axis=0, keepdims=True)
        squares = squares + jnp.sum(cells * cells, axis=0, keepdims=True)
    mean = total / full
    inv_std = lax.rsqrt(squares / full - mean * mean + EPS_NORM)
    stats_ref[0] = jnp.concatenate([mean, inv_std, jnp.zeros((6, tokens), F32)], axis=0)
    gain, bias = column_of(norm_ref[0:1]), column_of(norm_ref[1:2])
    for slot in range(count):
        span = slice(slot * feats, (slot + 1) * feats)
        centered = (gathered_ref[slot, 0].astype(F32) - mean) * inv_std
        normed_ref[0, span] = (centered * gain[span] + bias[span]).astype(BF16)
    normed = normed_ref[0]
    mask = mask_ref[slide, chunk].astype(F32)
    onehot = segments_of(starts_ref[pl.ds(slide, 1)], scalars_ref, tokens, chunk * tokens)
    counts = dot(jnp.broadcast_to(mask, (16, tokens)).astype(BF16), onehot, NT)[:8]
    own = scalars_ref[2] == slide
    fresh = chunk == 0
    for head in range(heads):
        row = head * 3 * HD
        projected = dot(weight_ref[row : row + 3 * HD], normed)
        rows_ref[0, head, :HD] = (projected[:HD] * mask * HD ** (-0.5)).astype(BF16)
        rows_ref[0, head, HD:] = (projected[HD:] * mask).astype(BF16)
        sums = dot(rows_ref[0, head, : 2 * HD], onehot, NT)
        sums = jnp.concatenate([sums, counts], axis=0) + jnp.where(fresh, 0.0, sums_ref[head])
        sums_ref[head] = sums
        kept_ref[head] = jnp.where(own, sums, kept_ref[head])
        sent_ref[head] = jnp.where(own, sent_ref[head], sums)


def norm_project(scalars, gathered, weight, norm_params, mask, starts, after):
    count, slides, feats, tokens = gathered.shape
    heads = weight.shape[0] // (3 * HD)
    width = 384 if tokens % 384 == 0 else tokens
    chunks = tokens // width
    mask = mask.reshape(slides, chunks, 1, width)
    half = jax.ShapeDtypeStruct((heads, 2 * HD + 8, starts.shape[1]), F32)
    return call(
        ordered(norm_kernel, len(after), 6 + len(after)),
        (
            jax.ShapeDtypeStruct((slides, count * feats, tokens), BF16),
            jax.ShapeDtypeStruct((slides, 8, tokens), F32),
            jax.ShapeDtypeStruct((slides, heads, 3 * HD, tokens), BF16),
            half,
            half,
        ),
        0.1,
        room=LARGE_ROOM,
        grid=(slides, chunks),
        in_specs=[
            SCALARS,
            pl.BlockSpec((count, 1, feats, width), lambda s, c: (0, s, 0, c)),
        ]
        + [whole_block(item.shape) for item in (weight, norm_params, mask, starts)]
        + [ANYWHERE] * len(after),
        out_specs=(
            pl.BlockSpec((1, count * feats, width), lambda s, c: (s, 0, c)),
            pl.BlockSpec((1, 8, width), lambda s, c: (s, 0, c)),
            pl.BlockSpec((1, heads, 3 * HD, width), lambda s, c: (s, 0, 0, c)),
            whole_block(half.shape),
            whole_block(half.shape),
        ),
        scratch_shapes=[pltpu.VMEM(half.shape, F32)],
    )(scalars, gathered, weight, norm_params, mask, starts, *after)


def low_kernel(scalars_ref, far_ref, weight_ref, far_kernel_ref, low_ref, kept_ref, sent_ref, near_ref, kernel_ref, sem, kernel_sem):
    count, slides, feats, tokens = far_ref.shape
    heads = low_ref.shape[1]
    rows, kernels = [], []
    for s in range(slides):
        rows.append(
            [
                pltpu.make_async_copy(far_ref.at[slot, s], near_ref.at[slot, s], sem.at[slot, s])
                for slot in range(count)
            ]
        )
        kernels.append(
            pltpu.make_async_copy(far_kernel_ref.at[s], kernel_ref.at[s], kernel_sem.at[s])
        )
    for s in range(slides):
        for copy in rows[s] + [kernels[s]]:
            copy.start()
    sums = [[None] * heads for _ in range(slides)]
    for s in range(slides):
        for copy in rows[s]:
            copy.wait()
        low = dot(weight_ref[...], near_ref[:, s].reshape(count * feats, tokens)).astype(BF16)
        for head in range(heads):
            low_ref[s, head] = low[head * HD : (head + 1) * HD]
        kernels[s].wait()
        for head in range(heads):
            sums[s][head] = dot(low_ref[s, head], kernel_ref[s, head], NT)
    put_halves(kept_ref, sent_ref, scalars_ref[2], sums)


def head_gradient(scalars, gathered, weight, kernel, after):
    count, slides, feats, tokens = gathered.shape
    heads = feats // HD
    half = jax.ShapeDtypeStruct((heads, HD, kernel.shape[2]), F32)
    return call(
        ordered(low_kernel, 1, 5),
        (jax.ShapeDtypeStruct((slides, heads, HD, tokens), BF16), half, half),
        0.1,
        room=LARGE_ROOM,
        in_specs=[SCALARS, STAY, WHOLE, STAY, ANYWHERE],
        scratch_shapes=[
            pltpu.VMEM(gathered.shape, BF16),
            pltpu.VMEM(kernel.shape, BF16),
            pltpu.SemaphoreType.DMA((count, slides)),
            pltpu.SemaphoreType.DMA((slides,)),
        ],
    )(scalars, gathered, weight, kernel, after)


def section_kernel(gathered_ref, weight_ref, patch_ref, biases_ref, out_ref):
    count, slides, feats, tokens = gathered_ref.shape
    bias = column_of(biases_ref[0:1])
    for s in range(slides):
        branch = dot(weight_ref[...], gathered_ref[:, s].reshape(count * feats, tokens), TN)
        out_ref[s] = patch_ref[s].astype(F32) + branch + bias


def section(gathered, weight, patches, biases):
    return call(section_kernel, jax.ShapeDtypeStruct(patches.shape, F32), 1)(
        gathered, weight, patches, biases
    )


def final_kernel(grad_ref, gain_ref, stats_ref, table_ref, patch_ref, back_ref, out_ref):
    slides, feats, tokens = out_ref.shape
    full = table_ref.shape[1]
    gain = column_of(gain_ref[...])
    lines = {}
    for s, which, row, begin, end in line_pieces(slides, tokens, full):
        lines.setdefault((s, which), []).append(table_ref[row : row + 1, : end - begin])
    for s in range(slides):
        mean, inv_std = stats_ref[s, 0:1], stats_ref[s, 1:2]
        first, second = (jnp.concatenate(lines[s, which], axis=1) / full for which in range(2))
        centered = (patch_ref[s].astype(F32) - mean) * inv_std
        grad = grad_ref[s].astype(F32) * gain - first - centered * second
        out_ref[s] = inv_std * grad + back_ref[s]


def token_probs(marks, queries):
    scores = dot(marks[HD:], queries, TN)
    raised = jnp.exp(scores - jnp.max(scores, axis=0, keepdims=True))
    return raised * (1.0 / jnp.sum(raised, axis=0, keepdims=True))


def token_weights(marks, keys, mask):
    return jnp.exp(dot(marks[:HD], keys, TN)) * mask


def framed(values):
    return jnp.concatenate([values, jnp.ones((16, values.shape[1]), BF16)], axis=0)


def forward_kernel(scalars_ref, rows_ref, marks_ref, mask_ref, kernel_ref, kept_ref, sent_ref):
    sums = [[None] * rows_ref.shape[1] for _ in range(rows_ref.shape[0])]
    for at in pairs_of(rows_ref):
        rows, marks = rows_ref[at], marks_ref[at]
        weights = token_weights(marks, rows[HD : 2 * HD], mask_ref[at[0] : at[0] + 1].astype(F32)).astype(BF16)
        sums[at[0]][at[1]] = dot(framed(rows[2 * HD :]), weights, NT)[: HD + 8]
        kernel_ref[at] = token_probs(marks, rows[:HD]).astype(BF16)
    put_halves(kept_ref, sent_ref, scalars_ref[2], sums)


def mixed_kernel(pack_ref, kernel_ref, residual_ref, out_ref):
    for s, h in pairs_of(pack_ref):
        attended = dot(pack_ref[s, h], kernel_ref[s, h])
        out_ref[s, h * HD : (h + 1) * HD] = (attended + residual_ref[s, h]).astype(BF16)


def pull_one_kernel(rows_ref, marks_ref, pack_ref, low_ref, grads_ref, sums_ref):
    for at in pairs_of(rows_ref):
        queries, marks = rows_ref[at[0], at[1], :HD], marks_ref[at]
        probs = token_probs(marks, queries)
        pulled = probs * dot(pack_ref[at], low_ref[at], TN)
        grad_scores = (pulled - probs * jnp.sum(pulled, axis=0, keepdims=True)).astype(BF16)
        grads_ref[at] = dot(marks[HD:], grad_scores).astype(BF16)
        sums_ref[at] = dot(queries, grad_scores, NT)


def pull_three_kernel(scalars_ref, rows_ref, marks_ref, pack_ref, mask_ref, other_ref, grads_ref, value_ref, kept_ref, sent_ref):
    sums = [[None] * rows_ref.shape[1] for _ in range(rows_ref.shape[0])]
    for at in pairs_of(rows_ref):
        rows, marks, pack = rows_ref[at], marks_ref[at], pack_ref[at]
        keys = rows[HD : 2 * HD]
        raised = token_weights(marks, keys, mask_ref[at[0] : at[0] + 1].astype(F32))
        grad_three = (dot(pack, framed(rows[2 * HD :]), TN) * raised).astype(BF16)
        own = dot(keys, grad_three, NT)
        sums[at[0]][at[1]] = jnp.concatenate([own, other_ref[at]], axis=0)
        grads_ref[at] = dot(marks[:HD], grad_three).astype(BF16)
        value_ref[at] = dot(pack[:HD], raised.astype(BF16)).astype(BF16)
    put_halves(kept_ref, sent_ref, scalars_ref[2], sums)


def token_forward(scalars, rows, marks, mask, after):
    slides, heads, _, tokens = rows.shape
    size = marks.shape[-1]
    half = jax.ShapeDtypeStruct((heads, HD + 8, size), F32)
    return call(
        ordered(forward_kernel, 1, 5),
        (jax.ShapeDtypeStruct((slides, heads, size, tokens), BF16), half, half),
        0.1,
        in_specs=[SCALARS] + [WHOLE] * 3 + [ANYWHERE],
    )(scalars, rows, marks, mask, after)


def mixed_heads(pack, kernel, residual, after):
    slides, heads, size, tokens = kernel.shape
    return call(
        ordered(mixed_kernel, 1, 4),
        jax.ShapeDtypeStruct((slides, heads * HD, tokens), BF16),
        0.1,
        in_specs=[WHOLE] * 3 + [ANYWHERE],
    )(pack, kernel, residual, after)


def pull_one(rows, marks, pack, low, after):
    slides, heads, _, tokens = rows.shape
    return call(
        ordered(pull_one_kernel, 1, 5),
        (
            jax.ShapeDtypeStruct((slides, heads, HD, tokens), BF16),
            jax.ShapeDtypeStruct((slides, heads, HD, marks.shape[-1]), F32),
        ),
        1,
        in_specs=[WHOLE] * 4 + [ANYWHERE],
    )(rows, marks, pack, low, after)


def pull_three(scalars, rows, marks, pack, mask, other, after):
    slides, heads, _, tokens = rows.shape
    half = jax.ShapeDtypeStruct((heads, 2 * HD, marks.shape[-1]), F32)
    token = jax.ShapeDtypeStruct((slides, heads, HD, tokens), BF16)
    return call(
        ordered(pull_three_kernel, 1, 7),
        (token, token, half, half),
        1,
        in_specs=[SCALARS] + [WHOLE] * 5 + [STAY],
    )(scalars, rows, marks, pack, mask, other, after)


def project_kernel(scalars_ref, query_ref, key_ref, value_ref, line_ref, marks_ref, mask_ref, starts_ref, weight_ref, gathered_ref, normed_ref, stats_ref, norm_ref, out_rows_ref, low_ref, near_ref, moments_ref, lines_ref, kept_ref, sent_ref, rows_ref, sums_ref):
    count, slides, feats, tokens = gathered_ref.shape
    heads = query_ref.shape[1]
    gains = column_of(norm_ref[0:1])
    norms = [[0.0, 0.0] for _ in range(count)]
    for s in range(slides):
        mask = mask_ref[s : s + 1].astype(F32)
        onehot = segments_of(starts_ref[s : s + 1], scalars_ref, tokens)
        for head in range(heads):
            row = head * 3 * HD
            spread = dot(marks_ref[s, head], onehot)
            query = (query_ref[s, head].astype(F32) + spread[:HD]).astype(BF16).astype(F32) * mask
            key = (key_ref[s, head].astype(F32) + spread[HD:]).astype(BF16).astype(F32) * mask
            value = (value_ref[s, head].astype(F32) + line_ref[s, head].astype(F32)).astype(BF16)
            rows_ref[s, row : row + HD] = (query * HD ** (-0.5)).astype(BF16)
            rows_ref[s, row + HD : row + 2 * HD] = key.astype(BF16)
            rows_ref[s, row + 2 * HD : row + 3 * HD] = (value.astype(F32) * mask).astype(BF16)
        rows = rows_ref[s]
        mean, inv_std = stats_ref[s, 0:1], stats_ref[s, 1:2]
        first, second = 0.0, 0.0
        for slot in range(count):
            span = slice(slot * feats, (slot + 1) * feats)
            grad = dot(weight_ref[:, span], rows, TN)
            near_ref[slot, s] = grad.astype(BF16)
            centered = (gathered_ref[slot, s].astype(F32) - mean) * inv_std
            pulled = grad * centered
            gain = gains[span]
            first = first + jnp.sum(grad * gain, axis=0, keepdims=True)
            second = second + jnp.sum(pulled * gain, axis=0, keepdims=True)
            norms[slot][0] += jnp.sum(pulled, axis=1, keepdims=True)
            norms[slot][1] += jnp.sum(grad, axis=1, keepdims=True)
        moments_ref[s] = jnp.concatenate([first, second], axis=0)
    qkv_grad = 0.0
    out_grads = [0.0] * count
    for s in range(slides):
        qkv_grad = qkv_grad + dot(rows_ref[s], normed_ref[s], NT)
        for slot in range(count):
            out_grads[slot] += dot(out_rows_ref[s], low_ref[slot, s], NT)
    lines_ref[...] = jnp.zeros_like(lines_ref)
    sums_ref[: 3 * feats] = qkv_grad
    for slot in range(count):
        span = slice(slot * feats, (slot + 1) * feats)
        sums_ref[3 * feats : 4 * feats, span] = out_grads[slot]
        for line in range(2):
            lines_ref[line : line + 1, span] = row_of(norms[slot][line])
    half = sums_ref.shape[0] // 2
    own_first = scalars_ref[2] == 0
    first, second = sums_ref[:half], sums_ref[half:]
    kept_ref[...] = jnp.where(own_first, first, second)
    sent_ref[...] = jnp.where(own_first, second, first).astype(BF16)


def project_back(scalars, query, key, value, line, marks, mask, starts, weight, gathered, normed, stats, norm_params, heads_out, low):
    count, slides, feats, tokens = gathered.shape
    held = (query, key, value, line, marks, mask, starts, weight, gathered, normed, stats, norm_params, heads_out, low)
    return call(
        project_kernel,
        (
            jax.ShapeDtypeStruct((count, slides, feats, tokens), BF16),
            jax.ShapeDtypeStruct((slides, 2, tokens), F32),
            jax.ShapeDtypeStruct((8, count * feats), F32),
            jax.ShapeDtypeStruct((2 * feats, count * feats), F32),
            jax.ShapeDtypeStruct((2 * feats, count * feats), BF16),
        ),
        7,
        in_specs=[SCALARS] + [WHOLE] * len(held),
        scratch_shapes=[
            pltpu.VMEM((slides, weight.shape[0], tokens), BF16),
            pltpu.VMEM((4 * feats, count * feats), F32),
        ],
    )(scalars, *held)


DECAY = 1.0 - STEP ** (-0.8)


def second_of(old, grad):
    return DECAY * old + (1.0 - DECAY) * (grad * grad + EPS_FACTOR)


def shrink(update, usq_sum, weight_sq, entries):
    clip_factor = jnp.maximum(1.0, jnp.sqrt(usq_sum / entries))
    return RATE * jnp.sqrt(weight_sq / entries) * update / clip_factor


def scalar_line(values):
    lane = lax.broadcasted_iota(jnp.int32, (1, 128), 1)
    line = jnp.zeros((1, 128), F32)
    for index, value in values:
        line = jnp.where(lane == index, value, line)
    return line


def block_masks(shape):
    row = lax.broadcasted_iota(jnp.int32, shape, 0)
    return [jnp.where((row >= low) & (row < high), 1.0, 0.0) for low, high in BLOCKS]


def squares_kernel(qkv_ref, out_ref, biases_ref, kernels_ref, conv_ref, line_ref):
    def square(ref):
        value = ref[...]
        return value * value

    biases = square(biases_ref)
    kernels = square(kernels_ref)
    values = [(1, total_of(square(qkv_ref))), (3, total_of(square(out_ref)))]
    values.append((5, total_of(square(conv_ref))))
    values += [(7 + 2 * row, total_of(biases[row : row + 1])) for row in range(4)]
    masks = block_masks(kernels.shape)
    values += [(15 + 2 * block, total_of(kernels * mask)) for block, mask in enumerate(masks)]
    line_ref[...] = jnp.broadcast_to(scalar_line(values), line_ref.shape)


def weight_squares(*weights):
    return call(squares_kernel, jax.ShapeDtypeStruct((8, 128), F32), 2, room=LARGE_ROOM)(*weights)


def weight_grad(sums_ref, feats, index):
    return sums_ref[3 * feats * index : 3 * feats + feats * index].astype(F32)


def conv_grad_of(part_ref, heads):
    row = part_ref[CONV_ROW : CONV_ROW + 1]
    return jnp.concatenate([row[:, 64 * head : 64 * head + TAPS] for head in range(heads)], axis=0)


def part_row(part_ref, feats, row):
    share = part_ref.shape[1] // feats
    at = row % share * feats
    return part_ref[row // share : row // share + 1, at : at + feats]


def lay_bias_grad(part_ref, out_ref):
    feats = out_ref.shape[1]
    for row in range(4):
        out_ref[row : row + 1] = part_row(part_ref, feats, 49 + min(row, 1))


def lay_kernel_grad(part_ref, out_ref):
    feats = out_ref.shape[1]
    taps = list(range(49))
    taps += [7 * row + col for row in range(1, 6) for col in range(1, 6)]
    taps += [7 * row + col for row in range(2, 5) for col in range(2, 5)]
    for row, tap in enumerate(taps):
        out_ref[row : row + 1] = part_row(part_ref, feats, tap)


def rows_new_of(grad, rows):
    mean = jnp.sum(grad * grad, axis=1, keepdims=True) / grad.shape[1]
    return DECAY * column_of(rows) + (1.0 - DECAY) * (mean + EPS_FACTOR)


def line_pieces(slides, tokens, full):
    share = -(-tokens // full)
    return [
        (s, which, 8 + (2 * s + which) * share + piece, piece * full, min(tokens, (piece + 1) * full))
        for s in range(slides)
        for which in range(2)
        for piece in range(share)
    ]


def table_kernel(sums_ref, part_ref, qkv_rows_ref, out_rows_ref, bias_second_ref, kernel_second_ref, conv_second_ref, line_ref, moments_ref, table_ref, bias_ref, kernel_ref):
    feats = bias_second_ref.shape[1]
    heads = conv_second_ref.shape[0]
    values = []
    table_ref[...] = jnp.zeros_like(table_ref)
    for index, rows_ref in enumerate((qkv_rows_ref, out_rows_ref)):
        grad = weight_grad(sums_ref, feats, index)
        squares = grad * grad
        rows_new = rows_new_of(grad, rows_ref[...])
        table_ref[2 * index : 2 * index + 1] = jnp.sum(squares, axis=0, keepdims=True)
        table_ref[2 * index + 1 : 2 * index + 2] = jnp.sum(
            squares * (1.0 / rows_new), axis=0, keepdims=True
        )
        values.append((2 * index, total_of(rows_new)))
    table_ref[4:6] = part_ref[NORM_ROW : NORM_ROW + 2]

    def update_squares(grad, second):
        return grad * grad / second_of(second, grad)

    conv_grad = conv_grad_of(part_ref, heads)
    values.append((4, total_of(update_squares(conv_grad, conv_second_ref[...]))))
    lay_bias_grad(part_ref, bias_ref)
    bias_squares = update_squares(bias_ref[...], bias_second_ref[...])
    values += [(6 + 2 * row, total_of(bias_squares[row : row + 1])) for row in range(4)]
    lay_kernel_grad(part_ref, kernel_ref)
    kernel_squares = update_squares(kernel_ref[...], kernel_second_ref[...])
    masks = block_masks(kernel_squares.shape)
    values += [
        (14 + 2 * block, total_of(kernel_squares * mask)) for block, mask in enumerate(masks)
    ]
    table_ref[6:7, :128] = scalar_line(values) + line_ref[0:1]
    slides, _, tokens = moments_ref.shape
    for s, which, row, begin, end in line_pieces(slides, tokens, table_ref.shape[1]):
        table_ref[row : row + 1, : end - begin] = moments_ref[s, which : which + 1, begin:end]


def optimizer_table(gradients, rows, seconds, line, moments):
    full = gradients[0].shape[1]
    lines = len(line_pieces(moments.shape[0], moments.shape[2], full))
    return call(
        table_kernel,
        jax.ShapeDtypeStruct((8 + -(-lines // 8) * 8, full), F32),
        0.2,
        scratch_shapes=[pltpu.VMEM(seconds[0].shape, F32), pltpu.VMEM(seconds[1].shape, F32)],
    )(*gradients, *rows, *seconds, line, moments)


def state_kernel(sums_ref, part_ref, qkv_rows_ref, out_rows_ref, bias_second_ref, kernel_second_ref, conv_second_ref, qkv_grad_ref, out_grad_ref, bias_grad_ref, kernel_grad_ref, conv_grad_ref, qkv_rows_new_ref, out_rows_new_ref, bias_new_ref, kernel_new_ref, conv_new_ref):
    feats = bias_second_ref.shape[1]
    heads = conv_second_ref.shape[0]
    for index, (rows_ref, grad_ref, rows_new_ref) in enumerate(
        (
            (qkv_rows_ref, qkv_grad_ref, qkv_rows_new_ref),
            (out_rows_ref, out_grad_ref, out_rows_new_ref),
        )
    ):
        grad = weight_grad(sums_ref, feats, index)
        grad_ref[...] = grad
        rows_new_ref[...] = row_of(rows_new_of(grad, rows_ref[...]))
    conv_grad_ref[...] = conv_grad_of(part_ref, heads)
    lay_bias_grad(part_ref, bias_grad_ref)
    lay_kernel_grad(part_ref, kernel_grad_ref)
    conv_new_ref[...] = second_of(conv_second_ref[...], conv_grad_ref[...])
    bias_new_ref[...] = second_of(bias_second_ref[...], bias_grad_ref[...])
    kernel_new_ref[...] = second_of(kernel_second_ref[...], kernel_grad_ref[...])


def optimizer_state(gradients, rows, seconds, weights, after):
    return call(
        ordered(state_kernel, 1, 8),
        tuple(like(item) for item in weights + rows + seconds),
        0.2,
        room=LARGE_ROOM,
        in_specs=[WHOLE] * 7 + [ANYWHERE],
    )(*gradients, *rows, *seconds, after)


def step_kernel(
    table_ref,
    sums_ref,
    part_ref,
    qkv_rows_ref,
    out_rows_ref,
    bias_second_ref,
    kernel_second_ref,
    conv_second_ref,
    qkv_cols_ref,
    out_cols_ref,
    norm_second_ref,
    norm_ref,
    qkv_weight_ref,
    out_weight_ref,
    biases_ref,
    kernels_ref,
    conv_weight_ref,
    norm_grad_ref,
    qkv_cols_new_ref,
    out_cols_new_ref,
    norm_second_new_ref,
    qkv_new_ref,
    out_new_ref,
    norm_new_ref,
    bias_new_ref,
    kernel_new_ref,
    conv_new_ref,
):
    feats, full = out_weight_ref.shape
    heads = conv_weight_ref.shape[0]

    def scalar(index):
        return table_ref[6:7, index : index + 1]

    for index, (rows, cols_ref, cols_new_ref, rows_ref, weight_ref, new_ref) in enumerate(
        (
            (3 * full, qkv_cols_ref, qkv_cols_new_ref, qkv_rows_ref, qkv_weight_ref, qkv_new_ref),
            (full, out_cols_ref, out_cols_new_ref, out_rows_ref, out_weight_ref, out_new_ref),
        )
    ):
        mean = scalar(2 * index) / rows
        cols = DECAY * cols_ref[...] + (1.0 - DECAY) * (
            table_ref[2 * index : 2 * index + 1] / rows + EPS_FACTOR
        )
        cols_new_ref[...] = cols
        usq = mean * total_of(table_ref[2 * index + 1 : 2 * index + 2] / cols)
        grad = weight_grad(sums_ref, feats, index)
        update = grad * lax.rsqrt(rows_new_of(grad, rows_ref[...]) * cols / mean)
        new_ref[...] = weight_ref[...] - shrink(update, usq, scalar(2 * index + 1), rows * full)

    norm_grad = table_ref[4:6]
    norm_grad_ref[...] = norm_grad
    norm_second = second_of(norm_second_ref[...], norm_grad)
    norm_second_new_ref[...] = norm_second
    update = norm_grad * lax.rsqrt(norm_second)
    norm = norm_ref[...]
    norm_new_ref[...] = norm - shrink(
        update,
        jnp.sum(update * update, axis=1, keepdims=True),
        jnp.sum(norm * norm, axis=1, keepdims=True),
        full,
    )

    conv_grad = conv_grad_of(part_ref, heads)
    conv_update = conv_grad * lax.rsqrt(second_of(conv_second_ref[...], conv_grad))
    conv_new_ref[...] = conv_weight_ref[...] - shrink(
        conv_update, scalar(4), scalar(5), HEADS * TAPS
    )
    lay_bias_grad(part_ref, bias_new_ref)
    bias_grad = bias_new_ref[...]
    bias_update = bias_grad * lax.rsqrt(second_of(bias_second_ref[...], bias_grad))
    for row in range(4):
        at = slice(row, row + 1)
        bias_new_ref[at] = biases_ref[at] - shrink(
            bias_update[at], scalar(6 + 2 * row), scalar(7 + 2 * row), full
        )
    lay_kernel_grad(part_ref, kernel_new_ref)
    kernel_grad = kernel_new_ref[...]
    kernel_update = kernel_grad * lax.rsqrt(second_of(kernel_second_ref[...], kernel_grad))
    usq, wsq, entries = 0.0, 0.0, 0.0
    masks = block_masks(kernel_grad.shape)
    for index, (low, high) in enumerate(BLOCKS):
        usq = usq + masks[index] * scalar(14 + 2 * index)
        wsq = wsq + masks[index] * scalar(15 + 2 * index)
        entries = entries + masks[index] * ((high - low) * full)
    kernel_new_ref[...] = kernels_ref[...] - shrink(kernel_update, usq, wsq, entries)


def last_kernel(inputs, outputs, *refs):
    split = inputs + outputs
    step_kernel(*refs[:inputs], *refs[inputs + 5 : split + 5])
    table_ref, patch_ref = refs[0], refs[split + 5]
    grad_ref, gain_ref, stats_ref, patches_ref, back_ref = refs[inputs : inputs + 5]
    final_kernel(grad_ref, gain_ref, stats_ref, table_ref, patches_ref, back_ref, patch_ref)


def optimizer_step(table, gradients, rows, seconds, cols, norm_params, weights, patch, after):
    held = (table,) + gradients + rows + seconds + cols + (norm_params,) + weights
    outs = (norm_params,) + cols + weights[:2] + (norm_params,) + weights[2:]
    patch_out = jax.ShapeDtypeStruct(patch[3].shape, F32)
    total = len(held) + len(patch)
    return call(
        ordered(functools.partial(last_kernel, len(held), len(outs)), 1, total + 1),
        tuple(like(item) for item in outs) + (patch_out,),
        0.2,
        room=LARGE_ROOM,
        in_specs=[WHOLE] * total + [ANYWHERE],
    )(*held, *patch, after)


def like(value):
    return jax.ShapeDtypeStruct(value.shape, value.dtype)


def local(
    patches,
    hole_mask,
    seg_start,
    cotangent,
    qkv_weight,
    out_weight,
    norm_params,
    biases,
    kernels,
    conv_weight,
    qkv_rows,
    qkv_cols,
    out_rows,
    out_cols,
    norm_second,
    bias_second,
    kernel_second,
    conv_second,
):
    patch_count = lax.axis_size("patch")
    head_count = lax.axis_size("head")
    patch_index = lax.axis_index("patch")
    head_index = lax.axis_index("head")
    slide_count, feat_width, tokens_dev = patches.shape
    heads = feat_width // HD
    full_width = feat_width * head_count
    total_tokens = tokens_dev * patch_count
    grid_cols = math.isqrt(total_tokens)
    offset = head_index * feat_width
    halo = 3 * grid_cols

    scalars = jnp.stack(
        [patch_index * tokens_dev, jnp.int32(total_tokens)]
        + [bit_of("patch", bit) for bit in range((patch_count - 1).bit_length())]
    )

    gathered = lax.all_gather(patches, "head")

    out_low = out_weight.astype(BF16)
    out_blocks = [lax.dynamic_slice_in_dim(out_low, offset, feat_width, 1)]
    for hop in range(1, head_count):
        block = lax.dynamic_slice_in_dim(
            out_low, ((head_index + hop) % head_count) * feat_width, feat_width, 1
        )
        out_blocks.append(
            lax.ppermute(block, "head", [(i, (i + hop) % head_count) for i in range(head_count)])
        )
    out_blocks = jnp.stack(out_blocks)
    out_own = jnp.concatenate(
        [
            lax.dynamic_index_in_dim(out_blocks, (head_index - z) % head_count, 0, keepdims=False)
            for z in range(head_count)
        ]
    )

    cot_before, cot_after = neighbours(cotangent, halo)
    taps = full_kernel(kernels).reshape(49, feat_width)
    back_flat, grad_low, bias_part = grid_back(scalars, cot_before, cotangent, cot_after, taps, grid_cols, out_own)
    grad_all = lax.all_gather(grad_low, "head")

    qkv_low = qkv_weight.astype(BF16)
    scalars_row = jnp.zeros((8, 128), F32)
    weight_sums = weight_squares(qkv_weight, out_weight, biases, kernels, conv_weight)

    normed, stats, rows, *mark_sums = norm_project(
        scalars,
        gathered,
        qkv_low,
        norm_params,
        hole_mask,
        seg_start,
        (grad_low, out_own, weight_sums),
    )
    value_before, value_after = neighbours(rows[:, :, 2 * HD :], REACH)
    own_sums = sum_to_owner(scalars, *mark_sums, direct=(value_before, value_after))
    own_counts = own_sums[2 * HD : 2 * HD + 1]
    own_marks = (own_sums[: 2 * HD] / own_counts).astype(BF16)
    residual, residual_done = residual_of(scalars, value_before, rows, value_after, conv_weight)
    marks = from_owner(own_marks, heads, scalars, residual_done)

    kernel_one, *value_parts = token_forward(scalars, rows, marks, hole_mask, residual_done)
    own_kernel, *own_early, own_carried, early_done = inverse_early(own_marks, value_parts[0])
    own_inverse_z, *own_late = inverse_late(own_carried, own_marks)
    own_values = sum_to_owner(scalars, *value_parts, after=early_done)
    own_mixed = mixed_marks_of(own_values, own_inverse_z, residual_done)
    mixed_marks = from_owner(own_mixed, heads, scalars, scalars_row)

    head_low, *mixed_parts = head_gradient(scalars, grad_all, out_low, kernel_one, own_values)
    heads_out = mixed_heads(mixed_marks, kernel_one, residual, mixed_parts[0])
    heads_all = lax.all_gather(heads_out, "head")
    own_grad_mixed = sum_to_owner(scalars, *mixed_parts)
    low_before, low_after = neighbours(head_low, REACH)
    query_grads, key_mark_parts = pull_one(rows, marks, mixed_marks, head_low, heads_out)
    own_pack = grad_values_of(own_values, own_grad_mixed, own_inverse_z, key_mark_parts)
    own_thin, thin_done = thin_chains(own_values, own_grad_mixed, own_kernel, own_early[0], own_late[0])

    pack = from_owner(own_pack, heads, scalars, thin_done)
    key_grads, value_grads, *mark_parts = pull_three(
        scalars, rows, marks, pack, hole_mask, key_mark_parts, scalars_row
    )
    own_grads = sum_to_owner(scalars, *mark_parts)
    own_inverse = landmark_pull(
        own_marks, own_grad_mixed, own_kernel, own_early, own_late, own_thin, mark_parts[0], (low_before, low_after)
    )
    own_mark_grads = finish_marks(own_grads, own_inverse, own_counts, own_counts)
    value_from_conv, conv_lines = back_line(
        scalars, value_before, rows, value_after, low_before, head_low, low_after, conv_weight, own_mark_grads
    )
    mark_grads = from_owner(own_mark_grads, heads, scalars, conv_lines)

    grad_normed, moments, lines, *sums = project_back(
        scalars,
        query_grads,
        key_grads,
        value_grads,
        value_from_conv,
        mark_grads,
        hole_mask,
        seg_start,
        qkv_low,
        gathered,
        normed,
        stats,
        norm_params,
        heads_out,
        grad_all,
    )
    section_one = section(heads_all, out_own, patches, biases)
    sec_before, sec_after = neighbours(section_one, halo)
    own_grad = lax.psum_scatter(grad_normed, "head", scatter_dimension=0, tiled=True)[0]

    block_out, held, grads = None, jnp.zeros((49, 8, feat_width), F32), []
    grid_args = (scalars, sec_before, section_one, sec_after)
    for slide in range(slide_count):
        held = grid_kernel_grad(*grid_args, cotangent, held, grid_cols, slide)
        block_out = grid_mix(*grid_args, taps, biases, grid_cols, slide, block_out)
        grads.append(held)
    kernel_part = pack_sums(held, bias_part, lines, conv_lines, full_width)

    sums, part = sum_rows(scalars, *sums, kernel_part, "patch", (section_one, grads[0]))

    gradients = (sums, part)
    rows_old = (qkv_rows[None, :], out_rows[None, :])
    seconds = (bias_second, kernel_second, conv_second)
    table = optimizer_table(gradients, rows_old, seconds, weight_sums, moments)
    gain_own = lax.dynamic_slice_in_dim(norm_params, offset, feat_width, 1)[0:1]
    weights = (qkv_weight, out_weight, biases, kernels, conv_weight)
    emitted = optimizer_state(gradients, rows_old, seconds, weights, table)
    qkv_grad, out_grad, bias_grad, kernel_grad, conv_grad = emitted[:5]
    qkv_rows_new, out_rows_new, bias_second_new, kernel_second_new, conv_second_new = emitted[5:]
    table = all_sum(table, "head")
    cols = (qkv_cols[None, :], out_cols[None, :], norm_second)
    norm_grad, qkv_cols_new, out_cols_new, norm_second_new, *news = optimizer_step(
        table,
        gradients,
        rows_old,
        seconds,
        cols,
        norm_params,
        weights,
        (own_grad, gain_own, stats, patches, back_flat),
        emitted[9],
    )
    qkv_new, out_new, norm_new, bias_new, kernel_new, conv_new, patch_grad = news
    return (
        block_out,
        patch_grad,
        qkv_grad,
        out_grad,
        norm_grad,
        bias_grad,
        kernel_grad,
        conv_grad,
        qkv_rows_new[0],
        qkv_cols_new[0],
        out_rows_new[0],
        out_cols_new[0],
        norm_second_new,
        bias_second_new,
        kernel_second_new,
        conv_second_new,
        qkv_new,
        out_new,
        norm_new,
        bias_new,
        kernel_new,
        conv_new,
    )


def solution(mesh):
    placed = (
        P(None, "head", "patch"),
        P(None, "patch"),
        P(),
        P(None, "head", "patch"),
        P("head", None),
        P("head", None),
        P(),
        P(None, "head"),
        P(None, "head"),
        P("head", None),
        P("head"),
        P(),
        P("head"),
        P(),
        P(),
        P(None, "head"),
        P(None, "head"),
        P("head", None),
    )
    return jax.shard_map(
        local,
        mesh=mesh,
        in_specs=placed,
        out_specs=(
            P(None, "head", "patch"),
            P(None, "head", "patch"),
            P("head", None),
            P("head", None),
            P(),
            P(None, "head"),
            P(None, "head"),
            P("head", None),
            P("head"),
            P(),
            P("head"),
            P(),
            P(),
            P(None, "head"),
            P(None, "head"),
            P("head", None),
            P("head", None),
            P("head", None),
            P(),
            P(None, "head"),
            P(None, "head"),
            P("head", None),
        ),
        check_vma=False,
    )
```

```python
import functools
import math

import jax
import jax.numpy as jnp
from jax import lax
from jax.experimental import pallas as pl
from jax.experimental.pallas import tpu as pltpu
from jax.sharding import PartitionSpec as P

HEADS = 8
HD = 64
PINV_ITERS = 6
STEP = 10
TAPS = 33
REACH = 16

EPS_NORM = 1e-05
EPS_FACTOR = 1e-30
RATE = 0.5
BLOCKS = ((0, 49), (49, 74), (74, 83))

SMALL = 16
CONV_ROW = 13
NORM_ROW = 14
ROOM = 16
GRID_ROOM = 18
LARGE_ROOM = 56
PULL_ROOM = 56
MARK_ROOM = 56
PULL_MICROS = 2
F32 = jnp.float32
BF16 = jnp.bfloat16


def swap(value, axis, bit):
    return swap_bits(value, axis, 1 << bit)


def swap_bits(value, axis, bits):
    count = lax.axis_size(axis)
    return lax.ppermute(value, axis, [(i, i ^ bits) for i in range(count)])


def bit_of(axis, bit):
    return (lax.axis_index(axis) >> bit) & 1


def keep_half(value, axis, bit):
    mine = bit_of(axis, bit)
    kept = lax.dynamic_index_in_dim(value, mine, 0, keepdims=False)
    sent = lax.dynamic_index_in_dim(value, 1 - mine, 0, keepdims=False)
    return kept + swap(sent, axis, bit)


def join_half(value, axis, bit):
    other = swap(value, axis, bit)
    first = bit_of(axis, bit) == 0
    return jnp.stack([jnp.where(first, value, other), jnp.where(first, other, value)])


def all_sum(value, axis, first_bit=0):
    bits = (lax.axis_size(axis) - 1).bit_length()
    for bit in range(first_bit, bits):
        value = value + swap(value, axis, bit)
    return value


def sum_to_owner(scalars, kept, sent, after=None, direct=()):
    received = swap(sent, "patch", 0)
    count = lax.axis_size("patch")
    if kept.shape[0] != 2:
        return all_sum((kept + received)[0], "patch", 1)
    flat = (2 * kept.shape[1], kept.shape[2])
    kept, sent = fold_halves(
        scalars, kept.reshape(flat), received.reshape(flat), 1, scalars, F32
    )
    if direct and count >= 8:
        near, far = swap_bits(sent, "patch", 2), swap_bits(sent, "patch", 6)
        value = add_four(kept, swap_bits(kept, "patch", 4), near, far, direct)
        return all_sum(value, "patch", 3)
    received = swap(sent, "patch", 1)
    value = kept + received if after is None else add_parts(kept, received, after)
    return all_sum(value, "patch", 2)


def from_owner(value, heads, scalars, after):
    if heads == 2:
        value = join_heads(scalars, value, swap(value, "patch", 1), after)
    else:
        value = value[None]
    return join_half(value, "patch", 0)


def sum_rows(scalars, kept, sent, small, axis, orders):
    bits = (lax.axis_size(axis) - 1).bit_length()
    for bit in range(1, bits):
        received = swap(sent, axis, bit - 1)
        after = orders[bit - 1] if bit <= len(orders) else scalars
        kept, sent = fold_halves(scalars, kept, received, bit, after)
    value = (kept + swap(sent, axis, bits - 1).astype(F32)).astype(BF16)
    for bit in reversed(range(bits)):
        rows = value.shape[0]
        small = lax.reduce_precision(small, 8, 7)
        other = swap(jnp.concatenate([value, small.astype(BF16)], axis=0), axis, bit)
        small = small + other[rows:].astype(F32)
        other = other[:rows]
        first = bit_of(axis, bit) == 0
        value = jnp.concatenate(
            [jnp.where(first, value, other), jnp.where(first, other, value)], axis=0
        )
    return value, small


def neighbours(value, width, kind=BF16):
    count = lax.axis_size("patch")
    odd = bit_of("patch", 0) == 1
    last = value.shape[-1] - width
    axis = value.ndim - 1
    inner = lax.dynamic_slice_in_dim(value, jnp.where(odd, 0, last), width, axis)
    outer = lax.dynamic_slice_in_dim(value, jnp.where(odd, last, 0), width, axis)
    inner, outer = inner.astype(kind), outer.astype(kind)
    inner = swap(inner, "patch", 0)
    steps = [(i, i + 1) for i in range(1, count - 1, 2)]
    outer = lax.ppermute(outer, "patch", steps + [(j, i) for i, j in steps])
    return inner, outer


def in_order(scalars_ref, inner, outer):
    odd = scalars_ref[2] == 1
    return jnp.where(odd, inner, outer), jnp.where(odd, outer, inner)


NN = (((1,), (0,)), ((), ()))
NT = (((1,), (1,)), ((), ()))
TN = (((0,), (0,)), ((), ()))


def dot(left, right, dims=NN):
    return lax.dot_general(left, right, dims, preferred_element_type=F32)


def parts(value):
    high = value.astype(BF16)
    return high, (value - high.astype(F32)).astype(BF16)


def dot3(left, right, dims=NN):
    return dot(left[0], right[0], dims) + (
        dot(left[0], right[1], dims) + dot(left[1], right[0], dims)
    )


def eye(size):
    rows = lax.broadcasted_iota(jnp.int32, (size, size), 0)
    cols = lax.broadcasted_iota(jnp.int32, (size, size), 1)
    return (rows == cols).astype(F32)


HALF = PINV_ITERS // 2


def inverse_turns(product, inverse, turns, q_ref, p_ref):
    identity = eye(product.shape[0])
    for turn in range(turns):
        p_ref[turn] = product
        now = parts(product)
        square = dot3(now, now)
        square_parts = parts(square)
        cube = dot3(square_parts, now)
        fourth = dot3(square_parts, square_parts)
        factor = 0.25 * (13.0 * identity - 15.0 * product + 7.0 * square - cube)
        q_ref[turn] = factor
        inverse = dot3(parts(inverse), parts(factor))
        product = 0.25 * (13.0 * product - 15.0 * square + 7.0 * cube - fourth)
    return product, inverse


def inverse_early_kernel(marks_ref, kernel_ref, q_ref, p_ref, carried_ref, done_ref):
    done_ref[...] = jnp.zeros_like(done_ref)
    marks = marks_ref[...]
    scores = dot(marks[:HD], marks[HD:], TN)
    raised = jnp.exp(scores - jnp.max(scores, axis=-1, keepdims=True))
    kernel = raised * (1.0 / jnp.sum(raised, axis=-1, keepdims=True))
    kernel_ref[...] = kernel
    scale = 1.0 / norm_of(kernel)
    halves = parts(kernel)
    product = dot3(halves, halves, NT) * scale
    carried_ref[0], carried_ref[1] = inverse_turns(product, kernel.T * scale, HALF, q_ref, p_ref)


def inverse_late_kernel(carried_ref, z_ref, q_ref, p_ref):
    turns = PINV_ITERS - HALF
    _, z_ref[...] = inverse_turns(carried_ref[0], carried_ref[1], turns, q_ref, p_ref)


def norm_of(kernel):
    return jnp.sum(jnp.sum(kernel * kernel, axis=0, keepdims=True), axis=1, keepdims=True)


def mixed_marks_kernel(sums_ref, z_ref, out_ref):
    values = sums_ref[:HD] / sums_ref[HD : HD + 1]
    out_ref[...] = dot3(parts(values), parts(z_ref[...]), NT).astype(BF16)


def grad_values_kernel(sums_ref, grads_ref, z_ref, out_ref):
    weight_sum = sums_ref[HD : HD + 1]
    values = sums_ref[:HD] / weight_sum
    left = dot3(parts(grads_ref[...]), parts(z_ref[...]))
    high, low = parts(-jnp.sum(left * values, axis=0, keepdims=True) / weight_sum)
    rows = out_ref.shape[0] - HD
    row = lax.broadcasted_iota(jnp.int32, (rows, out_ref.shape[1]), 0)
    tail = jnp.where(row == 0, high.astype(F32), jnp.where(row == 1, low.astype(F32), 0.0))
    out_ref[:HD] = (left / weight_sum).astype(BF16)
    out_ref[HD:] = tail.astype(BF16)


def total_of(value):
    return jnp.sum(jnp.sum(value, axis=0, keepdims=True), axis=1, keepdims=True)


def even(value):
    return 0.5 * (value + value.T)


def pull_turns(carried, turns, q_ref, p_ref, thin_ref, first):
    for turn in reversed(range(turns)):
        product = parts(p_ref[turn])
        left, right = thin_ref[first + turn], thin_ref[PINV_ITERS + first + turn]
        outer = dot3(parts(left), parts(right), TN)
        held = 0.0
        if carried is not None:
            now = parts(carried)
            outer = outer + dot3(product, now)
            held = dot3(now, parts(q_ref[turn]))
        outer = even(outer)
        once = dot3(product, parts(outer))
        once_parts = parts(once)
        twice = dot3(product, once_parts) + 0.5 * dot3(once_parts, product)
        carried = even(held + 3.5 * once - 0.5 * twice) - 3.75 * outer
    return carried


def chains_kernel(sums_ref, grads_ref, kernel_ref, early_ref, late_ref, thin_ref, done_ref):
    kernel = kernel_ref[...]
    factors = [parts(early_ref[turn]) for turn in range(HALF)]
    factors += [parts(late_ref[turn]) for turn in range(PINV_ITERS - HALF)]
    right = sums_ref[:HD] / sums_ref[HD : HD + 1]
    left = dot3(parts(grads_ref[...]), parts(kernel), NT) * (1.0 / norm_of(kernel))
    for turn in range(PINV_ITERS):
        back = PINV_ITERS - 1 - turn
        thin_ref[turn] = left
        thin_ref[PINV_ITERS + back] = right
        left = dot3(parts(left), factors[turn])
        right = dot3(parts(right), factors[back])
    thin_ref[2 * PINV_ITERS] = right
    done_ref[...] = jnp.zeros_like(done_ref)


def pull_late_kernel(thin_ref, q_ref, p_ref, out_ref):
    out_ref[...] = pull_turns(None, PINV_ITERS - HALF, q_ref, p_ref, thin_ref, HALF)


def pull_early_kernel(carried_ref, marks_ref, grads_ref, kernel_ref, q_ref, p_ref, thin_ref, out_ref):
    marks = marks_ref[...]
    kernel = kernel_ref[...]
    scale = 1.0 / norm_of(kernel)
    halves = parts(kernel)
    grads = grads_ref[...]
    whole = parts(thin_ref[2 * PINV_ITERS])
    carried = pull_turns(carried_ref[...], HALF, q_ref, p_ref, thin_ref, 0)
    mixed = dot3(whole, halves) * scale
    grad_norm = -(total_of(grads * mixed) + total_of(carried * p_ref[0])) * scale
    grad_kernel = (
        dot3(whole, parts(grads), TN) * scale
        + (2.0 * scale) * dot3(parts(carried), halves)
        + 2.0 * grad_norm * kernel
    )
    grad_scores = kernel * (grad_kernel - jnp.sum(kernel * grad_kernel, axis=-1, keepdims=True))
    high, low = parts(grad_scores)
    out_ref[:HD] = dot(marks[HD:], high, NT) + dot(marks[HD:], low, NT)
    out_ref[HD:] = dot(marks[:HD], high) + dot(marks[:HD], low)


def ordered(kernel, count, inputs):
    def body(*refs):
        return kernel(*refs[: inputs - count], *refs[inputs:])

    return body


ANYWHERE = pl.BlockSpec(memory_space=pl.ANY)
WHOLE = pl.BlockSpec(memory_space=pltpu.VMEM)
SCALARS = pl.BlockSpec(memory_space=pltpu.SMEM)
STAY = pl.BlockSpec(memory_space=pltpu.HBM)


def call(kernel, outs, micros, room=ROOM, **grid):
    return pl.pallas_call(
        kernel,
        out_shape=outs,
        compiler_params=pltpu.CompilerParams(vmem_limit_bytes=room * 1024 * 1024),
        **grid,
        cost_estimate=pl.CostEstimate(
            flops=int(micros * 10**9), bytes_accessed=1024, transcendentals=0
        ),
    )


def inverse_early(marks, after):
    size = marks.shape[-1]
    stack = jax.ShapeDtypeStruct((HALF, size, size), F32)
    return call(
        ordered(inverse_early_kernel, 1, 2),
        (
            jax.ShapeDtypeStruct((size, size), F32),
            stack,
            stack,
            jax.ShapeDtypeStruct((2, size, size), F32),
            jax.ShapeDtypeStruct((8, 128), F32),
        ),
        0.1,
        room=MARK_ROOM,
        in_specs=[WHOLE, ANYWHERE],
    )(marks, after)


def inverse_late(carried, after):
    size = carried.shape[-1]
    stack = jax.ShapeDtypeStruct((PINV_ITERS - HALF, size, size), F32)
    return call(
        ordered(inverse_late_kernel, 1, 2),
        (jax.ShapeDtypeStruct((size, size), F32), stack, stack),
        0.1,
        room=MARK_ROOM,
        in_specs=[WHOLE, ANYWHERE],
    )(carried, after)


def mixed_marks_of(sums, inverse, after):
    return call(
        ordered(mixed_marks_kernel, 1, 3),
        jax.ShapeDtypeStruct((HD, sums.shape[1]), BF16),
        0.1,
        in_specs=[WHOLE] * 2 + [ANYWHERE],
    )(sums, inverse, after)


def grad_values_of(sums, grads, inverse, after):
    return call(
        ordered(grad_values_kernel, 1, 4),
        jax.ShapeDtypeStruct((HD + 16, sums.shape[1]), BF16),
        0.1,
        in_specs=[WHOLE] * 3 + [ANYWHERE],
    )(sums, grads, inverse, after)


def thin_chains(sums, grads, kernel, early, late):
    size = kernel.shape[-1]
    return call(
        chains_kernel,
        (
            jax.ShapeDtypeStruct((2 * PINV_ITERS + 1, HD, size), F32),
            jax.ShapeDtypeStruct((8, 128), F32),
        ),
        1,
        room=PULL_ROOM,
    )(sums, grads, kernel, early, late)


def landmark_pull(marks, grads, kernel, early, late, thin, after, later):
    size = kernel.shape[-1]
    carried = call(
        ordered(pull_late_kernel, 1, 4),
        jax.ShapeDtypeStruct((size, size), F32),
        PULL_MICROS,
        room=PULL_ROOM,
        in_specs=[WHOLE] * 3 + [ANYWHERE],
    )(thin, *late, after)
    return call(
        ordered(pull_early_kernel, len(later), 7 + len(later)),
        jax.ShapeDtypeStruct((2 * HD, size), F32),
        PULL_MICROS,
        room=PULL_ROOM,
        in_specs=[WHOLE] * 7 + [ANYWHERE] * len(later),
    )(carried, marks, grads, kernel, *early, thin, *later)


def finish_kernel(sums_ref, inverse_ref, counts_ref, out_ref):
    out_ref[...] = ((sums_ref[...] + inverse_ref[...]) / counts_ref[...]).astype(BF16)


def finish_marks(sums, inverse, counts, after):
    return call(
        ordered(finish_kernel, 1, 4),
        jax.ShapeDtypeStruct(sums.shape, BF16),
        0.5,
        in_specs=[WHOLE] * 3 + [ANYWHERE],
    )(sums, inverse, counts, after)


def fold_kernel(bit, scalars_ref, kept_ref, received_ref, out_kept_ref, out_sent_ref):
    value = kept_ref[...] + received_ref[...].astype(F32)
    half = value.shape[0] // 2
    own_first = scalars_ref[2 + bit] == 0
    first, second = value[:half], value[half:]
    out_kept_ref[...] = jnp.where(own_first, first, second)
    out_sent_ref[...] = jnp.where(own_first, second, first).astype(out_sent_ref.dtype)


def fold_halves(scalars, kept, received, bit, after, kind=BF16):
    shape = (kept.shape[0] // 2, kept.shape[1])
    return call(
        ordered(functools.partial(fold_kernel, bit), 1, 4),
        (jax.ShapeDtypeStruct(shape, F32), jax.ShapeDtypeStruct(shape, kind)),
        0.1,
        in_specs=[SCALARS, WHOLE, WHOLE, ANYWHERE],
    )(scalars, kept, received, after)


def add_kernel(first_ref, second_ref, out_ref):
    out_ref[...] = first_ref[...] + second_ref[...]


def add_four_kernel(kept_ref, beside_ref, near_ref, far_ref, out_ref):
    out_ref[...] = (kept_ref[...] + beside_ref[...]) + (near_ref[...] + far_ref[...])


def add_four(kept, beside, near, far, after):
    return call(
        ordered(add_four_kernel, len(after), 4 + len(after)),
        jax.ShapeDtypeStruct(kept.shape, kept.dtype),
        0.1,
        in_specs=[WHOLE] * 4 + [ANYWHERE] * len(after),
    )(kept, beside, near, far, *after)


def add_parts(first, second, after):
    return call(
        ordered(add_kernel, 1, 3),
        jax.ShapeDtypeStruct(first.shape, first.dtype),
        0.1,
        in_specs=[WHOLE, WHOLE, ANYWHERE],
    )(first, second, after)


def join_kernel(scalars_ref, own_ref, other_ref, out_ref):
    own, other = own_ref[...], other_ref[...]
    own_first = scalars_ref[3] == 0
    out_ref[0] = jnp.where(own_first, own, other)
    out_ref[1] = jnp.where(own_first, other, own)


def join_heads(scalars, own, other, after):
    return call(
        ordered(join_kernel, 1, 4),
        jax.ShapeDtypeStruct((2,) + own.shape, own.dtype),
        0.1,
        in_specs=[SCALARS, WHOLE, WHOLE, ANYWHERE],
    )(scalars, own, other, after)


def row_of(column):
    return jnp.broadcast_to(column, (column.shape[0], 128)).T[:1]


def column_of(row):
    return jnp.broadcast_to(row, (8, row.shape[1])).T[:, :1]


def segments_of(starts, scalars_ref, tokens):
    size = starts.shape[1]
    starts = starts.astype(F32)
    lane = lax.broadcasted_iota(jnp.int32, (1, size), 1)
    last = scalars_ref[1].astype(F32)
    ends = jnp.where(lane == size - 1, last, pltpu.roll(starts, size - 1, 1))
    place = lax.broadcasted_iota(jnp.int32, (1, tokens), 1) + scalars_ref[0]
    place = place.astype(F32)
    member = (place >= column_of(starts)) & (place < column_of(ends))
    return jnp.where(member, 1.0, 0.0).astype(BF16)


def full_kernel(kernels):
    channels = kernels.shape[1]
    large_part = kernels[0:49].reshape(7, 7, channels)
    middle_part = jnp.pad(kernels[49:74].reshape(5, 5, channels), ((1, 1), (1, 1), (0, 0)))
    small_part = jnp.pad(kernels[74:83].reshape(3, 3, channels), ((2, 2), (2, 2), (0, 0)))
    return large_part + middle_part + small_part


def lay_grid(scalars_ref, inner_ref, own_ref, outer_ref, padded_ref, shifted_ref):
    rows, cols, feats = shifted_ref.shape[1:]
    padded_ref[:, 0:8] = jnp.zeros((rows, 8, feats), F32)
    padded_ref[:, 8 + cols :] = jnp.zeros((rows, 8, feats), F32)

    def laid(value):
        return value.astype(F32).T.reshape(-1, cols, feats)

    before, after = in_order(scalars_ref, inner_ref[0], outer_ref[0])
    padded_ref[0:3, 8 : 8 + cols] = laid(before)
    padded_ref[3 : rows - 3, 8 : 8 + cols] = laid(own_ref[0])
    padded_ref[rows - 3 :, 8 : 8 + cols] = laid(after)
    for col in range(7):
        shifted_ref[col] = padded_ref[:, 5 + col : 5 + col + cols]


def back_kernel(scalars_ref, before_ref, own_ref, after_ref, taps_ref, out_ref, low_ref, sums_ref, padded_ref, shifted_ref, flat_ref):
    lay_grid(scalars_ref, before_ref, own_ref, after_ref, padded_ref, shifted_ref)
    rows, cols, feats = shifted_ref.shape[1:]

    def one_row(row, sums):
        centre = shifted_ref[3, row + 3]
        total = centre
        for col in range(7):
            for shift in range(7):
                tap = 48 - (shift * 7 + col)
                total = total + taps_ref[tap : tap + 1] * shifted_ref[col, row + shift]
        flat_ref[row] = total
        return (
            sums[0] + jnp.sum(total, axis=0, keepdims=True),
            sums[1] + jnp.sum(centre, axis=0, keepdims=True),
        )

    zero = jnp.zeros((1, feats), F32)
    sums = lax.fori_loop(0, rows - 6, one_row, (zero, zero))
    sums = jnp.concatenate([sums[0], sums[1], jnp.zeros((6, feats), F32)], axis=0)

    @pl.when(pl.program_id(0) == 0)
    def _():
        sums_ref[...] = sums

    @pl.when(pl.program_id(0) > 0)
    def _():
        sums_ref[...] += sums

    back = flat_ref[...].reshape(-1, feats).T
    out_ref[0] = back
    low_ref[0] = back.astype(BF16)


def kernel_grad_kernel(scalars_ref, inner_ref, own_ref, outer_ref, cot_ref, held_ref, grad_ref, padded_ref, shifted_ref, cot_grid_ref):
    lay_grid(scalars_ref, inner_ref, own_ref, outer_ref, padded_ref, shifted_ref)
    rows, cols, feats = shifted_ref.shape[1:]
    cot_grid_ref[...] = cot_ref[0].astype(F32).T.reshape(-1, cols, feats)
    grad_ref[...] = held_ref[...]

    def one_row(row, carried):
        cot = cot_grid_ref[row]
        for col in range(7):
            for shift in range(7):
                cells = cot * shifted_ref[col, row + shift]
                grad_ref[shift * 7 + col] += jnp.sum(cells.reshape(-1, 8, feats), axis=0)
        return carried

    lax.fori_loop(0, rows - 6, one_row, 0)


def mix_kernel(scalars_ref, inner_ref, own_ref, outer_ref, taps_ref, biases_ref, out_ref, padded_ref, shifted_ref, flat_ref):
    lay_grid(scalars_ref, inner_ref, own_ref, outer_ref, padded_ref, shifted_ref)
    rows, cols, feats = shifted_ref.shape[1:]
    bias = biases_ref[1:2] + biases_ref[2:3] + biases_ref[3:4]

    def one_row(row, carried):
        total = shifted_ref[3, row + 3] + bias
        for col in range(7):
            for shift in range(7):
                tap = shift * 7 + col
                total = total + taps_ref[tap : tap + 1] * shifted_ref[col, row + shift]
        flat_ref[row] = total
        return carried

    lax.fori_loop(0, rows - 6, one_row, 0)
    out_ref[0] = flat_ref[...].reshape(-1, feats).T.astype(BF16)


def grid_scratch(rows, cols, feats):
    return [
        pltpu.VMEM((rows + 6, cols + 16, feats), F32),
        pltpu.VMEM((7, rows + 6, cols, feats), F32),
        pltpu.VMEM((rows, cols, feats), F32),
    ]


def per_slide(shape):
    zeros = (0,) * (len(shape) - 1)
    return pl.BlockSpec((1,) + tuple(shape[1:]), lambda s: (s,) + zeros)


def whole_block(shape):
    zeros = (0,) * len(shape)
    return pl.BlockSpec(tuple(shape), lambda *_: zeros)


def grid_back(scalars, before, own, after, taps, cols, first):
    slides, feats, tokens = own.shape
    rows = tokens // cols
    return call(
        ordered(back_kernel, 1, 6),
        (
            jax.ShapeDtypeStruct(own.shape, F32),
            jax.ShapeDtypeStruct(own.shape, BF16),
            jax.ShapeDtypeStruct((8, feats), F32),
        ),
        8,
        room=GRID_ROOM,
        grid=(slides,),
        in_specs=[
            SCALARS,
            per_slide(before.shape),
            per_slide(own.shape),
            per_slide(after.shape),
            whole_block(taps.shape),
            ANYWHERE,
        ],
        out_specs=(per_slide(own.shape), per_slide(own.shape), whole_block((8, feats))),
        scratch_shapes=grid_scratch(rows, cols, feats),
    )(scalars, before, own, after, taps, first)


def one_slide(slide, shape):
    return pl.BlockSpec((1,) + tuple(shape[1:]), lambda i: (slide, 0, 0))


def grid_kernel_grad(scalars, inner, own, outer, cotangent, held, cols, slide):
    slides, feats, tokens = own.shape
    rows = tokens // cols
    return call(
        kernel_grad_kernel,
        jax.ShapeDtypeStruct(held.shape, F32),
        1,
        room=GRID_ROOM,
        grid=(1,),
        in_specs=[SCALARS]
        + [one_slide(slide, item.shape) for item in (inner, own, outer, cotangent)]
        + [whole_block(held.shape)],
        out_specs=whole_block(held.shape),
        scratch_shapes=grid_scratch(rows, cols, feats),
    )(scalars, inner, own, outer, cotangent, held)


def grid_mix(scalars, inner, own, outer, taps, biases, cols, slide, out=None):
    slides, feats, tokens = own.shape
    rows = tokens // cols
    kernel, extra, specs, aliases = mix_kernel, (), [], {}
    if out is not None:
        kernel, extra, specs, aliases = ordered(mix_kernel, 1, 7), (out,), [ANYWHERE], {6: 0}
    return call(
        kernel,
        jax.ShapeDtypeStruct(own.shape, BF16),
        1,
        room=GRID_ROOM,
        grid=(1,),
        in_specs=[SCALARS]
        + [one_slide(slide, item.shape) for item in (inner, own, outer)]
        + [whole_block(item.shape) for item in (taps, biases)]
        + specs,
        out_specs=one_slide(slide, own.shape),
        scratch_shapes=grid_scratch(rows, cols, feats),
        input_output_aliases=aliases,
    )(scalars, inner, own, outer, taps, biases, *extra)


def pack_kernel(sums_ref, bias_ref, lines_ref, conv_ref, out_ref):
    feats = sums_ref.shape[2]
    share = out_ref.shape[1] // feats
    out_ref[...] = jnp.zeros_like(out_ref)
    totals = jnp.sum(sums_ref[...], axis=1)
    for row in range(51):
        line = totals[row : row + 1] if row < 49 else bias_ref[row - 49 : row - 48]
        at = row % share * feats
        out_ref[row // share : row // share + 1, at : at + feats] = line
    for head in range(conv_ref.shape[0]):
        line = conv_ref[head, :, 0:1]
        line = jnp.concatenate([line, jnp.zeros((64 - line.shape[0], 1), F32)], axis=0)
        out_ref[CONV_ROW : CONV_ROW + 1, head * 64 : head * 64 + 64] = row_of(line)
    out_ref[NORM_ROW : NORM_ROW + 2] = lines_ref[0:2]


def pack_sums(sums, bias_sums, lines, conv, full):
    return call(pack_kernel, jax.ShapeDtypeStruct((SMALL, full), F32), 0.2)(
        sums, bias_sums, lines, conv
    )


def lay_line(before, rows, after, line_ref):
    tokens = rows.shape[1]
    width = line_ref.shape[1]
    line_ref[:, :REACH] = before
    line_ref[:, REACH : REACH + tokens] = rows
    line_ref[:, REACH + tokens : 2 * REACH + tokens] = after
    line_ref[:, 2 * REACH + tokens :] = jnp.zeros((HD, width - tokens - 2 * REACH), BF16)


def line_width(tokens):
    return (-(-tokens // 128) + 1) * 128


def pairs_of(ref):
    return [(s, h) for h in range(ref.shape[1]) for s in range(ref.shape[0])]


def band(line):
    wide = jnp.broadcast_to(line, (128, 256))
    return parts(pltpu.roll(wide, 0, 1, stride=1, stride_axis=0))


def line_conv(line_ref, bands, out_ref, at):
    tokens = out_ref.shape[-1]
    high, low = bands
    for begin in range(0, tokens, 128):
        width = min(128, tokens - begin)
        held = line_ref[:, begin : begin + 256]
        out = dot(held, high, NT) + dot(held, low, NT)
        out_ref[at[0], at[1], :, begin : begin + width] = out[:, :width].astype(out_ref.dtype)


def residual_kernel(scalars_ref, inner_ref, rows_ref, outer_ref, taps_ref, out_ref, done_ref, lines_ref):
    done_ref[...] = jnp.zeros_like(done_ref)
    for index, at in enumerate(pairs_of(rows_ref)):
        line_ref = lines_ref.at[index]
        before, after = in_order(scalars_ref, inner_ref[at], outer_ref[at])
        lay_line(before, rows_ref[at[0], at[1], 2 * HD :], after, line_ref)
        line_conv(line_ref, band(taps_ref[at[1]]), out_ref, at)


def back_line_kernel(
    scalars_ref, value_inner_ref, rows_ref, value_outer_ref, inner_ref, low_ref, outer_ref, taps_ref,
    out_ref, grad_ref, values_ref, lines_ref,
):
    tokens = out_ref.shape[-1]
    gap = lax.broadcasted_iota(jnp.int32, (128, 256), 1) - lax.broadcasted_iota(
        jnp.int32, (128, 256), 0
    )
    cross = jnp.zeros((128, 256), F32)
    for index, at in enumerate(pairs_of(rows_ref)):
        value_ref, line_ref = values_ref.at[index], lines_ref.at[index]
        rows = rows_ref[at[0], at[1], 2 * HD :]
        before, after = in_order(scalars_ref, value_inner_ref[at], value_outer_ref[at])
        lay_line(before, rows, after, value_ref)
        before, after = in_order(scalars_ref, inner_ref[at], outer_ref[at])
        lay_line(before, low_ref[at], after, line_ref)
        line_conv(line_ref, band(taps_ref[at[1]]), out_ref, at)
        for begin in range(0, tokens, 128):
            width = min(128, tokens - begin)
            lane = lax.broadcasted_iota(jnp.int32, (HD, 256), 1)
            inside = (lane >= REACH) & (lane < REACH + width)
            centre = line_ref[:, begin : begin + 256].astype(F32)
            centre = jnp.where(inside, centre, 0.0).astype(BF16)
            held = value_ref[:, begin : begin + 256]
            cross = cross + dot(centre, held, TN)[: 128 + REACH][REACH:]
        if at[0] == rows_ref.shape[0] - 1:
            lines = [
                jnp.sum(jnp.where(gap == tap, cross, 0.0), axis=0, keepdims=True)
                for tap in range(TAPS)
            ]
            lines.append(jnp.zeros((40 - TAPS, 256), F32))
            totals = jnp.sum(jnp.concatenate(lines, axis=0), axis=1, keepdims=True)
            grad_ref[at[1]] = jnp.broadcast_to(totals, (40, 128))
            cross = jnp.zeros((128, 256), F32)


def line_taps(conv_weight):
    return jnp.pad(conv_weight, ((0, 0), (0, 256 - TAPS)))[:, None, :]


def residual_of(scalars, before, rows, after, conv_weight):
    slides, heads, _, tokens = rows.shape
    return call(
        residual_kernel,
        (
            jax.ShapeDtypeStruct((slides, heads, HD, tokens), F32),
            jax.ShapeDtypeStruct((8, 128), F32),
        ),
        0.1,
        in_specs=[SCALARS] + [WHOLE] * 4,
        scratch_shapes=[pltpu.VMEM((slides * heads, HD, line_width(tokens)), BF16)],
    )(scalars, before, rows, after, line_taps(conv_weight))


def back_line(scalars, value_before, rows, value_after, before, low, after, conv_weight, later):
    slides, heads, _, tokens = rows.shape
    lines = pltpu.VMEM((slides * heads, HD, line_width(tokens)), BF16)
    return call(
        ordered(back_line_kernel, 1, 9),
        (
            jax.ShapeDtypeStruct((slides, heads, HD, tokens), BF16),
            jax.ShapeDtypeStruct((heads, 40, 128), F32),
        ),
        1,
        in_specs=[SCALARS] + [WHOLE] * 7 + [ANYWHERE],
        scratch_shapes=[lines, lines],
    )(scalars, value_before, rows, value_after, before, low, after, line_taps(conv_weight[:, ::-1]), later)


def put_halves(kept_ref, sent_ref, mine, sums):
    own_first = mine == 0
    for head, (first, second) in enumerate(zip(*sums)):
        kept_ref[head] = jnp.where(own_first, first, second)
        sent_ref[head] = jnp.where(own_first, second, first)


def all_blocks(shape):
    zeros = (0,) * (len(shape) - 2)
    return pl.BlockSpec((shape[0], 1) + tuple(shape[2:]), lambda s: (0, s) + zeros)


def norm_kernel(scalars_ref, gathered_ref, weight_ref, norm_ref, mask_ref, starts_ref, normed_ref, stats_ref, rows_ref, kept_ref, sent_ref):
    count, _, feats, tokens = gathered_ref.shape
    heads = rows_ref.shape[1]
    full = feats * count
    slide = pl.program_id(0)
    total, squares = 0.0, 0.0
    for slot in range(count):
        cells = gathered_ref[slot, 0].astype(F32)
        total = total + jnp.sum(cells, axis=0, keepdims=True)
        squares = squares + jnp.sum(cells * cells, axis=0, keepdims=True)
    mean = total / full
    inv_std = lax.rsqrt(squares / full - mean * mean + EPS_NORM)
    stats_ref[0] = jnp.concatenate([mean, inv_std, jnp.zeros((6, tokens), F32)], axis=0)
    gain, bias = column_of(norm_ref[0:1]), column_of(norm_ref[1:2])
    for slot in range(count):
        span = slice(slot * feats, (slot + 1) * feats)
        centered = (gathered_ref[slot, 0].astype(F32) - mean) * inv_std
        normed_ref[0, span] = (centered * gain[span] + bias[span]).astype(BF16)
    normed = normed_ref[0]
    mask = mask_ref[slide].astype(F32)
    onehot = segments_of(starts_ref[pl.ds(slide, 1)], scalars_ref, tokens)
    counts = dot(jnp.broadcast_to(mask, (16, tokens)).astype(BF16), onehot, NT)[:8]
    own = scalars_ref[2] == slide
    for head in range(heads):
        row = head * 3 * HD
        projected = dot(weight_ref[row : row + 3 * HD], normed)
        rows_ref[0, head, :HD] = (projected[:HD] * mask * HD ** (-0.5)).astype(BF16)
        rows_ref[0, head, HD:] = (projected[HD:] * mask).astype(BF16)
        sums = dot(rows_ref[0, head, : 2 * HD], onehot, NT)
        sums = jnp.concatenate([sums, counts], axis=0)
        kept_ref[head] = jnp.where(own, sums, kept_ref[head])
        sent_ref[head] = jnp.where(own, sent_ref[head], sums)


def norm_project(scalars, gathered, weight, norm_params, mask, starts, after):
    count, slides, feats, tokens = gathered.shape
    heads = weight.shape[0] // (3 * HD)
    mask = mask[:, None, :]
    half = jax.ShapeDtypeStruct((heads, 2 * HD + 8, starts.shape[1]), F32)
    return call(
        ordered(norm_kernel, len(after), 6 + len(after)),
        (
            jax.ShapeDtypeStruct((slides, count * feats, tokens), BF16),
            jax.ShapeDtypeStruct((slides, 8, tokens), F32),
            jax.ShapeDtypeStruct((slides, heads, 3 * HD, tokens), BF16),
            half,
            half,
        ),
        0.1,
        room=LARGE_ROOM,
        grid=(slides,),
        in_specs=[SCALARS, all_blocks(gathered.shape)]
        + [whole_block(item.shape) for item in (weight, norm_params, mask, starts)]
        + [ANYWHERE] * len(after),
        out_specs=(
            per_slide((slides, count * feats, tokens)),
            per_slide((slides, 8, tokens)),
            per_slide((slides, heads, 3 * HD, tokens)),
            whole_block(half.shape),
            whole_block(half.shape),
        ),
    )(scalars, gathered, weight, norm_params, mask, starts, *after)


def low_kernel(scalars_ref, far_ref, weight_ref, far_kernel_ref, low_ref, kept_ref, sent_ref, near_ref, kernel_ref, sem, kernel_sem):
    count, slides, feats, tokens = far_ref.shape
    heads = low_ref.shape[1]
    rows, kernels = [], []
    for s in range(slides):
        rows.append(
            [
                pltpu.make_async_copy(far_ref.at[slot, s], near_ref.at[slot, s], sem.at[slot, s])
                for slot in range(count)
            ]
        )
        kernels.append(
            pltpu.make_async_copy(far_kernel_ref.at[s], kernel_ref.at[s], kernel_sem.at[s])
        )
    for s in range(slides):
        for copy in rows[s] + [kernels[s]]:
            copy.start()
    sums = [[None] * heads for _ in range(slides)]
    for s in range(slides):
        for copy in rows[s]:
            copy.wait()
        low = dot(weight_ref[...], near_ref[:, s].reshape(count * feats, tokens)).astype(BF16)
        for head in range(heads):
            low_ref[s, head] = low[head * HD : (head + 1) * HD]
        kernels[s].wait()
        for head in range(heads):
            sums[s][head] = dot(low_ref[s, head], kernel_ref[s, head], NT)
    put_halves(kept_ref, sent_ref, scalars_ref[2], sums)


def head_gradient(scalars, gathered, weight, kernel, after):
    count, slides, feats, tokens = gathered.shape
    heads = feats // HD
    half = jax.ShapeDtypeStruct((heads, HD, kernel.shape[2]), F32)
    return call(
        ordered(low_kernel, 1, 5),
        (jax.ShapeDtypeStruct((slides, heads, HD, tokens), BF16), half, half),
        0.1,
        room=LARGE_ROOM,
        in_specs=[SCALARS, STAY, WHOLE, STAY, ANYWHERE],
        scratch_shapes=[
            pltpu.VMEM(gathered.shape, BF16),
            pltpu.VMEM(kernel.shape, BF16),
            pltpu.SemaphoreType.DMA((count, slides)),
            pltpu.SemaphoreType.DMA((slides,)),
        ],
    )(scalars, gathered, weight, kernel, after)


def section_kernel(gathered_ref, weight_ref, patch_ref, biases_ref, out_ref):
    count, slides, feats, tokens = gathered_ref.shape
    bias = column_of(biases_ref[0:1])
    for s in range(slides):
        branch = dot(weight_ref[...], gathered_ref[:, s].reshape(count * feats, tokens), TN)
        out_ref[s] = patch_ref[s].astype(F32) + branch + bias


def section(gathered, weight, patches, biases):
    return call(section_kernel, jax.ShapeDtypeStruct(patches.shape, F32), 1)(
        gathered, weight, patches, biases
    )


def final_kernel(grad_ref, gain_ref, stats_ref, table_ref, patch_ref, back_ref, out_ref):
    slides, feats, tokens = out_ref.shape
    full = table_ref.shape[1]
    gain = column_of(gain_ref[...])
    lines = {}
    for s, which, row, begin, end in line_pieces(slides, tokens, full):
        lines.setdefault((s, which), []).append(table_ref[row : row + 1, : end - begin])
    for s in range(slides):
        mean, inv_std = stats_ref[s, 0:1], stats_ref[s, 1:2]
        first, second = (jnp.concatenate(lines[s, which], axis=1) / full for which in range(2))
        centered = (patch_ref[s].astype(F32) - mean) * inv_std
        grad = grad_ref[s].astype(F32) * gain - first - centered * second
        out_ref[s] = inv_std * grad + back_ref[s]


def token_probs(marks, queries):
    scores = dot(marks[HD:], queries, TN)
    raised = jnp.exp(scores - jnp.max(scores, axis=0, keepdims=True))
    return raised * (1.0 / jnp.sum(raised, axis=0, keepdims=True))


def token_weights(marks, keys, mask):
    return jnp.exp(dot(marks[:HD], keys, TN)) * mask


def framed(values):
    return jnp.concatenate([values, jnp.ones((16, values.shape[1]), BF16)], axis=0)


def forward_kernel(scalars_ref, rows_ref, marks_ref, mask_ref, kernel_ref, kept_ref, sent_ref):
    sums = [[None] * rows_ref.shape[1] for _ in range(rows_ref.shape[0])]
    for at in pairs_of(rows_ref):
        rows, marks = rows_ref[at], marks_ref[at]
        weights = token_weights(marks, rows[HD : 2 * HD], mask_ref[at[0] : at[0] + 1].astype(F32)).astype(BF16)
        sums[at[0]][at[1]] = dot(framed(rows[2 * HD :]), weights, NT)[: HD + 8]
        kernel_ref[at] = token_probs(marks, rows[:HD]).astype(BF16)
    put_halves(kept_ref, sent_ref, scalars_ref[2], sums)


def mixed_kernel(pack_ref, kernel_ref, residual_ref, out_ref):
    for s, h in pairs_of(pack_ref):
        attended = dot(pack_ref[s, h], kernel_ref[s, h])
        out_ref[s, h * HD : (h + 1) * HD] = (attended + residual_ref[s, h]).astype(BF16)


def pull_one_kernel(rows_ref, marks_ref, pack_ref, low_ref, grads_ref, sums_ref):
    for at in pairs_of(rows_ref):
        queries, marks = rows_ref[at[0], at[1], :HD], marks_ref[at]
        probs = token_probs(marks, queries)
        pulled = probs * dot(pack_ref[at], low_ref[at], TN)
        grad_scores = (pulled - probs * jnp.sum(pulled, axis=0, keepdims=True)).astype(BF16)
        grads_ref[at] = dot(marks[HD:], grad_scores).astype(BF16)
        sums_ref[at] = dot(queries, grad_scores, NT)


def pull_three_kernel(scalars_ref, rows_ref, marks_ref, pack_ref, mask_ref, other_ref, grads_ref, value_ref, kept_ref, sent_ref):
    sums = [[None] * rows_ref.shape[1] for _ in range(rows_ref.shape[0])]
    for at in pairs_of(rows_ref):
        rows, marks, pack = rows_ref[at], marks_ref[at], pack_ref[at]
        keys = rows[HD : 2 * HD]
        raised = token_weights(marks, keys, mask_ref[at[0] : at[0] + 1].astype(F32))
        grad_three = (dot(pack, framed(rows[2 * HD :]), TN) * raised).astype(BF16)
        own = dot(keys, grad_three, NT)
        sums[at[0]][at[1]] = jnp.concatenate([own, other_ref[at]], axis=0)
        grads_ref[at] = dot(marks[:HD], grad_three).astype(BF16)
        value_ref[at] = dot(pack[:HD], raised.astype(BF16)).astype(BF16)
    put_halves(kept_ref, sent_ref, scalars_ref[2], sums)


def token_forward(scalars, rows, marks, mask, after):
    slides, heads, _, tokens = rows.shape
    size = marks.shape[-1]
    half = jax.ShapeDtypeStruct((heads, HD + 8, size), F32)
    return call(
        ordered(forward_kernel, 1, 5),
        (jax.ShapeDtypeStruct((slides, heads, size, tokens), BF16), half, half),
        0.1,
        in_specs=[SCALARS] + [WHOLE] * 3 + [ANYWHERE],
    )(scalars, rows, marks, mask, after)


def mixed_heads(pack, kernel, residual, after):
    slides, heads, size, tokens = kernel.shape
    return call(
        ordered(mixed_kernel, 1, 4),
        jax.ShapeDtypeStruct((slides, heads * HD, tokens), BF16),
        0.1,
        in_specs=[WHOLE] * 3 + [ANYWHERE],
    )(pack, kernel, residual, after)


def pull_one(rows, marks, pack, low, after):
    slides, heads, _, tokens = rows.shape
    return call(
        ordered(pull_one_kernel, 1, 5),
        (
            jax.ShapeDtypeStruct((slides, heads, HD, tokens), BF16),
            jax.ShapeDtypeStruct((slides, heads, HD, marks.shape[-1]), F32),
        ),
        1,
        in_specs=[WHOLE] * 4 + [ANYWHERE],
    )(rows, marks, pack, low, after)


def pull_three(scalars, rows, marks, pack, mask, other, after):
    slides, heads, _, tokens = rows.shape
    half = jax.ShapeDtypeStruct((heads, 2 * HD, marks.shape[-1]), F32)
    token = jax.ShapeDtypeStruct((slides, heads, HD, tokens), BF16)
    return call(
        ordered(pull_three_kernel, 1, 7),
        (token, token, half, half),
        1,
        in_specs=[SCALARS] + [WHOLE] * 5 + [STAY],
    )(scalars, rows, marks, pack, mask, other, after)


def project_kernel(scalars_ref, query_ref, key_ref, value_ref, line_ref, marks_ref, mask_ref, starts_ref, weight_ref, gathered_ref, normed_ref, stats_ref, norm_ref, out_rows_ref, low_ref, near_ref, moments_ref, lines_ref, kept_ref, sent_ref, rows_ref, sums_ref):
    count, slides, feats, tokens = gathered_ref.shape
    heads = query_ref.shape[1]
    gains = column_of(norm_ref[0:1])
    norms = [[0.0, 0.0] for _ in range(count)]
    for s in range(slides):
        mask = mask_ref[s : s + 1].astype(F32)
        onehot = segments_of(starts_ref[s : s + 1], scalars_ref, tokens)
        for head in range(heads):
            row = head * 3 * HD
            spread = dot(marks_ref[s, head], onehot)
            query = (query_ref[s, head].astype(F32) + spread[:HD]).astype(BF16).astype(F32) * mask
            key = (key_ref[s, head].astype(F32) + spread[HD:]).astype(BF16).astype(F32) * mask
            value = (value_ref[s, head].astype(F32) + line_ref[s, head].astype(F32)).astype(BF16)
            rows_ref[s, row : row + HD] = (query * HD ** (-0.5)).astype(BF16)
            rows_ref[s, row + HD : row + 2 * HD] = key.astype(BF16)
            rows_ref[s, row + 2 * HD : row + 3 * HD] = (value.astype(F32) * mask).astype(BF16)
        rows = rows_ref[s]
        mean, inv_std = stats_ref[s, 0:1], stats_ref[s, 1:2]
        first, second = 0.0, 0.0
        for slot in range(count):
            span = slice(slot * feats, (slot + 1) * feats)
            grad = dot(weight_ref[:, span], rows, TN)
            near_ref[slot, s] = grad.astype(BF16)
            centered = (gathered_ref[slot, s].astype(F32) - mean) * inv_std
            pulled = grad * centered
            gain = gains[span]
            first = first + jnp.sum(grad * gain, axis=0, keepdims=True)
            second = second + jnp.sum(pulled * gain, axis=0, keepdims=True)
            norms[slot][0] += jnp.sum(pulled, axis=1, keepdims=True)
            norms[slot][1] += jnp.sum(grad, axis=1, keepdims=True)
        moments_ref[s] = jnp.concatenate([first, second], axis=0)
    qkv_grad = 0.0
    out_grads = [0.0] * count
    for s in range(slides):
        qkv_grad = qkv_grad + dot(rows_ref[s], normed_ref[s], NT)
        for slot in range(count):
            out_grads[slot] += dot(out_rows_ref[s], low_ref[slot, s], NT)
    lines_ref[...] = jnp.zeros_like(lines_ref)
    sums_ref[: 3 * feats] = qkv_grad
    for slot in range(count):
        span = slice(slot * feats, (slot + 1) * feats)
        sums_ref[3 * feats : 4 * feats, span] = out_grads[slot]
        for line in range(2):
            lines_ref[line : line + 1, span] = row_of(norms[slot][line])
    half = sums_ref.shape[0] // 2
    own_first = scalars_ref[2] == 0
    first, second = sums_ref[:half], sums_ref[half:]
    kept_ref[...] = jnp.where(own_first, first, second)
    sent_ref[...] = jnp.where(own_first, second, first).astype(BF16)


def project_back(scalars, query, key, value, line, marks, mask, starts, weight, gathered, normed, stats, norm_params, heads_out, low):
    count, slides, feats, tokens = gathered.shape
    held = (query, key, value, line, marks, mask, starts, weight, gathered, normed, stats, norm_params, heads_out, low)
    return call(
        project_kernel,
        (
            jax.ShapeDtypeStruct((count, slides, feats, tokens), BF16),
            jax.ShapeDtypeStruct((slides, 2, tokens), F32),
            jax.ShapeDtypeStruct((8, count * feats), F32),
            jax.ShapeDtypeStruct((2 * feats, count * feats), F32),
            jax.ShapeDtypeStruct((2 * feats, count * feats), BF16),
        ),
        7,
        in_specs=[SCALARS] + [WHOLE] * len(held),
        scratch_shapes=[
            pltpu.VMEM((slides, weight.shape[0], tokens), BF16),
            pltpu.VMEM((4 * feats, count * feats), F32),
        ],
    )(scalars, *held)


DECAY = 1.0 - STEP ** (-0.8)


def second_of(old, grad):
    return DECAY * old + (1.0 - DECAY) * (grad * grad + EPS_FACTOR)


def shrink(update, usq_sum, weight_sq, entries):
    clip_factor = jnp.maximum(1.0, jnp.sqrt(usq_sum / entries))
    return RATE * jnp.sqrt(weight_sq / entries) * update / clip_factor


def scalar_line(values):
    lane = lax.broadcasted_iota(jnp.int32, (1, 128), 1)
    line = jnp.zeros((1, 128), F32)
    for index, value in values:
        line = jnp.where(lane == index, value, line)
    return line


def block_masks(shape):
    row = lax.broadcasted_iota(jnp.int32, shape, 0)
    return [jnp.where((row >= low) & (row < high), 1.0, 0.0) for low, high in BLOCKS]


def squares_kernel(qkv_ref, out_ref, biases_ref, kernels_ref, conv_ref, line_ref):
    def square(ref):
        value = ref[...]
        return value * value

    biases = square(biases_ref)
    kernels = square(kernels_ref)
    values = [(1, total_of(square(qkv_ref))), (3, total_of(square(out_ref)))]
    values.append((5, total_of(square(conv_ref))))
    values += [(7 + 2 * row, total_of(biases[row : row + 1])) for row in range(4)]
    masks = block_masks(kernels.shape)
    values += [(15 + 2 * block, total_of(kernels * mask)) for block, mask in enumerate(masks)]
    line_ref[...] = jnp.broadcast_to(scalar_line(values), line_ref.shape)


def weight_squares(*weights):
    return call(squares_kernel, jax.ShapeDtypeStruct((8, 128), F32), 2, room=LARGE_ROOM)(*weights)


def weight_grad(sums_ref, feats, index):
    return sums_ref[3 * feats * index : 3 * feats + feats * index].astype(F32)


def conv_grad_of(part_ref, heads):
    row = part_ref[CONV_ROW : CONV_ROW + 1]
    return jnp.concatenate([row[:, 64 * head : 64 * head + TAPS] for head in range(heads)], axis=0)


def part_row(part_ref, feats, row):
    share = part_ref.shape[1] // feats
    at = row % share * feats
    return part_ref[row // share : row // share + 1, at : at + feats]


def lay_bias_grad(part_ref, out_ref):
    feats = out_ref.shape[1]
    for row in range(4):
        out_ref[row : row + 1] = part_row(part_ref, feats, 49 + min(row, 1))


def lay_kernel_grad(part_ref, out_ref):
    feats = out_ref.shape[1]
    taps = list(range(49))
    taps += [7 * row + col for row in range(1, 6) for col in range(1, 6)]
    taps += [7 * row + col for row in range(2, 5) for col in range(2, 5)]
    for row, tap in enumerate(taps):
        out_ref[row : row + 1] = part_row(part_ref, feats, tap)


def rows_new_of(grad, rows):
    mean = jnp.sum(grad * grad, axis=1, keepdims=True) / grad.shape[1]
    return DECAY * column_of(rows) + (1.0 - DECAY) * (mean + EPS_FACTOR)


def line_pieces(slides, tokens, full):
    share = -(-tokens // full)
    return [
        (s, which, 8 + (2 * s + which) * share + piece, piece * full, min(tokens, (piece + 1) * full))
        for s in range(slides)
        for which in range(2)
        for piece in range(share)
    ]


def table_kernel(sums_ref, part_ref, qkv_rows_ref, out_rows_ref, bias_second_ref, kernel_second_ref, conv_second_ref, line_ref, moments_ref, table_ref, bias_ref, kernel_ref):
    feats = bias_second_ref.shape[1]
    heads = conv_second_ref.shape[0]
    values = []
    table_ref[...] = jnp.zeros_like(table_ref)
    for index, rows_ref in enumerate((qkv_rows_ref, out_rows_ref)):
        grad = weight_grad(sums_ref, feats, index)
        squares = grad * grad
        rows_new = rows_new_of(grad, rows_ref[...])
        table_ref[2 * index : 2 * index + 1] = jnp.sum(squares, axis=0, keepdims=True)
        table_ref[2 * index + 1 : 2 * index + 2] = jnp.sum(
            squares * (1.0 / rows_new), axis=0, keepdims=True
        )
        values.append((2 * index, total_of(rows_new)))
    table_ref[4:6] = part_ref[NORM_ROW : NORM_ROW + 2]

    def update_squares(grad, second):
        return grad * grad / second_of(second, grad)

    conv_grad = conv_grad_of(part_ref, heads)
    values.append((4, total_of(update_squares(conv_grad, conv_second_ref[...]))))
    lay_bias_grad(part_ref, bias_ref)
    bias_squares = update_squares(bias_ref[...], bias_second_ref[...])
    values += [(6 + 2 * row, total_of(bias_squares[row : row + 1])) for row in range(4)]
    lay_kernel_grad(part_ref, kernel_ref)
    kernel_squares = update_squares(kernel_ref[...], kernel_second_ref[...])
    masks = block_masks(kernel_squares.shape)
    values += [
        (14 + 2 * block, total_of(kernel_squares * mask)) for block, mask in enumerate(masks)
    ]
    table_ref[6:7, :128] = scalar_line(values) + line_ref[0:1]
    slides, _, tokens = moments_ref.shape
    for s, which, row, begin, end in line_pieces(slides, tokens, table_ref.shape[1]):
        table_ref[row : row + 1, : end - begin] = moments_ref[s, which : which + 1, begin:end]


def optimizer_table(gradients, rows, seconds, line, moments):
    full = gradients[0].shape[1]
    lines = len(line_pieces(moments.shape[0], moments.shape[2], full))
    return call(
        table_kernel,
        jax.ShapeDtypeStruct((8 + -(-lines // 8) * 8, full), F32),
        0.2,
        scratch_shapes=[pltpu.VMEM(seconds[0].shape, F32), pltpu.VMEM(seconds[1].shape, F32)],
    )(*gradients, *rows, *seconds, line, moments)


def state_kernel(sums_ref, part_ref, qkv_rows_ref, out_rows_ref, bias_second_ref, kernel_second_ref, conv_second_ref, qkv_grad_ref, out_grad_ref, bias_grad_ref, kernel_grad_ref, conv_grad_ref, qkv_rows_new_ref, out_rows_new_ref, bias_new_ref, kernel_new_ref, conv_new_ref):
    feats = bias_second_ref.shape[1]
    heads = conv_second_ref.shape[0]
    for index, (rows_ref, grad_ref, rows_new_ref) in enumerate(
        (
            (qkv_rows_ref, qkv_grad_ref, qkv_rows_new_ref),
            (out_rows_ref, out_grad_ref, out_rows_new_ref),
        )
    ):
        grad = weight_grad(sums_ref, feats, index)
        grad_ref[...] = grad
        rows_new_ref[...] = row_of(rows_new_of(grad, rows_ref[...]))
    conv_grad_ref[...] = conv_grad_of(part_ref, heads)
    lay_bias_grad(part_ref, bias_grad_ref)
    lay_kernel_grad(part_ref, kernel_grad_ref)
    conv_new_ref[...] = second_of(conv_second_ref[...], conv_grad_ref[...])
    bias_new_ref[...] = second_of(bias_second_ref[...], bias_grad_ref[...])
    kernel_new_ref[...] = second_of(kernel_second_ref[...], kernel_grad_ref[...])


def optimizer_state(gradients, rows, seconds, weights, after):
    return call(
        ordered(state_kernel, 1, 8),
        tuple(like(item) for item in weights + rows + seconds),
        0.2,
        room=LARGE_ROOM,
        in_specs=[WHOLE] * 7 + [ANYWHERE],
    )(*gradients, *rows, *seconds, after)


def step_kernel(
    table_ref,
    sums_ref,
    part_ref,
    qkv_rows_ref,
    out_rows_ref,
    bias_second_ref,
    kernel_second_ref,
    conv_second_ref,
    qkv_cols_ref,
    out_cols_ref,
    norm_second_ref,
    norm_ref,
    qkv_weight_ref,
    out_weight_ref,
    biases_ref,
    kernels_ref,
    conv_weight_ref,
    norm_grad_ref,
    qkv_cols_new_ref,
    out_cols_new_ref,
    norm_second_new_ref,
    qkv_new_ref,
    out_new_ref,
    norm_new_ref,
    bias_new_ref,
    kernel_new_ref,
    conv_new_ref,
):
    feats, full = out_weight_ref.shape
    heads = conv_weight_ref.shape[0]

    def scalar(index):
        return table_ref[6:7, index : index + 1]

    for index, (rows, cols_ref, cols_new_ref, rows_ref, weight_ref, new_ref) in enumerate(
        (
            (3 * full, qkv_cols_ref, qkv_cols_new_ref, qkv_rows_ref, qkv_weight_ref, qkv_new_ref),
            (full, out_cols_ref, out_cols_new_ref, out_rows_ref, out_weight_ref, out_new_ref),
        )
    ):
        mean = scalar(2 * index) / rows
        cols = DECAY * cols_ref[...] + (1.0 - DECAY) * (
            table_ref[2 * index : 2 * index + 1] / rows + EPS_FACTOR
        )
        cols_new_ref[...] = cols
        usq = mean * total_of(table_ref[2 * index + 1 : 2 * index + 2] / cols)
        grad = weight_grad(sums_ref, feats, index)
        update = grad * lax.rsqrt(rows_new_of(grad, rows_ref[...]) * cols / mean)
        new_ref[...] = weight_ref[...] - shrink(update, usq, scalar(2 * index + 1), rows * full)

    norm_grad = table_ref[4:6]
    norm_grad_ref[...] = norm_grad
    norm_second = second_of(norm_second_ref[...], norm_grad)
    norm_second_new_ref[...] = norm_second
    update = norm_grad * lax.rsqrt(norm_second)
    norm = norm_ref[...]
    norm_new_ref[...] = norm - shrink(
        update,
        jnp.sum(update * update, axis=1, keepdims=True),
        jnp.sum(norm * norm, axis=1, keepdims=True),
        full,
    )

    conv_grad = conv_grad_of(part_ref, heads)
    conv_update = conv_grad * lax.rsqrt(second_of(conv_second_ref[...], conv_grad))
    conv_new_ref[...] = conv_weight_ref[...] - shrink(
        conv_update, scalar(4), scalar(5), HEADS * TAPS
    )
    lay_bias_grad(part_ref, bias_new_ref)
    bias_grad = bias_new_ref[...]
    bias_update = bias_grad * lax.rsqrt(second_of(bias_second_ref[...], bias_grad))
    for row in range(4):
        at = slice(row, row + 1)
        bias_new_ref[at] = biases_ref[at] - shrink(
            bias_update[at], scalar(6 + 2 * row), scalar(7 + 2 * row), full
        )
    lay_kernel_grad(part_ref, kernel_new_ref)
    kernel_grad = kernel_new_ref[...]
    kernel_update = kernel_grad * lax.rsqrt(second_of(kernel_second_ref[...], kernel_grad))
    usq, wsq, entries = 0.0, 0.0, 0.0
    masks = block_masks(kernel_grad.shape)
    for index, (low, high) in enumerate(BLOCKS):
        usq = usq + masks[index] * scalar(14 + 2 * index)
        wsq = wsq + masks[index] * scalar(15 + 2 * index)
        entries = entries + masks[index] * ((high - low) * full)
    kernel_new_ref[...] = kernels_ref[...] - shrink(kernel_update, usq, wsq, entries)


def last_kernel(inputs, outputs, *refs):
    split = inputs + outputs
    step_kernel(*refs[:inputs], *refs[inputs + 5 : split + 5])
    table_ref, patch_ref = refs[0], refs[split + 5]
    grad_ref, gain_ref, stats_ref, patches_ref, back_ref = refs[inputs : inputs + 5]
    final_kernel(grad_ref, gain_ref, stats_ref, table_ref, patches_ref, back_ref, patch_ref)


def optimizer_step(table, gradients, rows, seconds, cols, norm_params, weights, patch, after):
    held = (table,) + gradients + rows + seconds + cols + (norm_params,) + weights
    outs = (norm_params,) + cols + weights[:2] + (norm_params,) + weights[2:]
    patch_out = jax.ShapeDtypeStruct(patch[3].shape, F32)
    total = len(held) + len(patch)
    return call(
        ordered(functools.partial(last_kernel, len(held), len(outs)), 1, total + 1),
        tuple(like(item) for item in outs) + (patch_out,),
        0.2,
        room=LARGE_ROOM,
        in_specs=[WHOLE] * total + [ANYWHERE],
    )(*held, *patch, after)


def like(value):
    return jax.ShapeDtypeStruct(value.shape, value.dtype)


def local(
    patches,
    hole_mask,
    seg_start,
    cotangent,
    qkv_weight,
    out_weight,
    norm_params,
    biases,
    kernels,
    conv_weight,
    qkv_rows,
    qkv_cols,
    out_rows,
    out_cols,
    norm_second,
    bias_second,
    kernel_second,
    conv_second,
):
    patch_count = lax.axis_size("patch")
    head_count = lax.axis_size("head")
    patch_index = lax.axis_index("patch")
    head_index = lax.axis_index("head")
    slide_count, feat_width, tokens_dev = patches.shape
    heads = feat_width // HD
    full_width = feat_width * head_count
    total_tokens = tokens_dev * patch_count
    grid_cols = math.isqrt(total_tokens)
    offset = head_index * feat_width
    halo = 3 * grid_cols

    scalars = jnp.stack(
        [patch_index * tokens_dev, jnp.int32(total_tokens)]
        + [bit_of("patch", bit) for bit in range((patch_count - 1).bit_length())]
    )

    gathered = lax.all_gather(patches, "head")

    out_low = out_weight.astype(BF16)
    out_blocks = [lax.dynamic_slice_in_dim(out_low, offset, feat_width, 1)]
    for hop in range(1, head_count):
        block = lax.dynamic_slice_in_dim(
            out_low, ((head_index + hop) % head_count) * feat_width, feat_width, 1
        )
        out_blocks.append(
            lax.ppermute(block, "head", [(i, (i + hop) % head_count) for i in range(head_count)])
        )
    out_blocks = jnp.stack(out_blocks)
    out_own = jnp.concatenate(
        [
            lax.dynamic_index_in_dim(out_blocks, (head_index - z) % head_count, 0, keepdims=False)
            for z in range(head_count)
        ]
    )

    cot_before, cot_after = neighbours(cotangent, halo)
    taps = full_kernel(kernels).reshape(49, feat_width)
    back_flat, grad_low, bias_part = grid_back(scalars, cot_before, cotangent, cot_after, taps, grid_cols, out_own)
    grad_all = lax.all_gather(grad_low, "head")

    qkv_low = qkv_weight.astype(BF16)
    scalars_row = jnp.zeros((8, 128), F32)
    weight_sums = weight_squares(qkv_weight, out_weight, biases, kernels, conv_weight)

    normed, stats, rows, *mark_sums = norm_project(
        scalars,
        gathered,
        qkv_low,
        norm_params,
        hole_mask,
        seg_start,
        (grad_low, out_own, weight_sums),
    )
    value_before, value_after = neighbours(rows[:, :, 2 * HD :], REACH)
    own_sums = sum_to_owner(scalars, *mark_sums, direct=(value_before, value_after))
    own_counts = own_sums[2 * HD : 2 * HD + 1]
    own_marks = (own_sums[: 2 * HD] / own_counts).astype(BF16)
    residual, residual_done = residual_of(scalars, value_before, rows, value_after, conv_weight)
    marks = from_owner(own_marks, heads, scalars, residual_done)

    kernel_one, *value_parts = token_forward(scalars, rows, marks, hole_mask, residual_done)
    own_kernel, *own_early, own_carried, early_done = inverse_early(own_marks, value_parts[0])
    own_inverse_z, *own_late = inverse_late(own_carried, own_marks)
    own_values = sum_to_owner(scalars, *value_parts, after=early_done)
    own_mixed = mixed_marks_of(own_values, own_inverse_z, residual_done)
    mixed_marks = from_owner(own_mixed, heads, scalars, scalars_row)

    head_low, *mixed_parts = head_gradient(scalars, grad_all, out_low, kernel_one, own_values)
    heads_out = mixed_heads(mixed_marks, kernel_one, residual, mixed_parts[0])
    heads_all = lax.all_gather(heads_out, "head")
    own_grad_mixed = sum_to_owner(scalars, *mixed_parts)
    low_before, low_after = neighbours(head_low, REACH)
    query_grads, key_mark_parts = pull_one(rows, marks, mixed_marks, head_low, heads_out)
    own_pack = grad_values_of(own_values, own_grad_mixed, own_inverse_z, key_mark_parts)
    own_thin, thin_done = thin_chains(own_values, own_grad_mixed, own_kernel, own_early[0], own_late[0])

    pack = from_owner(own_pack, heads, scalars, thin_done)
    key_grads, value_grads, *mark_parts = pull_three(
        scalars, rows, marks, pack, hole_mask, key_mark_parts, scalars_row
    )
    own_grads = sum_to_owner(scalars, *mark_parts)
    own_inverse = landmark_pull(
        own_marks, own_grad_mixed, own_kernel, own_early, own_late, own_thin, mark_parts[0], (low_before, low_after)
    )
    own_mark_grads = finish_marks(own_grads, own_inverse, own_counts, own_counts)
    value_from_conv, conv_lines = back_line(
        scalars, value_before, rows, value_after, low_before, head_low, low_after, conv_weight, own_mark_grads
    )
    mark_grads = from_owner(own_mark_grads, heads, scalars, conv_lines)

    grad_normed, moments, lines, *sums = project_back(
        scalars,
        query_grads,
        key_grads,
        value_grads,
        value_from_conv,
        mark_grads,
        hole_mask,
        seg_start,
        qkv_low,
        gathered,
        normed,
        stats,
        norm_params,
        heads_out,
        grad_all,
    )
    section_one = section(heads_all, out_own, patches, biases)
    sec_before, sec_after = neighbours(section_one, halo)
    own_grad = lax.psum_scatter(grad_normed, "head", scatter_dimension=0, tiled=True)[0]

    block_out, held, grads = None, jnp.zeros((49, 8, feat_width), F32), []
    grid_args = (scalars, sec_before, section_one, sec_after)
    for slide in range(slide_count):
        held = grid_kernel_grad(*grid_args, cotangent, held, grid_cols, slide)
        block_out = grid_mix(*grid_args, taps, biases, grid_cols, slide, block_out)
        grads.append(held)
    kernel_part = pack_sums(held, bias_part, lines, conv_lines, full_width)

    sums, part = sum_rows(scalars, *sums, kernel_part, "patch", (section_one, grads[0]))

    gradients = (sums, part)
    rows_old = (qkv_rows[None, :], out_rows[None, :])
    seconds = (bias_second, kernel_second, conv_second)
    table = optimizer_table(gradients, rows_old, seconds, weight_sums, moments)
    gain_own = lax.dynamic_slice_in_dim(norm_params, offset, feat_width, 1)[0:1]
    weights = (qkv_weight, out_weight, biases, kernels, conv_weight)
    emitted = optimizer_state(gradients, rows_old, seconds, weights, table)
    qkv_grad, out_grad, bias_grad, kernel_grad, conv_grad = emitted[:5]
    qkv_rows_new, out_rows_new, bias_second_new, kernel_second_new, conv_second_new = emitted[5:]
    table = all_sum(table, "head")
    cols = (qkv_cols[None, :], out_cols[None, :], norm_second)
    norm_grad, qkv_cols_new, out_cols_new, norm_second_new, *news = optimizer_step(
        table,
        gradients,
        rows_old,
        seconds,
        cols,
        norm_params,
        weights,
        (own_grad, gain_own, stats, patches, back_flat),
        emitted[9],
    )
    qkv_new, out_new, norm_new, bias_new, kernel_new, conv_new, patch_grad = news
    return (
        block_out,
        patch_grad,
        qkv_grad,
        out_grad,
        norm_grad,
        bias_grad,
        kernel_grad,
        conv_grad,
        qkv_rows_new[0],
        qkv_cols_new[0],
        out_rows_new[0],
        out_cols_new[0],
        norm_second_new,
        bias_second_new,
        kernel_second_new,
        conv_second_new,
        qkv_new,
        out_new,
        norm_new,
        bias_new,
        kernel_new,
        conv_new,
    )


def solution(mesh):
    placed = (
        P(None, "head", "patch"),
        P(None, "patch"),
        P(),
        P(None, "head", "patch"),
        P("head", None),
        P("head", None),
        P(),
        P(None, "head"),
        P(None, "head"),
        P("head", None),
        P("head"),
        P(),
        P("head"),
        P(),
        P(),
        P(None, "head"),
        P(None, "head"),
        P("head", None),
    )
    return jax.shard_map(
        local,
        mesh=mesh,
        in_specs=placed,
        out_specs=(
            P(None, "head", "patch"),
            P(None, "head", "patch"),
            P("head", None),
            P("head", None),
            P(),
            P(None, "head"),
            P(None, "head"),
            P("head", None),
            P("head"),
            P(),
            P("head"),
            P(),
            P(),
            P(None, "head"),
            P(None, "head"),
            P("head", None),
            P("head", None),
            P("head", None),
            P(),
            P(None, "head"),
            P(None, "head"),
            P("head", None),
        ),
        check_vma=False,
    )
```

```python
import functools
import math

import jax
import jax.numpy as jnp
from jax import lax
from jax.experimental import pallas as pl
from jax.experimental.pallas import tpu as pltpu
from jax.sharding import PartitionSpec as P

HEADS = 8
HD = 64
PINV_ITERS = 6
STEP = 10
TAPS = 33
REACH = 16

EPS_NORM = 1e-05
EPS_FACTOR = 1e-30
RATE = 0.5
BLOCKS = ((0, 49), (49, 74), (74, 83))

SMALL = 16
CONV_ROW = 13
NORM_ROW = 14
ROOM = 16
GRID_ROOM = 18
LARGE_ROOM = 56
PULL_ROOM = 56
MARK_ROOM = 56
PULL_MICROS = 2
F32 = jnp.float32
BF16 = jnp.bfloat16


def swap(value, axis, bit):
    return swap_bits(value, axis, 1 << bit)


def swap_bits(value, axis, bits):
    count = lax.axis_size(axis)
    return lax.ppermute(value, axis, [(i, i ^ bits) for i in range(count)])


def bit_of(axis, bit):
    return (lax.axis_index(axis) >> bit) & 1


def keep_half(value, axis, bit):
    mine = bit_of(axis, bit)
    kept = lax.dynamic_index_in_dim(value, mine, 0, keepdims=False)
    sent = lax.dynamic_index_in_dim(value, 1 - mine, 0, keepdims=False)
    return kept + swap(sent, axis, bit)


def join_half(value, axis, bit):
    other = swap(value, axis, bit)
    first = bit_of(axis, bit) == 0
    return jnp.stack([jnp.where(first, value, other), jnp.where(first, other, value)])


def all_sum(value, axis, first_bit=0):
    bits = (lax.axis_size(axis) - 1).bit_length()
    for bit in range(first_bit, bits):
        value = value + swap(value, axis, bit)
    return value


def sum_to_owner(scalars, kept, sent, after=None, direct=()):
    received = swap(sent, "patch", 0)
    count = lax.axis_size("patch")
    if kept.shape[0] != 2:
        return all_sum((kept + received)[0], "patch", 1)
    flat = (2 * kept.shape[1], kept.shape[2])
    kept, sent = fold_halves(
        scalars, kept.reshape(flat), received.reshape(flat), 1, scalars, F32
    )
    if direct and count >= 8:
        near, far = swap_bits(sent, "patch", 2), swap_bits(sent, "patch", 6)
        value = add_four(kept, swap_bits(kept, "patch", 4), near, far, direct)
        return all_sum(value, "patch", 3)
    received = swap(sent, "patch", 1)
    value = kept + received if after is None else add_parts(kept, received, after)
    return all_sum(value, "patch", 2)


def from_owner(value, heads, scalars, after):
    if heads == 2:
        value = join_heads(scalars, value, swap(value, "patch", 1), after)
    else:
        value = value[None]
    return join_half(value, "patch", 0)


def sum_rows(scalars, kept, sent, small, axis, orders, later):
    bits = (lax.axis_size(axis) - 1).bit_length()
    for bit in range(1, bits):
        received = swap(sent, axis, bit - 1)
        after = orders[bit - 1] if bit <= len(orders) else scalars
        kept, sent = fold_halves(scalars, kept, received, bit, after)
    value = (kept + swap(sent, axis, bits - 1).astype(F32)).astype(BF16)
    for bit in reversed(range(bits)):
        rows = value.shape[0]
        small = lax.reduce_precision(small, 8, 7)
        other = swap(jnp.concatenate([value, small.astype(BF16)], axis=0), axis, bit)
        small = small + other[rows:].astype(F32)
        if bit in later:
            value = unfold_rows(scalars, value, other, bit, later[bit])
            continue
        other = other[:rows]
        first = bit_of(axis, bit) == 0
        value = jnp.concatenate(
            [jnp.where(first, value, other), jnp.where(first, other, value)], axis=0
        )
    return value, small


def neighbours(value, width, kind=BF16):
    count = lax.axis_size("patch")
    odd = bit_of("patch", 0) == 1
    last = value.shape[-1] - width
    axis = value.ndim - 1
    inner = lax.dynamic_slice_in_dim(value, jnp.where(odd, 0, last), width, axis)
    outer = lax.dynamic_slice_in_dim(value, jnp.where(odd, last, 0), width, axis)
    inner, outer = inner.astype(kind), outer.astype(kind)
    inner = swap(inner, "patch", 0)
    steps = [(i, i + 1) for i in range(1, count - 1, 2)]
    outer = lax.ppermute(outer, "patch", steps + [(j, i) for i, j in steps])
    return inner, outer


def in_order(scalars_ref, inner, outer):
    odd = scalars_ref[2] == 1
    return jnp.where(odd, inner, outer), jnp.where(odd, outer, inner)


NN = (((1,), (0,)), ((), ()))
NT = (((1,), (1,)), ((), ()))
TN = (((0,), (0,)), ((), ()))


def dot(left, right, dims=NN):
    return lax.dot_general(left, right, dims, preferred_element_type=F32)


def parts(value):
    high = value.astype(BF16)
    return high, (value - high.astype(F32)).astype(BF16)


def dot3(left, right, dims=NN):
    return dot(left[0], right[0], dims) + (
        dot(left[0], right[1], dims) + dot(left[1], right[0], dims)
    )


def eye(size):
    rows = lax.broadcasted_iota(jnp.int32, (size, size), 0)
    cols = lax.broadcasted_iota(jnp.int32, (size, size), 1)
    return (rows == cols).astype(F32)


HALF = PINV_ITERS // 2


def inverse_turns(product, inverse, turns, q_ref, p_ref):
    identity = eye(product.shape[0])
    for turn in range(turns):
        p_ref[turn] = product
        now = parts(product)
        square = dot3(now, now)
        square_parts = parts(square)
        cube = dot3(square_parts, now)
        fourth = dot3(square_parts, square_parts)
        factor = 0.25 * (13.0 * identity - 15.0 * product + 7.0 * square - cube)
        q_ref[turn] = factor
        inverse = dot3(parts(inverse), parts(factor))
        product = 0.25 * (13.0 * product - 15.0 * square + 7.0 * cube - fourth)
    return product, inverse


def inverse_early_kernel(marks_ref, kernel_ref, q_ref, p_ref, carried_ref, done_ref):
    done_ref[...] = jnp.zeros_like(done_ref)
    marks = marks_ref[...]
    scores = dot(marks[:HD], marks[HD:], TN)
    raised = jnp.exp(scores - jnp.max(scores, axis=-1, keepdims=True))
    kernel = raised * (1.0 / jnp.sum(raised, axis=-1, keepdims=True))
    kernel_ref[...] = kernel
    scale = 1.0 / norm_of(kernel)
    halves = parts(kernel)
    product = dot3(halves, halves, NT) * scale
    carried_ref[0], carried_ref[1] = inverse_turns(product, kernel.T * scale, HALF, q_ref, p_ref)


def inverse_late_kernel(carried_ref, z_ref, q_ref, p_ref):
    turns = PINV_ITERS - HALF
    _, z_ref[...] = inverse_turns(carried_ref[0], carried_ref[1], turns, q_ref, p_ref)


def norm_of(kernel):
    return jnp.sum(jnp.sum(kernel * kernel, axis=0, keepdims=True), axis=1, keepdims=True)


def mixed_marks_kernel(sums_ref, z_ref, out_ref):
    values = sums_ref[:HD] / sums_ref[HD : HD + 1]
    out_ref[...] = dot3(parts(values), parts(z_ref[...]), NT).astype(BF16)


def grad_values_kernel(sums_ref, grads_ref, z_ref, out_ref):
    weight_sum = sums_ref[HD : HD + 1]
    values = sums_ref[:HD] / weight_sum
    left = dot3(parts(grads_ref[...]), parts(z_ref[...]))
    high, low = parts(-jnp.sum(left * values, axis=0, keepdims=True) / weight_sum)
    rows = out_ref.shape[0] - HD
    row = lax.broadcasted_iota(jnp.int32, (rows, out_ref.shape[1]), 0)
    tail = jnp.where(row == 0, high.astype(F32), jnp.where(row == 1, low.astype(F32), 0.0))
    out_ref[:HD] = (left / weight_sum).astype(BF16)
    out_ref[HD:] = tail.astype(BF16)


def total_of(value):
    return jnp.sum(jnp.sum(value, axis=0, keepdims=True), axis=1, keepdims=True)


def even(value):
    return 0.5 * (value + value.T)


def pull_turns(carried, turns, q_ref, p_ref, thin_ref, first):
    for turn in reversed(range(turns)):
        product = parts(p_ref[turn])
        left, right = thin_ref[first + turn], thin_ref[PINV_ITERS + first + turn]
        outer = dot3(parts(left), parts(right), TN)
        held = 0.0
        if carried is not None:
            now = parts(carried)
            outer = outer + dot3(product, now)
            held = dot3(now, parts(q_ref[turn]))
        outer = even(outer)
        once = dot3(product, parts(outer))
        once_parts = parts(once)
        twice = dot3(product, once_parts) + 0.5 * dot3(once_parts, product)
        carried = even(held + 3.5 * once - 0.5 * twice) - 3.75 * outer
    return carried


def chains_kernel(sums_ref, grads_ref, kernel_ref, early_ref, late_ref, thin_ref, done_ref):
    kernel = kernel_ref[...]
    factors = [parts(early_ref[turn]) for turn in range(HALF)]
    factors += [parts(late_ref[turn]) for turn in range(PINV_ITERS - HALF)]
    right = sums_ref[:HD] / sums_ref[HD : HD + 1]
    left = dot3(parts(grads_ref[...]), parts(kernel), NT) * (1.0 / norm_of(kernel))
    for turn in range(PINV_ITERS):
        back = PINV_ITERS - 1 - turn
        thin_ref[turn] = left
        thin_ref[PINV_ITERS + back] = right
        left = dot3(parts(left), factors[turn])
        right = dot3(parts(right), factors[back])
    thin_ref[2 * PINV_ITERS] = right
    done_ref[...] = jnp.zeros_like(done_ref)


def pull_late_kernel(thin_ref, q_ref, p_ref, out_ref):
    out_ref[...] = pull_turns(None, PINV_ITERS - HALF, q_ref, p_ref, thin_ref, HALF)


def pull_early_kernel(carried_ref, marks_ref, grads_ref, kernel_ref, q_ref, p_ref, thin_ref, out_ref):
    marks = marks_ref[...]
    kernel = kernel_ref[...]
    scale = 1.0 / norm_of(kernel)
    halves = parts(kernel)
    grads = grads_ref[...]
    whole = parts(thin_ref[2 * PINV_ITERS])
    carried = pull_turns(carried_ref[...], HALF, q_ref, p_ref, thin_ref, 0)
    mixed = dot3(whole, halves) * scale
    grad_norm = -(total_of(grads * mixed) + total_of(carried * p_ref[0])) * scale
    grad_kernel = (
        dot3(whole, parts(grads), TN) * scale
        + (2.0 * scale) * dot3(parts(carried), halves)
        + 2.0 * grad_norm * kernel
    )
    grad_scores = kernel * (grad_kernel - jnp.sum(kernel * grad_kernel, axis=-1, keepdims=True))
    high, low = parts(grad_scores)
    out_ref[:HD] = dot(marks[HD:], high, NT) + dot(marks[HD:], low, NT)
    out_ref[HD:] = dot(marks[:HD], high) + dot(marks[:HD], low)


def ordered(kernel, count, inputs):
    def body(*refs):
        return kernel(*refs[: inputs - count], *refs[inputs:])

    return body


ANYWHERE = pl.BlockSpec(memory_space=pl.ANY)
WHOLE = pl.BlockSpec(memory_space=pltpu.VMEM)
SCALARS = pl.BlockSpec(memory_space=pltpu.SMEM)
STAY = pl.BlockSpec(memory_space=pltpu.HBM)


def call(kernel, outs, micros, room=ROOM, **grid):
    return pl.pallas_call(
        kernel,
        out_shape=outs,
        compiler_params=pltpu.CompilerParams(vmem_limit_bytes=room * 1024 * 1024),
        **grid,
        cost_estimate=pl.CostEstimate(
            flops=int(micros * 10**9), bytes_accessed=1024, transcendentals=0
        ),
    )


def inverse_early(marks, after):
    size = marks.shape[-1]
    stack = jax.ShapeDtypeStruct((HALF, size, size), F32)
    return call(
        ordered(inverse_early_kernel, 1, 2),
        (
            jax.ShapeDtypeStruct((size, size), F32),
            stack,
            stack,
            jax.ShapeDtypeStruct((2, size, size), F32),
            jax.ShapeDtypeStruct((8, 128), F32),
        ),
        0.1,
        room=MARK_ROOM,
        in_specs=[WHOLE, ANYWHERE],
    )(marks, after)


def inverse_late(carried, after):
    size = carried.shape[-1]
    stack = jax.ShapeDtypeStruct((PINV_ITERS - HALF, size, size), F32)
    return call(
        ordered(inverse_late_kernel, 1, 2),
        (jax.ShapeDtypeStruct((size, size), F32), stack, stack),
        0.1,
        room=MARK_ROOM,
        in_specs=[WHOLE, ANYWHERE],
    )(carried, after)


def mixed_marks_of(sums, inverse, after):
    return call(
        ordered(mixed_marks_kernel, 1, 3),
        jax.ShapeDtypeStruct((HD, sums.shape[1]), BF16),
        0.1,
        in_specs=[WHOLE] * 2 + [ANYWHERE],
    )(sums, inverse, after)


def grad_values_of(sums, grads, inverse, after):
    return call(
        ordered(grad_values_kernel, 1, 4),
        jax.ShapeDtypeStruct((HD + 16, sums.shape[1]), BF16),
        0.1,
        in_specs=[WHOLE] * 3 + [ANYWHERE],
    )(sums, grads, inverse, after)


def thin_chains(sums, grads, kernel, early, late):
    size = kernel.shape[-1]
    return call(
        chains_kernel,
        (
            jax.ShapeDtypeStruct((2 * PINV_ITERS + 1, HD, size), F32),
            jax.ShapeDtypeStruct((8, 128), F32),
        ),
        1,
        room=PULL_ROOM,
    )(sums, grads, kernel, early, late)


def landmark_pull(marks, grads, kernel, early, late, thin, after, later):
    size = kernel.shape[-1]
    carried = call(
        ordered(pull_late_kernel, 1, 4),
        jax.ShapeDtypeStruct((size, size), F32),
        PULL_MICROS,
        room=PULL_ROOM,
        in_specs=[WHOLE] * 3 + [ANYWHERE],
    )(thin, *late, after)
    return call(
        ordered(pull_early_kernel, len(later), 7 + len(later)),
        jax.ShapeDtypeStruct((2 * HD, size), F32),
        PULL_MICROS,
        room=PULL_ROOM,
        in_specs=[WHOLE] * 7 + [ANYWHERE] * len(later),
    )(carried, marks, grads, kernel, *early, thin, *later)


def finish_kernel(sums_ref, inverse_ref, counts_ref, out_ref):
    out_ref[...] = ((sums_ref[...] + inverse_ref[...]) / counts_ref[...]).astype(BF16)


def finish_marks(sums, inverse, counts, after):
    return call(
        ordered(finish_kernel, 1, 4),
        jax.ShapeDtypeStruct(sums.shape, BF16),
        0.5,
        in_specs=[WHOLE] * 3 + [ANYWHERE],
    )(sums, inverse, counts, after)


def fold_kernel(bit, scalars_ref, kept_ref, received_ref, out_kept_ref, out_sent_ref):
    value = kept_ref[...] + received_ref[...].astype(F32)
    half = value.shape[0] // 2
    own_first = scalars_ref[2 + bit] == 0
    first, second = value[:half], value[half:]
    out_kept_ref[...] = jnp.where(own_first, first, second)
    out_sent_ref[...] = jnp.where(own_first, second, first).astype(out_sent_ref.dtype)


def fold_halves(scalars, kept, received, bit, after, kind=BF16):
    shape = (kept.shape[0] // 2, kept.shape[1])
    return call(
        ordered(functools.partial(fold_kernel, bit), 1, 4),
        (jax.ShapeDtypeStruct(shape, F32), jax.ShapeDtypeStruct(shape, kind)),
        0.1,
        in_specs=[SCALARS, WHOLE, WHOLE, ANYWHERE],
    )(scalars, kept, received, after)


def add_kernel(first_ref, second_ref, out_ref):
    out_ref[...] = first_ref[...] + second_ref[...]


def unfold_kernel(bit, scalars_ref, value_ref, other_ref, out_ref):
    rows = value_ref.shape[0]
    own, other = value_ref[...], other_ref[:rows]
    own_first = scalars_ref[2 + bit] == 0
    out_ref[:rows] = jnp.where(own_first, own, other)
    out_ref[rows:] = jnp.where(own_first, other, own)


def unfold_rows(scalars, value, other, bit, after):
    shape = (2 * value.shape[0], value.shape[1])
    return call(
        ordered(functools.partial(unfold_kernel, bit), 1, 4),
        jax.ShapeDtypeStruct(shape, BF16),
        0.1,
        in_specs=[SCALARS, WHOLE, WHOLE, ANYWHERE],
    )(scalars, value, other, after)


def add_four_kernel(kept_ref, beside_ref, near_ref, far_ref, out_ref):
    out_ref[...] = (kept_ref[...] + beside_ref[...]) + (near_ref[...] + far_ref[...])


def add_four(kept, beside, near, far, after):
    return call(
        ordered(add_four_kernel, len(after), 4 + len(after)),
        jax.ShapeDtypeStruct(kept.shape, kept.dtype),
        0.1,
        in_specs=[WHOLE] * 4 + [ANYWHERE] * len(after),
    )(kept, beside, near, far, *after)


def add_parts(first, second, after):
    return call(
        ordered(add_kernel, 1, 3),
        jax.ShapeDtypeStruct(first.shape, first.dtype),
        0.1,
        in_specs=[WHOLE, WHOLE, ANYWHERE],
    )(first, second, after)


def join_kernel(scalars_ref, own_ref, other_ref, out_ref):
    own, other = own_ref[...], other_ref[...]
    own_first = scalars_ref[3] == 0
    out_ref[0] = jnp.where(own_first, own, other)
    out_ref[1] = jnp.where(own_first, other, own)


def join_heads(scalars, own, other, after):
    return call(
        ordered(join_kernel, 1, 4),
        jax.ShapeDtypeStruct((2,) + own.shape, own.dtype),
        0.1,
        in_specs=[SCALARS, WHOLE, WHOLE, ANYWHERE],
    )(scalars, own, other, after)


def row_of(column):
    return jnp.broadcast_to(column, (column.shape[0], 128)).T[:1]


def column_of(row):
    return jnp.broadcast_to(row, (8, row.shape[1])).T[:, :1]


def segments_of(starts, scalars_ref, tokens):
    size = starts.shape[1]
    starts = starts.astype(F32)
    lane = lax.broadcasted_iota(jnp.int32, (1, size), 1)
    last = scalars_ref[1].astype(F32)
    ends = jnp.where(lane == size - 1, last, pltpu.roll(starts, size - 1, 1))
    place = lax.broadcasted_iota(jnp.int32, (1, tokens), 1) + scalars_ref[0]
    place = place.astype(F32)
    member = (place >= column_of(starts)) & (place < column_of(ends))
    return jnp.where(member, 1.0, 0.0).astype(BF16)


def full_kernel(kernels):
    channels = kernels.shape[1]
    large_part = kernels[0:49].reshape(7, 7, channels)
    middle_part = jnp.pad(kernels[49:74].reshape(5, 5, channels), ((1, 1), (1, 1), (0, 0)))
    small_part = jnp.pad(kernels[74:83].reshape(3, 3, channels), ((2, 2), (2, 2), (0, 0)))
    return large_part + middle_part + small_part


def lay_grid(scalars_ref, inner_ref, own_ref, outer_ref, padded_ref, shifted_ref):
    rows, cols, feats = shifted_ref.shape[1:]
    padded_ref[:, 0:8] = jnp.zeros((rows, 8, feats), F32)
    padded_ref[:, 8 + cols :] = jnp.zeros((rows, 8, feats), F32)

    def laid(value):
        return value.astype(F32).T.reshape(-1, cols, feats)

    before, after = in_order(scalars_ref, inner_ref[0], outer_ref[0])
    padded_ref[0:3, 8 : 8 + cols] = laid(before)
    padded_ref[3 : rows - 3, 8 : 8 + cols] = laid(own_ref[0])
    padded_ref[rows - 3 :, 8 : 8 + cols] = laid(after)
    for col in range(7):
        shifted_ref[col] = padded_ref[:, 5 + col : 5 + col + cols]


def back_kernel(scalars_ref, before_ref, own_ref, after_ref, taps_ref, out_ref, low_ref, sums_ref, padded_ref, shifted_ref, flat_ref):
    lay_grid(scalars_ref, before_ref, own_ref, after_ref, padded_ref, shifted_ref)
    rows, cols, feats = shifted_ref.shape[1:]

    def one_row(row, sums):
        centre = shifted_ref[3, row + 3]
        total = centre
        for col in range(7):
            for shift in range(7):
                tap = 48 - (shift * 7 + col)
                total = total + taps_ref[tap : tap + 1] * shifted_ref[col, row + shift]
        flat_ref[row] = total
        return (
            sums[0] + jnp.sum(total, axis=0, keepdims=True),
            sums[1] + jnp.sum(centre, axis=0, keepdims=True),
        )

    zero = jnp.zeros((1, feats), F32)
    sums = lax.fori_loop(0, rows - 6, one_row, (zero, zero))
    sums = jnp.concatenate([sums[0], sums[1], jnp.zeros((6, feats), F32)], axis=0)

    @pl.when(pl.program_id(0) == 0)
    def _():
        sums_ref[...] = sums

    @pl.when(pl.program_id(0) > 0)
    def _():
        sums_ref[...] += sums

    back = flat_ref[...].reshape(-1, feats).T
    out_ref[0] = back
    low_ref[0] = back.astype(BF16)


def kernel_grad_kernel(scalars_ref, inner_ref, own_ref, outer_ref, cot_ref, held_ref, grad_ref, padded_ref, shifted_ref, cot_grid_ref):
    lay_grid(scalars_ref, inner_ref, own_ref, outer_ref, padded_ref, shifted_ref)
    rows, cols, feats = shifted_ref.shape[1:]
    cot_grid_ref[...] = cot_ref[0].astype(F32).T.reshape(-1, cols, feats)
    grad_ref[...] = held_ref[...]

    def one_row(row, carried):
        cot = cot_grid_ref[row]
        for col in range(7):
            for shift in range(7):
                cells = cot * shifted_ref[col, row + shift]
                grad_ref[shift * 7 + col] += jnp.sum(cells.reshape(-1, 8, feats), axis=0)
        return carried

    lax.fori_loop(0, rows - 6, one_row, 0)


def mix_kernel(scalars_ref, inner_ref, own_ref, outer_ref, taps_ref, biases_ref, out_ref, done_ref, padded_ref, shifted_ref, flat_ref):
    done_ref[...] = jnp.zeros_like(done_ref)
    lay_grid(scalars_ref, inner_ref, own_ref, outer_ref, padded_ref, shifted_ref)
    rows, cols, feats = shifted_ref.shape[1:]
    bias = biases_ref[1:2] + biases_ref[2:3] + biases_ref[3:4]

    def one_row(row, carried):
        total = shifted_ref[3, row + 3] + bias
        for col in range(7):
            for shift in range(7):
                tap = shift * 7 + col
                total = total + taps_ref[tap : tap + 1] * shifted_ref[col, row + shift]
        flat_ref[row] = total
        return carried

    lax.fori_loop(0, rows - 6, one_row, 0)
    out_ref[0] = flat_ref[...].reshape(-1, feats).T.astype(BF16)


def grid_scratch(rows, cols, feats):
    return [
        pltpu.VMEM((rows + 6, cols + 16, feats), F32),
        pltpu.VMEM((7, rows + 6, cols, feats), F32),
        pltpu.VMEM((rows, cols, feats), F32),
    ]


def per_slide(shape):
    zeros = (0,) * (len(shape) - 1)
    return pl.BlockSpec((1,) + tuple(shape[1:]), lambda s: (s,) + zeros)


def whole_block(shape):
    zeros = (0,) * len(shape)
    return pl.BlockSpec(tuple(shape), lambda *_: zeros)


def grid_back(scalars, before, own, after, taps, cols, first):
    slides, feats, tokens = own.shape
    rows = tokens // cols
    return call(
        ordered(back_kernel, 1, 6),
        (
            jax.ShapeDtypeStruct(own.shape, F32),
            jax.ShapeDtypeStruct(own.shape, BF16),
            jax.ShapeDtypeStruct((8, feats), F32),
        ),
        8,
        room=GRID_ROOM,
        grid=(slides,),
        in_specs=[
            SCALARS,
            per_slide(before.shape),
            per_slide(own.shape),
            per_slide(after.shape),
            whole_block(taps.shape),
            ANYWHERE,
        ],
        out_specs=(per_slide(own.shape), per_slide(own.shape), whole_block((8, feats))),
        scratch_shapes=grid_scratch(rows, cols, feats),
    )(scalars, before, own, after, taps, first)


def one_slide(slide, shape):
    return pl.BlockSpec((1,) + tuple(shape[1:]), lambda i: (slide, 0, 0))


def grid_kernel_grad(scalars, inner, own, outer, cotangent, held, cols, slide):
    slides, feats, tokens = own.shape
    rows = tokens // cols
    return call(
        kernel_grad_kernel,
        jax.ShapeDtypeStruct(held.shape, F32),
        1,
        room=GRID_ROOM,
        grid=(1,),
        in_specs=[SCALARS]
        + [one_slide(slide, item.shape) for item in (inner, own, outer, cotangent)]
        + [whole_block(held.shape)],
        out_specs=whole_block(held.shape),
        scratch_shapes=grid_scratch(rows, cols, feats),
    )(scalars, inner, own, outer, cotangent, held)


def grid_mix(scalars, inner, own, outer, taps, biases, cols, slide, out=None):
    slides, feats, tokens = own.shape
    rows = tokens // cols
    kernel, extra, specs, aliases = mix_kernel, (), [], {}
    if out is not None:
        kernel, extra, specs, aliases = ordered(mix_kernel, 1, 7), (out,), [ANYWHERE], {6: 0}
    return call(
        kernel,
        (jax.ShapeDtypeStruct(own.shape, BF16), jax.ShapeDtypeStruct((8, 128), F32)),
        1,
        room=GRID_ROOM,
        grid=(1,),
        in_specs=[SCALARS]
        + [one_slide(slide, item.shape) for item in (inner, own, outer)]
        + [whole_block(item.shape) for item in (taps, biases)]
        + specs,
        out_specs=(one_slide(slide, own.shape), whole_block((8, 128))),
        scratch_shapes=grid_scratch(rows, cols, feats),
        input_output_aliases=aliases,
    )(scalars, inner, own, outer, taps, biases, *extra)


def pack_kernel(sums_ref, bias_ref, lines_ref, conv_ref, out_ref):
    feats = sums_ref.shape[2]
    share = out_ref.shape[1] // feats
    out_ref[...] = jnp.zeros_like(out_ref)
    totals = jnp.sum(sums_ref[...], axis=1)
    for row in range(51):
        line = totals[row : row + 1] if row < 49 else bias_ref[row - 49 : row - 48]
        at = row % share * feats
        out_ref[row // share : row // share + 1, at : at + feats] = line
    for head in range(conv_ref.shape[0]):
        line = conv_ref[head, :, 0:1]
        line = jnp.concatenate([line, jnp.zeros((64 - line.shape[0], 1), F32)], axis=0)
        out_ref[CONV_ROW : CONV_ROW + 1, head * 64 : head * 64 + 64] = row_of(line)
    out_ref[NORM_ROW : NORM_ROW + 2] = lines_ref[0:2]


def pack_sums(sums, bias_sums, lines, conv, full):
    return call(pack_kernel, jax.ShapeDtypeStruct((SMALL, full), F32), 0.2)(
        sums, bias_sums, lines, conv
    )


def lay_line(before, rows, after, line_ref):
    tokens = rows.shape[1]
    width = line_ref.shape[1]
    line_ref[:, :REACH] = before
    line_ref[:, REACH : REACH + tokens] = rows
    line_ref[:, REACH + tokens : 2 * REACH + tokens] = after
    line_ref[:, 2 * REACH + tokens :] = jnp.zeros((HD, width - tokens - 2 * REACH), BF16)


def line_width(tokens):
    return (-(-tokens // 128) + 1) * 128


def pairs_of(ref):
    return [(s, h) for h in range(ref.shape[1]) for s in range(ref.shape[0])]


def band(line):
    wide = jnp.broadcast_to(line, (128, 256))
    return parts(pltpu.roll(wide, 0, 1, stride=1, stride_axis=0))


def line_conv(line_ref, bands, out_ref, at):
    tokens = out_ref.shape[-1]
    high, low = bands
    for begin in range(0, tokens, 128):
        width = min(128, tokens - begin)
        held = line_ref[:, begin : begin + 256]
        out = dot(held, high, NT) + dot(held, low, NT)
        out_ref[at[0], at[1], :, begin : begin + width] = out[:, :width].astype(out_ref.dtype)


def residual_kernel(scalars_ref, inner_ref, rows_ref, outer_ref, taps_ref, out_ref, done_ref, lines_ref):
    done_ref[...] = jnp.zeros_like(done_ref)
    for index, at in enumerate(pairs_of(rows_ref)):
        line_ref = lines_ref.at[index]
        before, after = in_order(scalars_ref, inner_ref[at], outer_ref[at])
        lay_line(before, rows_ref[at[0], at[1], 2 * HD :], after, line_ref)
        line_conv(line_ref, band(taps_ref[at[1]]), out_ref, at)


def back_line_kernel(
    scalars_ref, value_inner_ref, rows_ref, value_outer_ref, inner_ref, low_ref, outer_ref, taps_ref,
    out_ref, grad_ref, values_ref, lines_ref,
):
    tokens = out_ref.shape[-1]
    gap = lax.broadcasted_iota(jnp.int32, (128, 256), 1) - lax.broadcasted_iota(
        jnp.int32, (128, 256), 0
    )
    cross = jnp.zeros((128, 256), F32)
    for index, at in enumerate(pairs_of(rows_ref)):
        value_ref, line_ref = values_ref.at[index], lines_ref.at[index]
        rows = rows_ref[at[0], at[1], 2 * HD :]
        before, after = in_order(scalars_ref, value_inner_ref[at], value_outer_ref[at])
        lay_line(before, rows, after, value_ref)
        before, after = in_order(scalars_ref, inner_ref[at], outer_ref[at])
        lay_line(before, low_ref[at], after, line_ref)
        line_conv(line_ref, band(taps_ref[at[1]]), out_ref, at)
        for begin in range(0, tokens, 128):
            width = min(128, tokens - begin)
            lane = lax.broadcasted_iota(jnp.int32, (HD, 256), 1)
            inside = (lane >= REACH) & (lane < REACH + width)
            centre = line_ref[:, begin : begin + 256].astype(F32)
            centre = jnp.where(inside, centre, 0.0).astype(BF16)
            held = value_ref[:, begin : begin + 256]
            cross = cross + dot(centre, held, TN)[: 128 + REACH][REACH:]
        if at[0] == rows_ref.shape[0] - 1:
            lines = [
                jnp.sum(jnp.where(gap == tap, cross, 0.0), axis=0, keepdims=True)
                for tap in range(TAPS)
            ]
            lines.append(jnp.zeros((40 - TAPS, 256), F32))
            totals = jnp.sum(jnp.concatenate(lines, axis=0), axis=1, keepdims=True)
            grad_ref[at[1]] = jnp.broadcast_to(totals, (40, 128))
            cross = jnp.zeros((128, 256), F32)


def line_taps(conv_weight):
    return jnp.pad(conv_weight, ((0, 0), (0, 256 - TAPS)))[:, None, :]


def residual_of(scalars, before, rows, after, conv_weight):
    slides, heads, _, tokens = rows.shape
    return call(
        residual_kernel,
        (
            jax.ShapeDtypeStruct((slides, heads, HD, tokens), F32),
            jax.ShapeDtypeStruct((8, 128), F32),
        ),
        0.1,
        in_specs=[SCALARS] + [WHOLE] * 4,
        scratch_shapes=[pltpu.VMEM((slides * heads, HD, line_width(tokens)), BF16)],
    )(scalars, before, rows, after, line_taps(conv_weight))


def back_line(scalars, value_before, rows, value_after, before, low, after, conv_weight, later):
    slides, heads, _, tokens = rows.shape
    lines = pltpu.VMEM((slides * heads, HD, line_width(tokens)), BF16)
    return call(
        ordered(back_line_kernel, 1, 9),
        (
            jax.ShapeDtypeStruct((slides, heads, HD, tokens), BF16),
            jax.ShapeDtypeStruct((heads, 40, 128), F32),
        ),
        1,
        in_specs=[SCALARS] + [WHOLE] * 7 + [ANYWHERE],
        scratch_shapes=[lines, lines],
    )(scalars, value_before, rows, value_after, before, low, after, line_taps(conv_weight[:, ::-1]), later)


def put_halves(kept_ref, sent_ref, mine, sums):
    own_first = mine == 0
    for head, (first, second) in enumerate(zip(*sums)):
        kept_ref[head] = jnp.where(own_first, first, second)
        sent_ref[head] = jnp.where(own_first, second, first)


def all_blocks(shape):
    zeros = (0,) * (len(shape) - 2)
    return pl.BlockSpec((shape[0], 1) + tuple(shape[2:]), lambda s: (0, s) + zeros)


def norm_kernel(scalars_ref, gathered_ref, weight_ref, norm_ref, mask_ref, starts_ref, normed_ref, stats_ref, rows_ref, kept_ref, sent_ref):
    count, _, feats, tokens = gathered_ref.shape
    heads = rows_ref.shape[1]
    full = feats * count
    slide = pl.program_id(0)
    total, squares = 0.0, 0.0
    for slot in range(count):
        cells = gathered_ref[slot, 0].astype(F32)
        total = total + jnp.sum(cells, axis=0, keepdims=True)
        squares = squares + jnp.sum(cells * cells, axis=0, keepdims=True)
    mean = total / full
    inv_std = lax.rsqrt(squares / full - mean * mean + EPS_NORM)
    stats_ref[0] = jnp.concatenate([mean, inv_std, jnp.zeros((6, tokens), F32)], axis=0)
    gain, bias = column_of(norm_ref[0:1]), column_of(norm_ref[1:2])
    for slot in range(count):
        span = slice(slot * feats, (slot + 1) * feats)
        centered = (gathered_ref[slot, 0].astype(F32) - mean) * inv_std
        normed_ref[0, span] = (centered * gain[span] + bias[span]).astype(BF16)
    normed = normed_ref[0]
    mask = mask_ref[slide].astype(F32)
    onehot = segments_of(starts_ref[pl.ds(slide, 1)], scalars_ref, tokens)
    counts = dot(jnp.broadcast_to(mask, (16, tokens)).astype(BF16), onehot, NT)[:8]
    own = scalars_ref[2] == slide
    for head in range(heads):
        row = head * 3 * HD
        projected = dot(weight_ref[row : row + 3 * HD], normed)
        rows_ref[0, head, :HD] = (projected[:HD] * mask * HD ** (-0.5)).astype(BF16)
        rows_ref[0, head, HD:] = (projected[HD:] * mask).astype(BF16)
        sums = dot(rows_ref[0, head, : 2 * HD], onehot, NT)
        sums = jnp.concatenate([sums, counts], axis=0)
        kept_ref[head] = jnp.where(own, sums, kept_ref[head])
        sent_ref[head] = jnp.where(own, sent_ref[head], sums)


def norm_project(scalars, gathered, weight, norm_params, mask, starts, after):
    count, slides, feats, tokens = gathered.shape
    heads = weight.shape[0] // (3 * HD)
    mask = mask[:, None, :]
    half = jax.ShapeDtypeStruct((heads, 2 * HD + 8, starts.shape[1]), F32)
    return call(
        ordered(norm_kernel, len(after), 6 + len(after)),
        (
            jax.ShapeDtypeStruct((slides, count * feats, tokens), BF16),
            jax.ShapeDtypeStruct((slides, 8, tokens), F32),
            jax.ShapeDtypeStruct((slides, heads, 3 * HD, tokens), BF16),
            half,
            half,
        ),
        0.1,
        room=LARGE_ROOM,
        grid=(slides,),
        in_specs=[SCALARS, all_blocks(gathered.shape)]
        + [whole_block(item.shape) for item in (weight, norm_params, mask, starts)]
        + [ANYWHERE] * len(after),
        out_specs=(
            per_slide((slides, count * feats, tokens)),
            per_slide((slides, 8, tokens)),
            per_slide((slides, heads, 3 * HD, tokens)),
            whole_block(half.shape),
            whole_block(half.shape),
        ),
    )(scalars, gathered, weight, norm_params, mask, starts, *after)


def low_kernel(scalars_ref, far_ref, weight_ref, far_kernel_ref, low_ref, kept_ref, sent_ref, near_ref, kernel_ref, sem, kernel_sem):
    count, slides, feats, tokens = far_ref.shape
    heads = low_ref.shape[1]
    rows, kernels = [], []
    for s in range(slides):
        rows.append(
            [
                pltpu.make_async_copy(far_ref.at[slot, s], near_ref.at[slot, s], sem.at[slot, s])
                for slot in range(count)
            ]
        )
        kernels.append(
            pltpu.make_async_copy(far_kernel_ref.at[s], kernel_ref.at[s], kernel_sem.at[s])
        )
    for s in range(slides):
        for copy in rows[s] + [kernels[s]]:
            copy.start()
    sums = [[None] * heads for _ in range(slides)]
    for s in range(slides):
        for copy in rows[s]:
            copy.wait()
        low = dot(weight_ref[...], near_ref[:, s].reshape(count * feats, tokens)).astype(BF16)
        for head in range(heads):
            low_ref[s, head] = low[head * HD : (head + 1) * HD]
        kernels[s].wait()
        for head in range(heads):
            sums[s][head] = dot(low_ref[s, head], kernel_ref[s, head], NT)
    put_halves(kept_ref, sent_ref, scalars_ref[2], sums)


def head_gradient(scalars, gathered, weight, kernel, after):
    count, slides, feats, tokens = gathered.shape
    heads = feats // HD
    half = jax.ShapeDtypeStruct((heads, HD, kernel.shape[2]), F32)
    return call(
        ordered(low_kernel, 1, 5),
        (jax.ShapeDtypeStruct((slides, heads, HD, tokens), BF16), half, half),
        0.1,
        room=LARGE_ROOM,
        in_specs=[SCALARS, STAY, WHOLE, STAY, ANYWHERE],
        scratch_shapes=[
            pltpu.VMEM(gathered.shape, BF16),
            pltpu.VMEM(kernel.shape, BF16),
            pltpu.SemaphoreType.DMA((count, slides)),
            pltpu.SemaphoreType.DMA((slides,)),
        ],
    )(scalars, gathered, weight, kernel, after)


def section_kernel(gathered_ref, weight_ref, patch_ref, biases_ref, out_ref):
    count, slides, feats, tokens = gathered_ref.shape
    bias = column_of(biases_ref[0:1])
    for s in range(slides):
        branch = dot(weight_ref[...], gathered_ref[:, s].reshape(count * feats, tokens), TN)
        out_ref[s] = patch_ref[s].astype(F32) + branch + bias


def section(gathered, weight, patches, biases):
    return call(section_kernel, jax.ShapeDtypeStruct(patches.shape, F32), 1)(
        gathered, weight, patches, biases
    )


def final_kernel(grad_ref, gain_ref, stats_ref, table_ref, patch_ref, back_ref, out_ref):
    slides, feats, tokens = out_ref.shape
    full = table_ref.shape[1]
    gain = column_of(gain_ref[...])
    lines = {}
    for s, which, row, begin, end in line_pieces(slides, tokens, full):
        lines.setdefault((s, which), []).append(table_ref[row : row + 1, : end - begin])
    for s in range(slides):
        mean, inv_std = stats_ref[s, 0:1], stats_ref[s, 1:2]
        first, second = (jnp.concatenate(lines[s, which], axis=1) / full for which in range(2))
        centered = (patch_ref[s].astype(F32) - mean) * inv_std
        grad = grad_ref[s].astype(F32) * gain - first - centered * second
        out_ref[s] = inv_std * grad + back_ref[s]


def token_probs(marks, queries):
    scores = dot(marks[HD:], queries, TN)
    raised = jnp.exp(scores - jnp.max(scores, axis=0, keepdims=True))
    return raised * (1.0 / jnp.sum(raised, axis=0, keepdims=True))


def token_weights(marks, keys, mask):
    return jnp.exp(dot(marks[:HD], keys, TN)) * mask


def framed(values):
    return jnp.concatenate([values, jnp.ones((16, values.shape[1]), BF16)], axis=0)


def forward_kernel(scalars_ref, rows_ref, marks_ref, mask_ref, kernel_ref, kept_ref, sent_ref):
    sums = [[None] * rows_ref.shape[1] for _ in range(rows_ref.shape[0])]
    for at in pairs_of(rows_ref):
        rows, marks = rows_ref[at], marks_ref[at]
        weights = token_weights(marks, rows[HD : 2 * HD], mask_ref[at[0] : at[0] + 1].astype(F32)).astype(BF16)
        sums[at[0]][at[1]] = dot(framed(rows[2 * HD :]), weights, NT)[: HD + 8]
        kernel_ref[at] = token_probs(marks, rows[:HD]).astype(BF16)
    put_halves(kept_ref, sent_ref, scalars_ref[2], sums)


def mixed_kernel(pack_ref, kernel_ref, residual_ref, out_ref):
    for s, h in pairs_of(pack_ref):
        attended = dot(pack_ref[s, h], kernel_ref[s, h])
        out_ref[s, h * HD : (h + 1) * HD] = (attended + residual_ref[s, h]).astype(BF16)


def pull_one_kernel(rows_ref, marks_ref, pack_ref, low_ref, grads_ref, sums_ref):
    for at in pairs_of(rows_ref):
        queries, marks = rows_ref[at[0], at[1], :HD], marks_ref[at]
        probs = token_probs(marks, queries)
        pulled = probs * dot(pack_ref[at], low_ref[at], TN)
        grad_scores = (pulled - probs * jnp.sum(pulled, axis=0, keepdims=True)).astype(BF16)
        grads_ref[at] = dot(marks[HD:], grad_scores).astype(BF16)
        sums_ref[at] = dot(queries, grad_scores, NT)


def pull_three_kernel(scalars_ref, rows_ref, marks_ref, pack_ref, mask_ref, other_ref, grads_ref, value_ref, kept_ref, sent_ref):
    sums = [[None] * rows_ref.shape[1] for _ in range(rows_ref.shape[0])]
    for at in pairs_of(rows_ref):
        rows, marks, pack = rows_ref[at], marks_ref[at], pack_ref[at]
        keys = rows[HD : 2 * HD]
        raised = token_weights(marks, keys, mask_ref[at[0] : at[0] + 1].astype(F32))
        grad_three = (dot(pack, framed(rows[2 * HD :]), TN) * raised).astype(BF16)
        own = dot(keys, grad_three, NT)
        sums[at[0]][at[1]] = jnp.concatenate([own, other_ref[at]], axis=0)
        grads_ref[at] = dot(marks[:HD], grad_three).astype(BF16)
        value_ref[at] = dot(pack[:HD], raised.astype(BF16)).astype(BF16)
    put_halves(kept_ref, sent_ref, scalars_ref[2], sums)


def token_forward(scalars, rows, marks, mask, after):
    slides, heads, _, tokens = rows.shape
    size = marks.shape[-1]
    half = jax.ShapeDtypeStruct((heads, HD + 8, size), F32)
    return call(
        ordered(forward_kernel, 1, 5),
        (jax.ShapeDtypeStruct((slides, heads, size, tokens), BF16), half, half),
        0.1,
        in_specs=[SCALARS] + [WHOLE] * 3 + [ANYWHERE],
    )(scalars, rows, marks, mask, after)


def mixed_heads(pack, kernel, residual, after):
    slides, heads, size, tokens = kernel.shape
    return call(
        ordered(mixed_kernel, 1, 4),
        jax.ShapeDtypeStruct((slides, heads * HD, tokens), BF16),
        0.1,
        in_specs=[WHOLE] * 3 + [ANYWHERE],
    )(pack, kernel, residual, after)


def pull_one(rows, marks, pack, low, *after):
    slides, heads, _, tokens = rows.shape
    return call(
        ordered(pull_one_kernel, len(after), 4 + len(after)),
        (
            jax.ShapeDtypeStruct((slides, heads, HD, tokens), BF16),
            jax.ShapeDtypeStruct((slides, heads, HD, marks.shape[-1]), F32),
        ),
        1,
        in_specs=[WHOLE] * 4 + [ANYWHERE] * len(after),
    )(rows, marks, pack, low, *after)


def pull_three(scalars, rows, marks, pack, mask, other, after):
    slides, heads, _, tokens = rows.shape
    half = jax.ShapeDtypeStruct((heads, 2 * HD, marks.shape[-1]), F32)
    token = jax.ShapeDtypeStruct((slides, heads, HD, tokens), BF16)
    return call(
        ordered(pull_three_kernel, 1, 7),
        (token, token, half, half),
        1,
        in_specs=[SCALARS] + [WHOLE] * 5 + [STAY],
    )(scalars, rows, marks, pack, mask, other, after)


def project_kernel(scalars_ref, query_ref, key_ref, value_ref, line_ref, marks_ref, mask_ref, starts_ref, weight_ref, gathered_ref, normed_ref, stats_ref, norm_ref, out_rows_ref, low_ref, near_ref, moments_ref, lines_ref, kept_ref, sent_ref, rows_ref, sums_ref):
    count, slides, feats, tokens = gathered_ref.shape
    heads = query_ref.shape[1]
    gains = column_of(norm_ref[0:1])
    norms = [[0.0, 0.0] for _ in range(count)]
    for s in range(slides):
        mask = mask_ref[s : s + 1].astype(F32)
        onehot = segments_of(starts_ref[s : s + 1], scalars_ref, tokens)
        for head in range(heads):
            row = head * 3 * HD
            spread = dot(marks_ref[s, head], onehot)
            query = (query_ref[s, head].astype(F32) + spread[:HD]).astype(BF16).astype(F32) * mask
            key = (key_ref[s, head].astype(F32) + spread[HD:]).astype(BF16).astype(F32) * mask
            value = (value_ref[s, head].astype(F32) + line_ref[s, head].astype(F32)).astype(BF16)
            rows_ref[s, row : row + HD] = (query * HD ** (-0.5)).astype(BF16)
            rows_ref[s, row + HD : row + 2 * HD] = key.astype(BF16)
            rows_ref[s, row + 2 * HD : row + 3 * HD] = (value.astype(F32) * mask).astype(BF16)
        rows = rows_ref[s]
        mean, inv_std = stats_ref[s, 0:1], stats_ref[s, 1:2]
        first, second = 0.0, 0.0
        for slot in range(count):
            span = slice(slot * feats, (slot + 1) * feats)
            grad = dot(weight_ref[:, span], rows, TN)
            near_ref[slot, s] = grad.astype(BF16)
            centered = (gathered_ref[slot, s].astype(F32) - mean) * inv_std
            pulled = grad * centered
            gain = gains[span]
            first = first + jnp.sum(grad * gain, axis=0, keepdims=True)
            second = second + jnp.sum(pulled * gain, axis=0, keepdims=True)
            norms[slot][0] += jnp.sum(pulled, axis=1, keepdims=True)
            norms[slot][1] += jnp.sum(grad, axis=1, keepdims=True)
        moments_ref[s] = jnp.concatenate([first, second], axis=0)
    qkv_grad = 0.0
    out_grads = [0.0] * count
    for s in range(slides):
        qkv_grad = qkv_grad + dot(rows_ref[s], normed_ref[s], NT)
        for slot in range(count):
            out_grads[slot] += dot(out_rows_ref[s], low_ref[slot, s], NT)
    lines_ref[...] = jnp.zeros_like(lines_ref)
    sums_ref[: 3 * feats] = qkv_grad
    for slot in range(count):
        span = slice(slot * feats, (slot + 1) * feats)
        sums_ref[3 * feats : 4 * feats, span] = out_grads[slot]
        for line in range(2):
            lines_ref[line : line + 1, span] = row_of(norms[slot][line])
    half = sums_ref.shape[0] // 2
    own_first = scalars_ref[2] == 0
    first, second = sums_ref[:half], sums_ref[half:]
    kept_ref[...] = jnp.where(own_first, first, second)
    sent_ref[...] = jnp.where(own_first, second, first).astype(BF16)


def project_back(scalars, query, key, value, line, marks, mask, starts, weight, gathered, normed, stats, norm_params, heads_out, low):
    count, slides, feats, tokens = gathered.shape
    held = (query, key, value, line, marks, mask, starts, weight, gathered, normed, stats, norm_params, heads_out, low)
    return call(
        project_kernel,
        (
            jax.ShapeDtypeStruct((count, slides, feats, tokens), BF16),
            jax.ShapeDtypeStruct((slides, 2, tokens), F32),
            jax.ShapeDtypeStruct((8, count * feats), F32),
            jax.ShapeDtypeStruct((2 * feats, count * feats), F32),
            jax.ShapeDtypeStruct((2 * feats, count * feats), BF16),
        ),
        7,
        in_specs=[SCALARS] + [WHOLE] * len(held),
        scratch_shapes=[
            pltpu.VMEM((slides, weight.shape[0], tokens), BF16),
            pltpu.VMEM((4 * feats, count * feats), F32),
        ],
    )(scalars, *held)


DECAY = 1.0 - STEP ** (-0.8)


def second_of(old, grad):
    return DECAY * old + (1.0 - DECAY) * (grad * grad + EPS_FACTOR)


def shrink(update, usq_sum, weight_sq, entries):
    clip_factor = jnp.maximum(1.0, jnp.sqrt(usq_sum / entries))
    return RATE * jnp.sqrt(weight_sq / entries) * update / clip_factor


def scalar_line(values):
    lane = lax.broadcasted_iota(jnp.int32, (1, 128), 1)
    line = jnp.zeros((1, 128), F32)
    for index, value in values:
        line = jnp.where(lane == index, value, line)
    return line


def block_masks(shape):
    row = lax.broadcasted_iota(jnp.int32, shape, 0)
    return [jnp.where((row >= low) & (row < high), 1.0, 0.0) for low, high in BLOCKS]


def squares_kernel(qkv_ref, out_ref, biases_ref, kernels_ref, conv_ref, line_ref):
    def square(ref):
        value = ref[...]
        return value * value

    biases = square(biases_ref)
    kernels = square(kernels_ref)
    values = [(1, total_of(square(qkv_ref))), (3, total_of(square(out_ref)))]
    values.append((5, total_of(square(conv_ref))))
    values += [(7 + 2 * row, total_of(biases[row : row + 1])) for row in range(4)]
    masks = block_masks(kernels.shape)
    values += [(15 + 2 * block, total_of(kernels * mask)) for block, mask in enumerate(masks)]
    line_ref[...] = jnp.broadcast_to(scalar_line(values), line_ref.shape)


def weight_squares(*weights):
    return call(squares_kernel, jax.ShapeDtypeStruct((8, 128), F32), 2, room=LARGE_ROOM)(*weights)


def weight_grad(sums_ref, feats, index):
    return sums_ref[3 * feats * index : 3 * feats + feats * index].astype(F32)


def conv_grad_of(part_ref, heads):
    row = part_ref[CONV_ROW : CONV_ROW + 1]
    return jnp.concatenate([row[:, 64 * head : 64 * head + TAPS] for head in range(heads)], axis=0)


def part_row(part_ref, feats, row):
    share = part_ref.shape[1] // feats
    at = row % share * feats
    return part_ref[row // share : row // share + 1, at : at + feats]


def lay_bias_grad(part_ref, out_ref):
    feats = out_ref.shape[1]
    for row in range(4):
        out_ref[row : row + 1] = part_row(part_ref, feats, 49 + min(row, 1))


def lay_kernel_grad(part_ref, out_ref):
    feats = out_ref.shape[1]
    taps = list(range(49))
    taps += [7 * row + col for row in range(1, 6) for col in range(1, 6)]
    taps += [7 * row + col for row in range(2, 5) for col in range(2, 5)]
    for row, tap in enumerate(taps):
        out_ref[row : row + 1] = part_row(part_ref, feats, tap)


def rows_new_of(grad, rows):
    mean = jnp.sum(grad * grad, axis=1, keepdims=True) / grad.shape[1]
    return DECAY * column_of(rows) + (1.0 - DECAY) * (mean + EPS_FACTOR)


def line_pieces(slides, tokens, full):
    share = -(-tokens // full)
    return [
        (s, which, 8 + (2 * s + which) * share + piece, piece * full, min(tokens, (piece + 1) * full))
        for s in range(slides)
        for which in range(2)
        for piece in range(share)
    ]


def table_kernel(sums_ref, part_ref, qkv_rows_ref, out_rows_ref, bias_second_ref, kernel_second_ref, conv_second_ref, line_ref, moments_ref, table_ref, bias_ref, kernel_ref):
    feats = bias_second_ref.shape[1]
    heads = conv_second_ref.shape[0]
    values = []
    table_ref[...] = jnp.zeros_like(table_ref)
    for index, rows_ref in enumerate((qkv_rows_ref, out_rows_ref)):
        grad = weight_grad(sums_ref, feats, index)
        squares = grad * grad
        rows_new = rows_new_of(grad, rows_ref[...])
        table_ref[2 * index : 2 * index + 1] = jnp.sum(squares, axis=0, keepdims=True)
        table_ref[2 * index + 1 : 2 * index + 2] = jnp.sum(
            squares * (1.0 / rows_new), axis=0, keepdims=True
        )
        values.append((2 * index, total_of(rows_new)))
    table_ref[4:6] = part_ref[NORM_ROW : NORM_ROW + 2]

    def update_squares(grad, second):
        return grad * grad / second_of(second, grad)

    conv_grad = conv_grad_of(part_ref, heads)
    values.append((4, total_of(update_squares(conv_grad, conv_second_ref[...]))))
    lay_bias_grad(part_ref, bias_ref)
    bias_squares = update_squares(bias_ref[...], bias_second_ref[...])
    values += [(6 + 2 * row, total_of(bias_squares[row : row + 1])) for row in range(4)]
    lay_kernel_grad(part_ref, kernel_ref)
    kernel_squares = update_squares(kernel_ref[...], kernel_second_ref[...])
    masks = block_masks(kernel_squares.shape)
    values += [
        (14 + 2 * block, total_of(kernel_squares * mask)) for block, mask in enumerate(masks)
    ]
    table_ref[6:7, :128] = scalar_line(values) + line_ref[0:1]
    slides, _, tokens = moments_ref.shape
    for s, which, row, begin, end in line_pieces(slides, tokens, table_ref.shape[1]):
        table_ref[row : row + 1, : end - begin] = moments_ref[s, which : which + 1, begin:end]


def optimizer_table(gradients, rows, seconds, line, moments):
    full = gradients[0].shape[1]
    lines = len(line_pieces(moments.shape[0], moments.shape[2], full))
    return call(
        table_kernel,
        jax.ShapeDtypeStruct((8 + -(-lines // 8) * 8, full), F32),
        0.2,
        scratch_shapes=[pltpu.VMEM(seconds[0].shape, F32), pltpu.VMEM(seconds[1].shape, F32)],
    )(*gradients, *rows, *seconds, line, moments)


def state_kernel(sums_ref, part_ref, qkv_rows_ref, out_rows_ref, bias_second_ref, kernel_second_ref, conv_second_ref, qkv_grad_ref, out_grad_ref, bias_grad_ref, kernel_grad_ref, conv_grad_ref, qkv_rows_new_ref, out_rows_new_ref, bias_new_ref, kernel_new_ref, conv_new_ref):
    feats = bias_second_ref.shape[1]
    heads = conv_second_ref.shape[0]
    for index, (rows_ref, grad_ref, rows_new_ref) in enumerate(
        (
            (qkv_rows_ref, qkv_grad_ref, qkv_rows_new_ref),
            (out_rows_ref, out_grad_ref, out_rows_new_ref),
        )
    ):
        grad = weight_grad(sums_ref, feats, index)
        grad_ref[...] = grad
        rows_new_ref[...] = row_of(rows_new_of(grad, rows_ref[...]))
    conv_grad_ref[...] = conv_grad_of(part_ref, heads)
    lay_bias_grad(part_ref, bias_grad_ref)
    lay_kernel_grad(part_ref, kernel_grad_ref)
    conv_new_ref[...] = second_of(conv_second_ref[...], conv_grad_ref[...])
    bias_new_ref[...] = second_of(bias_second_ref[...], bias_grad_ref[...])
    kernel_new_ref[...] = second_of(kernel_second_ref[...], kernel_grad_ref[...])


def optimizer_state(gradients, rows, seconds, weights, after):
    return call(
        ordered(state_kernel, 1, 8),
        tuple(like(item) for item in weights + rows + seconds),
        0.2,
        room=LARGE_ROOM,
        in_specs=[WHOLE] * 7 + [ANYWHERE],
    )(*gradients, *rows, *seconds, after)


def step_kernel(
    table_ref,
    sums_ref,
    part_ref,
    qkv_rows_ref,
    out_rows_ref,
    bias_second_ref,
    kernel_second_ref,
    conv_second_ref,
    qkv_cols_ref,
    out_cols_ref,
    norm_second_ref,
    norm_ref,
    qkv_weight_ref,
    out_weight_ref,
    biases_ref,
    kernels_ref,
    conv_weight_ref,
    norm_grad_ref,
    qkv_cols_new_ref,
    out_cols_new_ref,
    norm_second_new_ref,
    qkv_new_ref,
    out_new_ref,
    norm_new_ref,
    bias_new_ref,
    kernel_new_ref,
    conv_new_ref,
):
    feats, full = out_weight_ref.shape
    heads = conv_weight_ref.shape[0]

    def scalar(index):
        return table_ref[6:7, index : index + 1]

    for index, (rows, cols_ref, cols_new_ref, rows_ref, weight_ref, new_ref) in enumerate(
        (
            (3 * full, qkv_cols_ref, qkv_cols_new_ref, qkv_rows_ref, qkv_weight_ref, qkv_new_ref),
            (full, out_cols_ref, out_cols_new_ref, out_rows_ref, out_weight_ref, out_new_ref),
        )
    ):
        mean = scalar(2 * index) / rows
        cols = DECAY * cols_ref[...] + (1.0 - DECAY) * (
            table_ref[2 * index : 2 * index + 1] / rows + EPS_FACTOR
        )
        cols_new_ref[...] = cols
        usq = mean * total_of(table_ref[2 * index + 1 : 2 * index + 2] / cols)
        grad = weight_grad(sums_ref, feats, index)
        update = grad * lax.rsqrt(rows_new_of(grad, rows_ref[...]) * cols / mean)
        new_ref[...] = weight_ref[...] - shrink(update, usq, scalar(2 * index + 1), rows * full)

    norm_grad = table_ref[4:6]
    norm_grad_ref[...] = norm_grad
    norm_second = second_of(norm_second_ref[...], norm_grad)
    norm_second_new_ref[...] = norm_second
    update = norm_grad * lax.rsqrt(norm_second)
    norm = norm_ref[...]
    norm_new_ref[...] = norm - shrink(
        update,
        jnp.sum(update * update, axis=1, keepdims=True),
        jnp.sum(norm * norm, axis=1, keepdims=True),
        full,
    )

    conv_grad = conv_grad_of(part_ref, heads)
    conv_update = conv_grad * lax.rsqrt(second_of(conv_second_ref[...], conv_grad))
    conv_new_ref[...] = conv_weight_ref[...] - shrink(
        conv_update, scalar(4), scalar(5), HEADS * TAPS
    )
    lay_bias_grad(part_ref, bias_new_ref)
    bias_grad = bias_new_ref[...]
    bias_update = bias_grad * lax.rsqrt(second_of(bias_second_ref[...], bias_grad))
    for row in range(4):
        at = slice(row, row + 1)
        bias_new_ref[at] = biases_ref[at] - shrink(
            bias_update[at], scalar(6 + 2 * row), scalar(7 + 2 * row), full
        )
    lay_kernel_grad(part_ref, kernel_new_ref)
    kernel_grad = kernel_new_ref[...]
    kernel_update = kernel_grad * lax.rsqrt(second_of(kernel_second_ref[...], kernel_grad))
    usq, wsq, entries = 0.0, 0.0, 0.0
    masks = block_masks(kernel_grad.shape)
    for index, (low, high) in enumerate(BLOCKS):
        usq = usq + masks[index] * scalar(14 + 2 * index)
        wsq = wsq + masks[index] * scalar(15 + 2 * index)
        entries = entries + masks[index] * ((high - low) * full)
    kernel_new_ref[...] = kernels_ref[...] - shrink(kernel_update, usq, wsq, entries)


def last_kernel(inputs, outputs, *refs):
    split = inputs + outputs
    step_kernel(*refs[:inputs], *refs[inputs + 5 : split + 5])
    table_ref, patch_ref = refs[0], refs[split + 5]
    grad_ref, gain_ref, stats_ref, patches_ref, back_ref = refs[inputs : inputs + 5]
    final_kernel(grad_ref, gain_ref, stats_ref, table_ref, patches_ref, back_ref, patch_ref)


def optimizer_step(table, gradients, rows, seconds, cols, norm_params, weights, patch, after):
    held = (table,) + gradients + rows + seconds + cols + (norm_params,) + weights
    outs = (norm_params,) + cols + weights[:2] + (norm_params,) + weights[2:]
    patch_out = jax.ShapeDtypeStruct(patch[3].shape, F32)
    total = len(held) + len(patch)
    return call(
        ordered(functools.partial(last_kernel, len(held), len(outs)), 1, total + 1),
        tuple(like(item) for item in outs) + (patch_out,),
        0.2,
        room=LARGE_ROOM,
        in_specs=[WHOLE] * total + [ANYWHERE],
    )(*held, *patch, after)


def like(value):
    return jax.ShapeDtypeStruct(value.shape, value.dtype)


def local(
    patches,
    hole_mask,
    seg_start,
    cotangent,
    qkv_weight,
    out_weight,
    norm_params,
    biases,
    kernels,
    conv_weight,
    qkv_rows,
    qkv_cols,
    out_rows,
    out_cols,
    norm_second,
    bias_second,
    kernel_second,
    conv_second,
):
    patch_count = lax.axis_size("patch")
    head_count = lax.axis_size("head")
    patch_index = lax.axis_index("patch")
    head_index = lax.axis_index("head")
    slide_count, feat_width, tokens_dev = patches.shape
    heads = feat_width // HD
    full_width = feat_width * head_count
    total_tokens = tokens_dev * patch_count
    grid_cols = math.isqrt(total_tokens)
    offset = head_index * feat_width
    halo = 3 * grid_cols

    scalars = jnp.stack(
        [patch_index * tokens_dev, jnp.int32(total_tokens)]
        + [bit_of("patch", bit) for bit in range((patch_count - 1).bit_length())]
    )

    gathered = lax.all_gather(patches, "head")

    out_low = out_weight.astype(BF16)
    out_blocks = [lax.dynamic_slice_in_dim(out_low, offset, feat_width, 1)]
    for hop in range(1, head_count):
        block = lax.dynamic_slice_in_dim(
            out_low, ((head_index + hop) % head_count) * feat_width, feat_width, 1
        )
        out_blocks.append(
            lax.ppermute(block, "head", [(i, (i + hop) % head_count) for i in range(head_count)])
        )
    out_blocks = jnp.stack(out_blocks)
    out_own = jnp.concatenate(
        [
            lax.dynamic_index_in_dim(out_blocks, (head_index - z) % head_count, 0, keepdims=False)
            for z in range(head_count)
        ]
    )

    cot_before, cot_after = neighbours(cotangent, halo)
    taps = full_kernel(kernels).reshape(49, feat_width)
    back_flat, grad_low, bias_part = grid_back(scalars, cot_before, cotangent, cot_after, taps, grid_cols, out_own)
    grad_all = lax.all_gather(grad_low, "head")

    qkv_low = qkv_weight.astype(BF16)
    scalars_row = jnp.zeros((8, 128), F32)
    weight_sums = weight_squares(qkv_weight, out_weight, biases, kernels, conv_weight)

    normed, stats, rows, *mark_sums = norm_project(
        scalars,
        gathered,
        qkv_low,
        norm_params,
        hole_mask,
        seg_start,
        (grad_low, out_own, weight_sums),
    )
    value_before, value_after = neighbours(rows[:, :, 2 * HD :], REACH)
    own_sums = sum_to_owner(scalars, *mark_sums, direct=(value_before, value_after))
    own_counts = own_sums[2 * HD : 2 * HD + 1]
    own_marks = (own_sums[: 2 * HD] / own_counts).astype(BF16)
    residual, residual_done = residual_of(scalars, value_before, rows, value_after, conv_weight)
    marks = from_owner(own_marks, heads, scalars, residual_done)

    kernel_one, *value_parts = token_forward(scalars, rows, marks, hole_mask, residual_done)
    own_kernel, *own_early, own_carried, early_done = inverse_early(own_marks, value_parts[0])
    own_inverse_z, *own_late = inverse_late(own_carried, own_marks)
    own_values = sum_to_owner(scalars, *value_parts, after=early_done)
    own_mixed = mixed_marks_of(own_values, own_inverse_z, residual_done)
    mixed_marks = from_owner(own_mixed, heads, scalars, scalars_row)

    head_low, *mixed_parts = head_gradient(scalars, grad_all, out_low, kernel_one, own_values)
    heads_out = mixed_heads(mixed_marks, kernel_one, residual, mixed_parts[0])
    heads_all = lax.all_gather(heads_out, "head")
    own_grad_mixed = sum_to_owner(scalars, *mixed_parts)
    low_before, low_after = neighbours(head_low, REACH)
    query_grads, key_mark_parts = pull_one(
        rows, marks, mixed_marks, head_low, heads_out, low_before, low_after
    )
    own_pack = grad_values_of(own_values, own_grad_mixed, own_inverse_z, key_mark_parts)
    own_thin, thin_done = thin_chains(own_values, own_grad_mixed, own_kernel, own_early[0], own_late[0])

    pack = from_owner(own_pack, heads, scalars, thin_done)
    key_grads, value_grads, *mark_parts = pull_three(
        scalars, rows, marks, pack, hole_mask, key_mark_parts, scalars_row
    )
    own_grads = sum_to_owner(scalars, *mark_parts)
    own_inverse = landmark_pull(
        own_marks, own_grad_mixed, own_kernel, own_early, own_late, own_thin, mark_parts[0], ()
    )
    own_mark_grads = finish_marks(own_grads, own_inverse, own_counts, own_counts)
    value_from_conv, conv_lines = back_line(
        scalars, value_before, rows, value_after, low_before, head_low, low_after, conv_weight, own_mark_grads
    )
    mark_grads = from_owner(own_mark_grads, heads, scalars, conv_lines)

    grad_normed, moments, lines, *sums = project_back(
        scalars,
        query_grads,
        key_grads,
        value_grads,
        value_from_conv,
        mark_grads,
        hole_mask,
        seg_start,
        qkv_low,
        gathered,
        normed,
        stats,
        norm_params,
        heads_out,
        grad_all,
    )
    section_one = section(heads_all, out_own, patches, biases)
    sec_before, sec_after = neighbours(section_one, halo)
    own_grad = lax.psum_scatter(grad_normed, "head", scatter_dimension=0, tiled=True)[0]

    block_out, held, grads, dones = None, jnp.zeros((49, 8, feat_width), F32), [], []
    grid_args = (scalars, sec_before, section_one, sec_after)
    for slide in range(slide_count):
        held = grid_kernel_grad(*grid_args, cotangent, held, grid_cols, slide)
        block_out, done = grid_mix(*grid_args, taps, biases, grid_cols, slide, block_out)
        grads.append(held)
        dones.append(done)
    kernel_part = pack_sums(held, bias_part, lines, conv_lines, full_width)

    sums, part = sum_rows(scalars, *sums, kernel_part, "patch", (section_one, grads[0]), {2: dones[0], 1: dones[1]})

    gradients = (sums, part)
    rows_old = (qkv_rows[None, :], out_rows[None, :])
    seconds = (bias_second, kernel_second, conv_second)
    table = optimizer_table(gradients, rows_old, seconds, weight_sums, moments)
    gain_own = lax.dynamic_slice_in_dim(norm_params, offset, feat_width, 1)[0:1]
    weights = (qkv_weight, out_weight, biases, kernels, conv_weight)
    emitted = optimizer_state(gradients, rows_old, seconds, weights, table)
    qkv_grad, out_grad, bias_grad, kernel_grad, conv_grad = emitted[:5]
    qkv_rows_new, out_rows_new, bias_second_new, kernel_second_new, conv_second_new = emitted[5:]
    table = all_sum(table, "head")
    cols = (qkv_cols[None, :], out_cols[None, :], norm_second)
    norm_grad, qkv_cols_new, out_cols_new, norm_second_new, *news = optimizer_step(
        table,
        gradients,
        rows_old,
        seconds,
        cols,
        norm_params,
        weights,
        (own_grad, gain_own, stats, patches, back_flat),
        emitted[9],
    )
    qkv_new, out_new, norm_new, bias_new, kernel_new, conv_new, patch_grad = news
    return (
        block_out,
        patch_grad,
        qkv_grad,
        out_grad,
        norm_grad,
        bias_grad,
        kernel_grad,
        conv_grad,
        qkv_rows_new[0],
        qkv_cols_new[0],
        out_rows_new[0],
        out_cols_new[0],
        norm_second_new,
        bias_second_new,
        kernel_second_new,
        conv_second_new,
        qkv_new,
        out_new,
        norm_new,
        bias_new,
        kernel_new,
        conv_new,
    )


def solution(mesh):
    placed = (
        P(None, "head", "patch"),
        P(None, "patch"),
        P(),
        P(None, "head", "patch"),
        P("head", None),
        P("head", None),
        P(),
        P(None, "head"),
        P(None, "head"),
        P("head", None),
        P("head"),
        P(),
        P("head"),
        P(),
        P(),
        P(None, "head"),
        P(None, "head"),
        P("head", None),
    )
    return jax.shard_map(
        local,
        mesh=mesh,
        in_specs=placed,
        out_specs=(
            P(None, "head", "patch"),
            P(None, "head", "patch"),
            P("head", None),
            P("head", None),
            P(),
            P(None, "head"),
            P(None, "head"),
            P("head", None),
            P("head"),
            P(),
            P("head"),
            P(),
            P(),
            P(None, "head"),
            P(None, "head"),
            P("head", None),
            P("head", None),
            P("head", None),
            P(),
            P(None, "head"),
            P(None, "head"),
            P("head", None),
        ),
        check_vma=False,
    )
```
